256 devices in a mesh: seq: 64 (over y, z, core), head: 4 (over x).
Axes of the slice: x: 4, y: 4, z: 8, core: 2. Of those that a mesh axis runs over, the one named last changes fastest.
Arguments:
- lin_query: bfloat16 [16384, 4096], P('seq', 'head'), may hold values from -6 to 6
- lin_key: bfloat16 [16384, 4096], P('seq', 'head'), may hold values from -6 to 6
- lin_value: bfloat16 [16384, 4096], P('seq', 'head'), may hold values from -6 to 6
- out_gate: bfloat16 [16384, 4096], P('seq', 'head'), may hold values from -6 to 6
- norm_gain: float32 [4096], P('head'), may hold values from 0.25 to 1.75
- decay_rate: float32 [32], P('head'), may hold values from 0 to 0.04, as said below
- soft_query: bfloat16 [16384, 4096], P('seq', 'head'), may hold values from -130 to 130
- soft_key: bfloat16 [16384, 4096], P('seq', 'head'), may hold values from -130 to 130
- soft_value: bfloat16 [16384, 4096], P('seq', 'head'), may hold values from -6 to 6
- doc_ids: int32 [128], replicated, may hold values from 0 to 31, never falling along the last dimension, each value on 1 to 8 neighbouring positions
- block_mask: int32 [128, 128], P('seq'), may hold values 0 or 1
Outputs:
- lin_output: bfloat16 [16384, 4096], P('seq', 'head')
- soft_output: bfloat16 [16384, 4096], P('seq', 'head')
The draws below stay inside these ranges and needn't reach their ends.
Inputs may be any that keep to these rules, and one draw needn't show every extreme that they name: `decay_rate`: each head's rate is positive. `doc_ids`: never falls; each document covers 1 to 8 blocks, one exactly 8.
All inputs are finite; a program needn't handle non-finite values. No bound on the sum of `block_mask` on one device may be relied on, other than what follows from the above.
Results may differ from the reference program's by a relative error of at most 0.0055.
Values may be sent and summed in bfloat16 or wider, within the bound.
No kernel may reach another device: no remote copies, remote signals or barrier semaphores. Data moves between devices by JAX's collectives and lax.ppermute only.
A program may use at most 128 MiB of HBM per device.

```python
import math
import jax
import jax.numpy as jnp
import numpy as np
from jax import lax

HEADS = 32
HD = 128
D = 4096
BLK = 128
NBLK = 128
MOST = 8
TOKENS = 16384


def loguniform_draw(key, shape, low, high):
    return jnp.exp(jax.random.uniform(key, shape, jnp.float32, math.log(low), math.log(high)))


def draw_decay_rate(key, part):
    key_fast, key_slow, key_pick = jax.random.split(jax.random.fold_in(key, 3), 3)
    slow_rate = loguniform_draw(key_slow, (HEADS,), 0.2, 2.0) / TOKENS
    fast_rate = loguniform_draw(key_fast, (HEADS,), 1.0 / 50.0, 1.0 / 30.0)
    fast_mask = jax.random.uniform(key_pick, (HEADS,)) < 0.5
    return jnp.where(fast_mask, fast_rate, slow_rate)


def query_key_pair(key):
    key_query, key_key = jax.random.split(jax.random.fold_in(key, 17), 2)
    key_rows = jnp.clip(jax.random.normal(key_key, (TOKENS, D), jnp.float32), -6.0, 6.0)
    query_rows = jnp.clip(jax.random.normal(key_query, (TOKENS, D), jnp.float32), -6.0, 6.0)
    return (query_rows, key_rows)


def draw_soft_query(key, part):
    return query_key_pair(key)[0].astype(jnp.bfloat16)


def draw_soft_key(key, part):
    return query_key_pair(key)[1].astype(jnp.bfloat16)


def plant(drawn, own_key, least, high):
    index_at = [jax.random.randint(jax.random.fold_in(own_key, axis), (), 0, length) for axis, length in enumerate(drawn.shape)]
    widest = drawn.shape.index(max(drawn.shape))
    next_to = index_at[:widest] + [(index_at[widest] + 1) % drawn.shape[widest]] + index_at[widest + 1:]
    return drawn.at[tuple(index_at)].set(least).at[tuple(next_to)].set(high)


def level_of(stream_key, dims, cuts, low, high):
    loudness = 1.0
    for position, parts in cuts:
        heights = jax.random.uniform(jax.random.fold_in(jax.random.fold_in(stream_key, 6), position), (parts,), jnp.float32, low / len(cuts), high / len(cuts))
        loudness = loudness * jnp.repeat(jnp.exp(heights), dims[position] // parts).reshape((-1,) + (1,) * (len(dims) - 1 - position))
    return loudness


def length_profile(amount, total, reach, slope):
    weights = [(1 << 20) // math.isqrt(rank ** slope) + 1 for rank in range(2, amount + 1)]
    rest, holding = total - reach - (amount - 1), [1] * (amount - 1)
    while rest > 0:
        candidates = [i for i in range(amount - 1) if holding[i] < reach]
        pool, remaining = sum([weights[i] for i in candidates]), rest
        for i in candidates:
            more = min(reach - holding[i], max(1, remaining * weights[i] // pool), rest)
            holding[i] = holding[i] + more
            rest = rest - more
    return np.array([reach] + holding)


def uneven_parts(key, number_of, total, limit, skew):
    if number_of == 2:
        one = jax.random.randint(key, (), max(1, total - limit), min(limit, total - 1) + 1)
        return jnp.stack([one, total - one])
    tallies = jnp.asarray(length_profile(number_of, total, limit, skew), jnp.int32)
    couples = (number_of - 1) // 2
    giver, sink = tallies[1:1 + 2 * couples:2], tallies[2:2 + 2 * couples:2]
    room = jnp.minimum(giver - 1, limit - sink)
    passed = jax.random.randint(jax.random.fold_in(key, 1), (couples,), 0, 1 << 20) % (room + 1)
    tallies = tallies.at[1:1 + 2 * couples:2].set(giver - passed).at[2:2 + 2 * couples:2].set(sink + passed)
    return tallies[jax.random.permutation(jax.random.fold_in(key, 2), number_of)]


def bell_draw(own_key, extent, width, bound, shards=(), held_as=jnp.bfloat16):
    values = width * jax.random.normal(own_key, extent, jnp.float32)
    if shards:
        values = values * level_of(own_key, extent, shards, -0.22, 0.18)
    return jnp.clip(values, -bound, bound).astype(held_as)


def setup_inputs(seed: int = 0) -> dict:
    key_of = jax.random.split(jax.random.key(seed), 12)
    return {
        "lin_query": bell_draw(key_of[0], (TOKENS, D), 1.0, 6.0, ((0, 64), (1, 4))),
        "lin_key": bell_draw(key_of[1], (TOKENS, D), 1.0, 6.0, ((0, 64), (1, 4))),
        "lin_value": bell_draw(key_of[2], (TOKENS, D), 1.0, 6.0, ((0, 64), (1, 4))),
        "out_gate": bell_draw(key_of[3], (TOKENS, D), 1.5, 6.0, ((0, 64), (1, 4))),
        "norm_gain": jnp.clip(1.0 + 0.15 * jax.random.normal(key_of[4], (D,), jnp.float32), 0.25, 1.75),
        "decay_rate": draw_decay_rate(jax.random.fold_in(key_of[11], 71), 0),
        "soft_query": draw_soft_query(jax.random.fold_in(key_of[11], 71), 0),
        "soft_key": draw_soft_key(jax.random.fold_in(key_of[11], 71), 0),
        "soft_value": bell_draw(key_of[8], (TOKENS, D), 1.0, 6.0, ((0, 64), (1, 4))),
        "doc_ids": jnp.searchsorted(jnp.cumsum(uneven_parts(key_of[9], NBLK // 4, NBLK, MOST, 2)), jnp.arange(NBLK), side="right").astype(jnp.int32),
        "block_mask": plant((jax.random.randint(key_of[10], (NBLK, NBLK), 0, 4) < 3).astype(jnp.int32), jax.random.fold_in(key_of[10], 1), 0, 1),
    }


def reference(lin_query, lin_key, lin_value, out_gate, norm_gain, decay_rate, soft_query, soft_key, soft_value, doc_ids, block_mask):
    highest = lax.Precision.HIGHEST
    offsets = jnp.arange(BLK).astype(jnp.float32)
    distance = offsets[:, None] - offsets[None, :]
    intra_decay = jnp.where(distance[None] >= 0, jnp.exp(-decay_rate[:, None, None] * jnp.maximum(distance, 0.0)[None]), 0.0)
    query_decay = jnp.exp(-decay_rate[None, :] * (offsets[:, None] + 1.0))
    key_decay = jnp.exp(-decay_rate[None, :] * (BLK - 1.0 - offsets[:, None]))
    block_decay = jnp.exp(-decay_rate * BLK)

    def lin_block(kv_state, inputs):
        query_part, key_part, value_part, gate_part = inputs
        query_wide = query_part.astype(jnp.float32)
        key_wide = key_part.astype(jnp.float32)
        value_wide = value_part.astype(jnp.float32)
        scores = jnp.einsum('ihd,jhd->hij', query_wide, key_wide, precision=highest)
        weights = lax.optimization_barrier((scores * intra_decay).astype(jnp.bfloat16)).astype(jnp.float32)
        local_part = jnp.einsum('hij,jhd->ihd', weights, value_wide, precision=highest)
        state_round = lax.optimization_barrier(kv_state.astype(jnp.bfloat16)).astype(jnp.float32)
        carried = jnp.einsum('ihd,hde->ihe', query_wide, state_round, precision=highest) * query_decay[:, :, None]
        decayed_keys = lax.optimization_barrier((key_wide * key_decay[:, :, None]).astype(jnp.bfloat16)).astype(jnp.float32)
        updated = block_decay[:, None, None] * kv_state + jnp.einsum('jhd,jhe->hde', decayed_keys, value_wide, precision=highest)
        combined = (local_part + carried).reshape(BLK, D)
        mean_square = lax.optimization_barrier(jnp.mean(combined * combined, axis=1, keepdims=True))
        normed = combined * lax.rsqrt(mean_square + 1e-06) * norm_gain[None, :] * jax.nn.sigmoid(gate_part.astype(jnp.float32))
        return (updated, normed.astype(jnp.bfloat16))

    def split_blocks(array):
        return array.reshape(NBLK, BLK, HEADS, HD)
    zero_state = jnp.zeros((HEADS, HD, HD), jnp.float32)
    final_state, lin_blocks = lax.scan(lin_block, zero_state, (split_blocks(lin_query), split_blocks(lin_key), split_blocks(lin_value), out_gate.reshape(NBLK, BLK, D)))
    lin_output = lin_blocks.reshape(TOKENS, D)
    score_scale = HD ** (-0.5)

    def soft_block(query_block):
        first_block = jnp.clip(query_block - MOST + 1, 0, NBLK - MOST).astype(jnp.int32)
        query_rows = lax.dynamic_slice_in_dim(soft_query, (query_block * BLK).astype(jnp.int32), BLK, 0).astype(jnp.float32).reshape(BLK, HEADS, HD)
        key_rows = lax.dynamic_slice_in_dim(soft_key, (first_block * BLK).astype(jnp.int32), MOST * BLK, 0).astype(jnp.float32).reshape(MOST * BLK, HEADS, HD)
        value_rows = lax.dynamic_slice_in_dim(soft_value, (first_block * BLK).astype(jnp.int32), MOST * BLK, 0).astype(jnp.float32).reshape(MOST * BLK, HEADS, HD)
        key_blocks = first_block + jnp.arange(MOST, dtype=jnp.int32)
        mask_row = lax.dynamic_slice_in_dim(block_mask, query_block, 1, 0)[0]
        picked = mask_row[key_blocks]
        block_ok = (key_blocks < query_block) & (picked == 1) & (doc_ids[key_blocks] == doc_ids[query_block])
        key_pos = first_block * BLK + jnp.arange(MOST * BLK, dtype=jnp.int32)
        query_pos = query_block * BLK + jnp.arange(BLK, dtype=jnp.int32)
        same_block = jnp.repeat(key_blocks == query_block, BLK)
        allowed = jnp.repeat(block_ok, BLK)[None, :] | same_block[None, :] & (key_pos[None, :] <= query_pos[:, None])
        scores = jnp.einsum('ihd,jhd->hij', query_rows, key_rows, precision=highest) * score_scale
        masked = jnp.where(allowed[None], scores, -1e+30)
        row_max = lax.optimization_barrier(jnp.max(masked, axis=2, keepdims=True))
        weights_raw = jnp.where(allowed[None], jnp.exp(masked - row_max), 0.0)
        denominator = lax.optimization_barrier(jnp.sum(weights_raw, axis=2))
        weights = lax.optimization_barrier(weights_raw.astype(jnp.bfloat16)).astype(jnp.float32)
        combined = jnp.einsum('hij,jhd->ihd', weights, value_rows, precision=highest) / denominator.T[:, :, None]
        return combined.reshape(BLK, D).astype(jnp.bfloat16)
    soft_output = lax.map(soft_block, jnp.arange(NBLK, dtype=jnp.int32)).reshape(TOKENS, D)
    return (lin_output, soft_output)
```

```python
import math

import jax
import jax.numpy as jnp
from jax import lax
from jax.experimental import pallas as pl
from jax.experimental.pallas import tpu as pltpu
from jax.sharding import PartitionSpec as P

HD = 128
BLK = 128
NBLK = 128
ROWS = 256
LOCAL = 8
WIDTH = LOCAL * HD
D = 4096
SHARDS = 64
FILL = -1e30
EXP2_SCALE = HD ** (-0.5) * math.log2(math.e)

f32 = jnp.float32
bf16 = jnp.bfloat16

SMEM = pl.BlockSpec(memory_space=pltpu.SMEM)
VMEM = pl.BlockSpec(memory_space=pltpu.VMEM)


def call(body, outs, ins, specs, flops, scratch=()):
    moved = sum(math.prod(x.shape) * x.dtype.itemsize for x in (*ins, *outs))
    return pl.pallas_call(
        body,
        out_shape=outs,
        in_specs=specs,
        out_specs=[VMEM] * len(outs),
        scratch_shapes=list(scratch),
        compiler_params=pltpu.CompilerParams(vmem_limit_bytes=32 * 1024 * 1024),
        cost_estimate=pl.CostEstimate(flops=flops, bytes_accessed=moved, transcendentals=0),
    )(*ins)


def cols(h):
    return slice(h * HD, (h + 1) * HD)


def dot(a, b, dims):
    return lax.dot_general(a, b, (dims, ((), ())), preferred_element_type=f32)


def exact_dot(a, b, dims):
    return lax.dot_general(
        a, b, (dims, ((), ())), precision=lax.Precision.HIGHEST, preferred_element_type=f32
    )


def state_body(rate, k, v, out):
    back = (ROWS - 1.0) - lax.broadcasted_iota(jnp.int32, (ROWS, HD), 0).astype(f32)
    for h in range(LOCAL):
        decayed = (k[:, cols(h)].astype(f32) * jnp.exp(-rate[h] * back)).astype(bf16)
        out[cols(h), :] = dot(decayed, v[:, cols(h)], ((0,), (0,))).astype(bf16)


def prefix_body(index, rate, parts, out):
    step = jnp.exp(jnp.full((16, HD), -rate[index[0] // 8] * ROWS, f32))
    state = jnp.zeros((16, HD), f32)
    for i in range(SHARDS):
        out[i] = state.astype(bf16)
        if i + 1 < SHARDS:
            state = step * state + parts[i].astype(f32)


def inner_body(rate, q, k, v, out):
    row = lax.broadcasted_iota(jnp.int32, (ROWS, ROWS), 0)
    col = lax.broadcasted_iota(jnp.int32, (ROWS, ROWS), 1)
    gap = (row - col).astype(f32)
    for h in range(LOCAL):
        decay = jnp.where(row >= col, jnp.exp(-rate[h] * jnp.maximum(gap, 0.0)), 0.0)
        scores = dot(q[:, cols(h)], k[:, cols(h)], ((1,), (1,)))
        out[:, cols(h)] = dot((scores * decay).astype(bf16), v[:, cols(h)], ((1,), (0,)))


def carry_body(rate, inner, q, state, heads, squares):
    ahead = lax.broadcasted_iota(jnp.int32, (ROWS, HD), 0).astype(f32) + 1.0
    total = jnp.zeros((ROWS, HD), f32)
    for h in range(LOCAL):
        carried = dot(q[:, cols(h)], state[cols(h), :], ((1,), (0,)))
        value = inner[:, cols(h)] + carried * jnp.exp(-rate[h] * ahead)
        heads[:, cols(h)] = value
        total = total + value * value
    squares[...] = exact_dot(jnp.ones((8, HD), f32), total, ((1,), (1,)))


def norm_body(heads, gate, gain, s0, s1, s2, s3, out):
    total = s0[...] + s1[...] + s2[...] + s3[...]
    first = (lax.broadcasted_iota(jnp.int32, (8, HD), 0) == 0).astype(f32)
    spread = exact_dot(total, first, ((0,), (0,)))
    inverse = lax.rsqrt(spread / D + 1e-06)
    for h in range(LOCAL):
        scale = gain[:, cols(h)] * jax.nn.sigmoid(gate[:, cols(h)].astype(f32))
        out[:, cols(h)] = (heads[:, cols(h)] * inverse * scale).astype(bf16)


def block_ok(docs, mask, i, query, key):
    q_at = jnp.clip(query, 0, NBLK - 1)
    k_at = jnp.clip(key, 0, NBLK - 1)
    inside = (key >= 0) & (key < query) & (query < NBLK)
    return inside & (mask[i, k_at] == 1) & (docs[k_at] == docs[q_at])


def fill_bias(bias, at, docs, mask, query, key, own):
    for i in range(2):
        for j in range(2):
            rows = slice(i * BLK, (i + 1) * BLK)
            columns = slice(at + j * BLK, at + (j + 1) * BLK)
            if own and i == j:
                row = lax.broadcasted_iota(jnp.int32, (BLK, BLK), 0)
                col = lax.broadcasted_iota(jnp.int32, (BLK, BLK), 1)
                bias[rows, columns] = jnp.where(col <= row, 0.0, FILL)
            else:
                ok = block_ok(docs, mask, i, query + i, key + j)
                bias[rows, columns] = jnp.full((BLK, BLK), jnp.where(ok, 0.0, FILL), f32)


def attend_head(q, keys, values, bias):
    scores = dot(q, keys, ((1,), (1,))) + bias
    top = jnp.max(scores, axis=1, keepdims=True)
    weights = jnp.exp2((scores - top) * EXP2_SCALE).astype(bf16)
    ones = jnp.ones(values.shape, bf16)
    both = dot(weights, jnp.concatenate([values, ones], axis=1), ((1,), (0,)))
    return both[:, :HD], top, both[:, HD:]


def joined(refs, h):
    return jnp.concatenate([ref[:, cols(h)] for ref in refs], axis=0)


def far_body(index, docs, mask, q, k1, k2, v1, v2, out, stats, bias):
    me = index[0]
    query = 2 * (me + 2)
    fill_bias(bias, 0, docs, mask, query, 2 * (me - 2), False)
    fill_bias(bias, ROWS, docs, mask, query, 2 * ((me ^ 1) - 2), False)
    lane = lax.broadcasted_iota(jnp.int32, (ROWS, HD), 1)
    table = jnp.zeros((ROWS, HD), f32)
    for h in range(LOCAL):
        acc, top, total = attend_head(
            q[:, cols(h)], joined((k1, k2), h), joined((v1, v2), h), bias[...]
        )
        out[:, cols(h)] = (acc / total).astype(bf16)
        table = jnp.where(lane == h, top, table)
        table = jnp.where(lane == LOCAL + h, total, table)
    stats[...] = table.T[: 2 * LOCAL, :]


def near_body(
    index, docs, mask, q, k0, k1, k2, k3, v0, v1, v2, v3, out, tops, sums, bias
):
    me = index[0]
    query = 2 * me
    for at, source in enumerate((me, me ^ 1, me - 2, (me ^ 1) - 2)):
        fill_bias(bias, at * ROWS, docs, mask, query, 2 * source, at == 0)
    lane = lax.broadcasted_iota(jnp.int32, (ROWS, HD), 1)
    top_table = jnp.zeros((ROWS, HD), f32)
    sum_table = jnp.zeros((ROWS, HD), f32)
    for h in range(LOCAL):
        acc, top, total = attend_head(
            q[:, cols(h)], joined((k0, k1, k2, k3), h), joined((v0, v1, v2, v3), h), bias[...]
        )
        out[:, cols(h)] = acc
        top_table = jnp.where(lane == h, top, top_table)
        sum_table = jnp.where(lane == h, total, sum_table)
    tops[...] = top_table
    sums[...] = sum_table


def merge_body(near, tops, sums, far, stats, out):
    table = jnp.concatenate([stats[...], jnp.zeros((HD - 2 * LOCAL, ROWS), f32)], axis=0).T
    for h in range(LOCAL):
        top1 = tops[:, h : h + 1]
        sum1 = sums[:, h : h + 1]
        top2 = table[:, h : h + 1]
        sum2 = table[:, LOCAL + h : LOCAL + h + 1]
        top = jnp.maximum(top1, top2)
        scale1 = jnp.exp2((top1 - top) * EXP2_SCALE)
        scale2 = jnp.exp2((top2 - top) * EXP2_SCALE) * sum2
        total = scale1 * sum1 + scale2
        value = near[:, cols(h)] * (scale1 / total) + far[:, cols(h)].astype(f32) * (scale2 / total)
        out[:, cols(h)] = value.astype(bf16)


def shifted(x, distance):
    return lax.ppermute(x, "seq", [(i, (i + distance) % SHARDS) for i in range(SHARDS)])


def swapped(x):
    return lax.ppermute(x, "seq", [(i, i ^ 1) for i in range(SHARDS)])


def turned(x, distance):
    return lax.ppermute(x, "head", [(i, (i + distance) % 4) for i in range(4)])


def per_device(
    lin_query,
    lin_key,
    lin_value,
    out_gate,
    norm_gain,
    decay_rate,
    soft_query,
    soft_key,
    soft_value,
    doc_ids,
    block_mask,
):
    like = jax.ShapeDtypeStruct
    index = lax.axis_index("seq").astype(jnp.int32).reshape(1)
    wide = like((ROWS, WIDTH), f32)
    narrow = like((ROWS, WIDTH), bf16)

    key1 = shifted(soft_key, 2)
    value1 = shifted(soft_value, 2)
    query1 = shifted(soft_query, -2)
    mask1 = shifted(block_mask, -2)
    key_other = swapped(soft_key)
    value_other = swapped(soft_value)
    key2 = swapped(key1)
    value2 = swapped(value1)

    (state,) = call(
        state_body,
        [like((WIDTH, HD), bf16)],
        (decay_rate, lin_key, lin_value),
        [SMEM, VMEM, VMEM],
        2 * ROWS * WIDTH * HD,
    )
    parts = lax.all_to_all(state.reshape(SHARDS, 16, HD), "seq", 0, 0)
    (prefix,) = call(
        prefix_body,
        [like((SHARDS, 16, HD), bf16)],
        (index, decay_rate, parts),
        [SMEM, SMEM, VMEM],
        4 * SHARDS * 16 * HD,
    )
    entering = lax.all_to_all(prefix, "seq", 0, 0).reshape(WIDTH, HD)
    (inner,) = call(
        inner_body,
        [wide],
        (decay_rate, lin_query, lin_key, lin_value),
        [SMEM, VMEM, VMEM, VMEM],
        4 * ROWS * ROWS * WIDTH,
    )
    heads, squares = call(
        carry_body,
        [wide, like((8, ROWS), f32)],
        (decay_rate, inner, lin_query, entering),
        [SMEM, VMEM, VMEM, VMEM],
        2 * ROWS * WIDTH * HD,
    )
    others = [turned(squares, d) for d in (1, 2, 3)]
    (lin_output,) = call(
        norm_body,
        [narrow],
        (heads, out_gate, norm_gain.reshape(1, WIDTH), squares, *others),
        [VMEM] * 7,
        8 * ROWS * WIDTH,
    )

    far, far_stats = call(
        far_body,
        [narrow, like((2 * LOCAL, ROWS), f32)],
        (index, doc_ids, mask1, query1, key1, key2, value1, value2),
        [SMEM] * 3 + [VMEM] * 5,
        4 * ROWS * 2 * ROWS * WIDTH,
        [pltpu.VMEM((ROWS, 2 * ROWS), f32)],
    )
    far = shifted(far, 2)
    far_stats = shifted(far_stats, 2)
    near, tops, sums = call(
        near_body,
        [wide, like((ROWS, HD), f32), like((ROWS, HD), f32)],
        (
            index, doc_ids, block_mask, soft_query,
            soft_key, key_other, key1, key2,
            soft_value, value_other, value1, value2,
        ),
        [SMEM] * 3 + [VMEM] * 9,
        4 * ROWS * 4 * ROWS * WIDTH,
        [pltpu.VMEM((ROWS, 4 * ROWS), f32)],
    )
    (soft_output,) = call(
        merge_body,
        [narrow],
        (near, tops, sums, far, far_stats),
        [VMEM] * 5,
        8 * ROWS * WIDTH,
    )
    return (lin_output, soft_output)


def solution(mesh):
    rows = P("seq", "head")
    return jax.shard_map(
        per_device,
        mesh=mesh,
        in_specs=(
            rows, rows, rows, rows, P("head"), P("head"), rows, rows, rows, P(), P("seq", None),
        ),
        out_specs=(rows, rows),
        check_vma=False,
    )
```

```python
import math

import jax
import jax.numpy as jnp
from jax import lax
from jax.experimental import pallas as pl
from jax.experimental.pallas import tpu as pltpu
from jax.sharding import PartitionSpec as P

HD = 128
BLK = 128
NBLK = 128
ROWS = 256
LOCAL = 8
WIDTH = LOCAL * HD
HALF = WIDTH // 2
D = 4096
SHARDS = 64
FILL = -1e30
PREFIX_COST = 5_000_000_000
CARRY_COST = 10_000_000_000
EXP2_SCALE = HD ** (-0.5) * math.log2(math.e)

f32 = jnp.float32
bf16 = jnp.bfloat16

SMEM = pl.BlockSpec(memory_space=pltpu.SMEM)
VMEM = pl.BlockSpec(memory_space=pltpu.VMEM)


def call(body, outs, ins, specs, scratch=(), flops=1, room=16):
    return pl.pallas_call(
        body,
        out_shape=outs,
        in_specs=specs,
        out_specs=[VMEM] * len(outs),
        scratch_shapes=list(scratch),
        compiler_params=pltpu.CompilerParams(vmem_limit_bytes=room * 1024 * 1024),
        cost_estimate=pl.CostEstimate(flops=flops, bytes_accessed=1, transcendentals=0),
    )(*ins)


def cols(h):
    return slice(h * HD, (h + 1) * HD)


def dot(a, b, dims):
    return lax.dot_general(a, b, (dims, ((), ())), preferred_element_type=f32)


def exact_dot(a, b, dims):
    return lax.dot_general(
        a, b, (dims, ((), ())), precision=lax.Precision.HIGHEST, preferred_element_type=f32
    )


def state_body(rate_hbm, k_hbm, v_hbm, first, out, rate, k, v, rate_sem, k_sem, v_sem):
    def chunk(g):
        return slice(g * 2 * HD, (g + 1) * 2 * HD)

    copies = [pltpu.make_async_copy(rate_hbm, rate, rate_sem)]
    for g in range(LOCAL // 2):
        at = chunk(g)
        copies.append(pltpu.make_async_copy(k_hbm.at[:, at], k.at[:, at], k_sem.at[g]))
        copies.append(pltpu.make_async_copy(v_hbm.at[:, at], v.at[:, at], v_sem.at[g]))
    for copy in copies:
        copy.start()
    copies[0].wait()
    back = (BLK - 1.0) - lax.broadcasted_iota(jnp.int32, (BLK, HD), 0).astype(f32)
    for g in range(LOCAL // 2):
        copies[2 * g + 1].wait()
        copies[2 * g + 2].wait()
        for h in (2 * g, 2 * g + 1):
            decay = jnp.exp(-rate[h] * back)
            parts = []
            for b in range(2):
                rows = slice(b * BLK, (b + 1) * BLK)
                decayed = (k[rows, cols(h)].astype(f32) * decay).astype(bf16)
                parts.append(dot(decayed, v[rows, cols(h)], ((0,), (0,))))
            step = jnp.exp(jnp.full((HD, HD), -rate[h] * BLK, f32))
            first[cols(h), :] = parts[0]
            out[cols(h), :] = (step * parts[0] + parts[1]).astype(bf16)


def prefix_body(index, rate, parts, out):
    step = jnp.exp(jnp.full((16, HD), -rate[index[0] // 8] * ROWS, f32))
    state = jnp.zeros((16, HD), f32)
    for i in range(SHARDS):
        out[i] = state.astype(bf16)
        if i + 1 < SHARDS:
            state = step * state + parts[i].astype(f32)


def inner_body(rate, q, k, v, out):
    row = lax.broadcasted_iota(jnp.int32, (BLK, BLK), 0)
    col = lax.broadcasted_iota(jnp.int32, (BLK, BLK), 1)
    gap = jnp.maximum(row - col, 0).astype(f32)
    for h in range(LOCAL):
        decay = jnp.where(row >= col, jnp.exp(-rate[h] * gap), 0.0)
        for b in range(2):
            rows = slice(b * BLK, (b + 1) * BLK)
            scores = dot(q[rows, cols(h)], k[rows, cols(h)], ((1,), (1,)))
            out[rows, cols(h)] = dot(
                (scores * decay).astype(bf16), v[rows, cols(h)], ((1,), (0,))
            )


def carry_body(rate, inner, q, first, state, heads, squares):
    ahead = lax.broadcasted_iota(jnp.int32, (BLK, HD), 0).astype(f32) + 1.0
    totals = [jnp.zeros((BLK, HD), f32)] * 2
    for h in range(LOCAL):
        step = jnp.exp(jnp.full((HD, HD), -rate[h] * BLK, f32))
        decay = jnp.exp(-rate[h] * ahead)
        entering = state[cols(h), :]
        middle = (step * entering.astype(f32) + first[cols(h), :]).astype(bf16)
        for b, block_state in enumerate((entering, middle)):
            rows = slice(b * BLK, (b + 1) * BLK)
            carried = dot(q[rows, cols(h)], block_state, ((1,), (0,)))
            value = inner[rows, cols(h)] + carried * decay
            heads[rows, cols(h)] = value
            totals[b] = totals[b] + value * value
    total = jnp.concatenate(totals, axis=0)
    squares[...] = exact_dot(jnp.ones((8, HD), f32), total, ((1,), (1,)))


def norm_body(heads, gate, gain, s0, s1, s2, s3, out):
    total = s0[...] + s1[...] + s2[...] + s3[...]
    first = (lax.broadcasted_iota(jnp.int32, (8, HD), 0) == 0).astype(f32)
    spread = exact_dot(total, first, ((0,), (0,)))
    inverse = lax.rsqrt(spread / D + 1e-06)
    for h in range(LOCAL):
        scale = gain[:, cols(h)] * jax.nn.sigmoid(gate[:, cols(h)].astype(f32))
        out[:, cols(h)] = (heads[:, cols(h)] * inverse * scale).astype(bf16)


def half(c):
    return pl.ds(pl.multiple_of(c * HALF, HALF), HALF)


def split_body(index, mask, q, k, v, out, sem):
    other = 1 - index[0] % 2
    copies = [
        pltpu.make_async_copy(
            ref.at[:, half(other)], out.at[at * ROWS : (at + 1) * ROWS, :], sem.at[at]
        )
        for at, ref in enumerate((q, k, v))
    ]
    for copy in copies:
        copy.start()
    flags = mask[...].astype(f32)
    flags = jnp.concatenate([flags, jnp.zeros((14, NBLK), f32)], axis=0).astype(bf16)
    out[3 * ROWS :, :] = jnp.concatenate([flags] * 4, axis=1)
    for copy in copies:
        copy.wait()


def gather_body(index, mask, q, k, v, other, near_q, far_q, pair, flags):
    core = index[0] % 2

    def lay(own, at, mine):
        theirs = other[at * ROWS : (at + 1) * ROWS, :]
        first = jnp.where(core == 0, mine, theirs)
        second = jnp.where(core == 0, theirs, mine)
        return first, second

    q0, q1 = lay(q, 0, q[:, half(core)])
    near_q[:ROWS, :] = q0
    near_q[ROWS:, :] = q1
    far_q[:ROWS, :] = q0
    far_q[ROWS : 3 * BLK, :] = q1[:BLK]
    for at, ref in ((1, k), (2, v)):
        low, high = lay(ref, at, ref[:, half(core)])
        base = (at - 1) * 2 * ROWS
        pair[base : base + ROWS, :] = low
        pair[base + ROWS : base + 2 * ROWS, :] = high
    own = mask[...].astype(f32)
    theirs = other[3 * ROWS :, :NBLK].astype(f32)[:2]
    first = jnp.where(core == 0, own, theirs)
    second = jnp.where(core == 0, theirs, own)
    rows = jnp.concatenate([first, second, jnp.zeros((12, NBLK), f32)], axis=0)
    flags[...] = rows
    far_q[3 * BLK :, :] = jnp.concatenate([rows.astype(bf16)] * 4, axis=1)


def allowed(docs, flags, i, query, key):
    q_at = jnp.clip(query, 0, NBLK - 1)
    k_at = jnp.clip(key, 0, NBLK - 1)
    inside = (key >= 0) & (key < query) & (query < NBLK) & (docs[k_at] == docs[q_at])
    lane = lax.broadcasted_iota(jnp.int32, (1, NBLK), 1)
    wanted = jnp.where(inside, k_at, -1)
    ok = jnp.sum(jnp.where(lane == wanted, flags[i : i + 1, :], 0.0), axis=1, keepdims=True)
    return jnp.broadcast_to(jnp.where(ok > 0.5, 0.0, FILL), (BLK, BLK))


def block(i):
    return slice(i * BLK, (i + 1) * BLK)


def attend_head(q, keys, values, bias):
    scores = dot(q, keys, ((1,), (1,))) + bias
    top = jnp.max(scores, axis=1, keepdims=True)
    weights = jnp.exp2((scores - top) * EXP2_SCALE).astype(bf16)
    ones = jnp.ones(values.shape, bf16)
    both = dot(weights, jnp.concatenate([values, ones], axis=1), ((1,), (0,)))
    return both[:, :HD], top, both[:, HD:]


def far_body(index, docs, q, pair, out, bias):
    chip = index[0] // 2
    flags = q[3 * BLK :, :NBLK].astype(f32)
    for i in range(3):
        for j in range(3):
            bias[block(i), block(j)] = allowed(
                docs, flags, i, 4 * (chip + 1) + i, 4 * (chip - 1) + 1 + j
            )
    lane = lax.broadcasted_iota(jnp.int32, (3 * BLK, HD), 1)
    table = jnp.zeros((3 * BLK, HD), f32)
    for h in range(LOCAL // 2):
        acc, top, total = attend_head(
            q[: 3 * BLK, cols(h)],
            pair[BLK : 4 * BLK, cols(h)],
            pair[5 * BLK :, cols(h)],
            bias[...],
        )
        out[: 3 * BLK, cols(h)] = (acc / total).astype(bf16)
        table = jnp.where(lane == h, top, table)
        table = jnp.where(lane == LOCAL // 2 + h, total, table)
    rest = table.T[:LOCAL, :]
    rest = jnp.concatenate([rest, jnp.zeros((LOCAL, 3 * BLK), f32)], axis=0)
    rest = jnp.concatenate([rest, jnp.zeros((2 * LOCAL, BLK), f32)], axis=1)
    for piece in range(3):
        part = rest.astype(bf16)
        out[3 * BLK + piece * 2 * LOCAL : 3 * BLK + (piece + 1) * 2 * LOCAL, :] = part
        rest = rest - part.astype(f32)


def near_body(
    index, docs, flags, q, own, pair, out, tops, sums, bias
):
    chip = index[0] // 2
    rows = flags[...]
    for i in range(4):
        for j in range(4):
            if j == i:
                row = lax.broadcasted_iota(jnp.int32, (BLK, BLK), 0)
                col = lax.broadcasted_iota(jnp.int32, (BLK, BLK), 1)
                bias[block(i), block(j)] = jnp.where(col <= row, 0.0, FILL)
            elif j > i:
                bias[block(i), block(j)] = jnp.full((BLK, BLK), FILL, f32)
            else:
                bias[block(i), block(j)] = allowed(docs, rows, i, 4 * chip + i, 4 * chip + j)
            bias[block(i), block(4 + j)] = allowed(
                docs, rows, i, 4 * chip + i, 4 * (chip - 1) + j
            )
    lane = lax.broadcasted_iota(jnp.int32, (4 * BLK, HD), 1)
    top_table = jnp.zeros((4 * BLK, HD), f32)
    sum_table = jnp.zeros((4 * BLK, HD), f32)
    for h in range(LOCAL // 2):
        keys = jnp.concatenate([own[: 4 * BLK, cols(h)], pair[: 4 * BLK, cols(h)]], axis=0)
        values = jnp.concatenate([own[4 * BLK :, cols(h)], pair[4 * BLK :, cols(h)]], axis=0)
        acc, top, total = attend_head(q[:, cols(h)], keys, values, bias[...])
        out[:, cols(h)] = acc / total
        top_table = jnp.where(lane == h, top, top_table)
        sum_table = jnp.where(lane == h, total, sum_table)
    tops[...] = top_table
    sums[...] = sum_table


def merge_body(near, tops, sums, far, out):
    stats = jnp.zeros((2 * LOCAL, HALF), f32)
    for p in range(3):
        at = 3 * BLK + p * 2 * LOCAL
        stats = stats + far[at : at + 2 * LOCAL, :].astype(f32)
    heads = LOCAL // 2
    pad = jnp.zeros((HD - heads, 3 * BLK), f32)
    far_tops = jnp.concatenate([stats[:heads, : 3 * BLK], pad], axis=0).T
    far_sums = jnp.concatenate([stats[heads:LOCAL, : 3 * BLK], pad], axis=0).T
    rows = slice(0, 3 * BLK)
    top = jnp.maximum(tops[rows, :], far_tops)
    near_part = jnp.exp2((tops[rows, :] - top) * EXP2_SCALE) * sums[rows, :]
    far_part = jnp.exp2((far_tops - top) * EXP2_SCALE) * far_sums
    lane = lax.broadcasted_iota(jnp.int32, (3 * BLK, HD), 1)
    share = jnp.where(lane < heads, far_part / (near_part + far_part), 0.0)
    for h in range(heads):
        own = near[rows, cols(h)]
        there = far[rows, cols(h)].astype(f32)
        out[rows, cols(h)] = (own + (there - own) * share[:, h : h + 1]).astype(bf16)
        out[3 * BLK :, cols(h)] = near[3 * BLK :, cols(h)].astype(bf16)


def part_body(index, merged, mine, send):
    core = index[0] % 2
    mine[...] = merged[pl.ds(pl.multiple_of(core * ROWS, ROWS), ROWS), :]
    send[...] = merged[pl.ds(pl.multiple_of((1 - core) * ROWS, ROWS), ROWS), :]


def place_body(index, mine, other, out):
    core = index[0] % 2
    out[:, half(core)] = mine[...]
    out[:, half(1 - core)] = other[...]


def shifted(x, distance):
    return lax.ppermute(x, "seq", [(i, (i + distance) % SHARDS) for i in range(SHARDS)])


def swapped(x):
    return lax.ppermute(x, "seq", [(i, i ^ 1) for i in range(SHARDS)])


def turned(x, distance):
    return lax.ppermute(x, "head", [(i, (i + distance) % 4) for i in range(4)])


def per_device(
    lin_query,
    lin_key,
    lin_value,
    out_gate,
    norm_gain,
    decay_rate,
    soft_query,
    soft_key,
    soft_value,
    doc_ids,
    block_mask,
):
    like = jax.ShapeDtypeStruct
    index = lax.axis_index("seq").astype(jnp.int32).reshape(1)
    wide = like((ROWS, WIDTH), f32)
    narrow = like((ROWS, WIDTH), bf16)

    (sent,) = call(
        split_body,
        [like((3 * ROWS + 16, HALF), bf16)],
        (index, block_mask, soft_query, soft_key, soft_value),
        [SMEM, VMEM] + [pl.BlockSpec(memory_space=pl.ANY)] * 3,
        [pltpu.SemaphoreType.DMA((3,))],
        room=56,
    )
    other = swapped(sent)
    first, state = pl.pallas_call(
        state_body,
        out_shape=[like((WIDTH, HD), f32), like((WIDTH, HD), bf16)],
        in_specs=[pl.BlockSpec(memory_space=pl.ANY)] * 3,
        out_specs=[VMEM] * 2,
        scratch_shapes=[
            pltpu.SMEM((LOCAL,), f32),
            pltpu.VMEM((ROWS, WIDTH), bf16),
            pltpu.VMEM((ROWS, WIDTH), bf16),
            pltpu.SemaphoreType.DMA,
            pltpu.SemaphoreType.DMA((LOCAL // 2,)),
            pltpu.SemaphoreType.DMA((LOCAL // 2,)),
        ],
        compiler_params=pltpu.CompilerParams(vmem_limit_bytes=56 * 1024 * 1024),
        cost_estimate=pl.CostEstimate(
            flops=1, bytes_accessed=1, transcendentals=0
        ),
    )(decay_rate, lin_key, lin_value)
    parts = lax.all_to_all(state.reshape(SHARDS, 16, HD), "seq", 0, 0)
    near_q, far_q, own_pair, flags = call(
        gather_body,
        [
            like((2 * ROWS, HALF), bf16),
            like((3 * BLK + 16, HALF), bf16),
            like((8 * BLK, HALF), bf16),
            like((16, NBLK), f32),
        ],
        (index, block_mask, soft_query, soft_key, soft_value, other),
        [SMEM] + [VMEM] * 5,
        room=56,
    )
    pair = shifted(own_pair, 2)
    next_q = shifted(far_q, -2)

    (prefix,) = call(
        prefix_body,
        [like((SHARDS, 16, HD), bf16)],
        (index, decay_rate, parts),
        [SMEM, SMEM, VMEM],
        flops=PREFIX_COST,
    )
    prefix, next_q = lax.optimization_barrier((prefix, next_q))
    entering = lax.all_to_all(prefix, "seq", 0, 0).reshape(WIDTH, HD)
    (inner,) = call(
        inner_body,
        [wide],
        (decay_rate, lin_query, lin_key, lin_value),
        [SMEM, VMEM, VMEM, VMEM],
    )
    (far,) = call(
        far_body,
        [like((3 * BLK + 48, HALF), bf16)],
        (index, doc_ids, next_q, pair),
        [SMEM] * 2 + [VMEM] * 2,
        [pltpu.VMEM((3 * BLK, 3 * BLK), f32)],
    )
    far = shifted(far, 2)
    near, tops, sums = call(
        near_body,
        [like((4 * BLK, HALF), f32), like((4 * BLK, HD), f32), like((4 * BLK, HD), f32)],
        (index, doc_ids, flags, near_q, own_pair, pair),
        [SMEM] * 2 + [VMEM] * 4,
        [pltpu.VMEM((4 * BLK, 8 * BLK), f32)],
    )
    near, inner = lax.optimization_barrier((near, inner))
    heads, squares = call(
        carry_body,
        [wide, like((8, ROWS), f32)],
        (decay_rate, inner, lin_query, first, entering),
        [SMEM] + [VMEM] * 4,
        flops=CARRY_COST,
    )
    others = [turned(squares, d) for d in (1, 2, 3)]
    far, heads = lax.optimization_barrier((far, heads))
    (merged,) = call(
        merge_body, [like((4 * BLK, HALF), bf16)], (near, tops, sums, far), [VMEM] * 4
    )
    merged, *others = lax.optimization_barrier((merged, *others))
    (lin_output,) = call(
        norm_body,
        [narrow],
        (heads, out_gate, norm_gain.reshape(1, WIDTH), squares, *others),
        [VMEM] * 7,
    )

    mine, send = call(
        part_body, [like((ROWS, HALF), bf16)] * 2, (index, merged), [SMEM, VMEM]
    )
    (soft_output,) = call(
        place_body, [narrow], (index, mine, swapped(send)), [SMEM, VMEM, VMEM]
    )
    return (lin_output, soft_output)


def solution(mesh):
    rows = P("seq", "head")
    return jax.shard_map(
        per_device,
        mesh=mesh,
        in_specs=(
            rows, rows, rows, rows, P("head"), P("head"), rows, rows, rows, P(), P("seq", None),
        ),
        out_specs=(rows, rows),
        check_vma=False,
    )
```

```python
import math

import jax
import jax.numpy as jnp
from jax import lax
from jax.experimental import pallas as pl
from jax.experimental.pallas import tpu as pltpu
from jax.sharding import PartitionSpec as P

HD = 128
BLK = 128
NBLK = 128
ROWS = 256
LOCAL = 8
WIDTH = LOCAL * HD
HALF = WIDTH // 2
HEADS = LOCAL // 2
D = 4096
SHARDS = 64
FILL = -1e30
PREFIX_COST = 5_000_000_000
CARRY_COST = 10_000_000_000
EXP2_SCALE = HD ** (-0.5) * math.log2(math.e)

f32 = jnp.float32
bf16 = jnp.bfloat16

SMEM = pl.BlockSpec(memory_space=pltpu.SMEM)
VMEM = pl.BlockSpec(memory_space=pltpu.VMEM)


def call(body, outs, ins, specs, scratch=(), flops=1, room=16):
    return pl.pallas_call(
        body,
        out_shape=outs,
        in_specs=specs,
        out_specs=[VMEM] * len(outs),
        scratch_shapes=list(scratch),
        compiler_params=pltpu.CompilerParams(vmem_limit_bytes=room * 1024 * 1024),
        cost_estimate=pl.CostEstimate(flops=flops, bytes_accessed=1, transcendentals=0),
    )(*ins)


def cols(h):
    return slice(h * HD, (h + 1) * HD)


def dot(a, b, dims):
    return lax.dot_general(a, b, (dims, ((), ())), preferred_element_type=f32)


def exact_dot(a, b, dims):
    return lax.dot_general(
        a, b, (dims, ((), ())), precision=lax.Precision.HIGHEST, preferred_element_type=f32
    )


def start_body(
    index, rate_hbm, mask, k_hbm, v_hbm, sq, sk, sv, first, out, sent, rate, k, v, rate_sem, sems
):
    other = 1 - index[0] % 2
    copies = [pltpu.make_async_copy(rate_hbm, rate, rate_sem)]
    for g in range(LOCAL // 2):
        at = slice(g * 2 * HD, (g + 1) * 2 * HD)
        copies.append(pltpu.make_async_copy(k_hbm.at[:, at], k.at[:, at], sems.at[2 * g]))
        copies.append(pltpu.make_async_copy(v_hbm.at[:, at], v.at[:, at], sems.at[2 * g + 1]))
    for at, ref in enumerate((sq, sk, sv)):
        rows = slice(at * ROWS, (at + 1) * ROWS)
        copies.append(
            pltpu.make_async_copy(ref.at[:, half(other)], sent.at[rows, :], sems.at[LOCAL + at])
        )
    for copy in copies:
        copy.start()
    flags = mask[...].astype(f32)
    flags = jnp.concatenate([flags, jnp.zeros((14, NBLK), f32)], axis=0).astype(bf16)
    sent[3 * ROWS :, :] = jnp.concatenate([flags] * 4, axis=1)
    copies[0].wait()
    back = (BLK - 1.0) - lax.broadcasted_iota(jnp.int32, (BLK, HD), 0).astype(f32)
    for g in range(LOCAL // 2):
        copies[2 * g + 1].wait()
        copies[2 * g + 2].wait()
        for h in (2 * g, 2 * g + 1):
            decay = jnp.exp(-rate[h] * back)
            parts = []
            for b in range(2):
                rows = slice(b * BLK, (b + 1) * BLK)
                decayed = (k[rows, cols(h)].astype(f32) * decay).astype(bf16)
                parts.append(dot(decayed, v[rows, cols(h)], ((0,), (0,))))
            step = jnp.exp(jnp.full((HD, HD), -rate[h] * BLK, f32))
            first[cols(h), :] = parts[0]
            out[cols(h), :] = (step * parts[0] + parts[1]).astype(bf16)
    for copy in copies[LOCAL + 1 :]:
        copy.wait()


def prefix_body(index, rate, parts, out):
    step = jnp.exp(jnp.full((16, HD), -rate[index[0] // 8] * ROWS, f32))
    state = jnp.zeros((16, HD), f32)
    for i in range(SHARDS):
        out[i] = state.astype(bf16)
        if i + 1 < SHARDS:
            state = step * state + parts[i].astype(f32)


def inner_body(rate, q, k, v, out):
    row = lax.broadcasted_iota(jnp.int32, (BLK, BLK), 0)
    col = lax.broadcasted_iota(jnp.int32, (BLK, BLK), 1)
    gap = jnp.maximum(row - col, 0).astype(f32)
    for h in range(LOCAL):
        decay = jnp.where(row >= col, jnp.exp(-rate[h] * gap), 0.0)
        for b in range(2):
            rows = slice(b * BLK, (b + 1) * BLK)
            scores = dot(q[rows, cols(h)], k[rows, cols(h)], ((1,), (1,)))
            out[rows, cols(h)] = dot(
                (scores * decay).astype(bf16), v[rows, cols(h)], ((1,), (0,))
            )


def carry_body(
    rate_hbm, inner_hbm, q_hbm, first_hbm, state, heads, squares, rate, inner, q, first, rate_sem, sems
):
    copies = [pltpu.make_async_copy(rate_hbm, rate, rate_sem)]
    for g in range(LOCAL // 2):
        at = slice(g * 2 * HD, (g + 1) * 2 * HD)
        copies.append(pltpu.make_async_copy(q_hbm.at[:, at], q.at[:, at], sems.at[3 * g]))
        copies.append(pltpu.make_async_copy(first_hbm.at[at, :], first.at[at, :], sems.at[3 * g + 1]))
        copies.append(pltpu.make_async_copy(inner_hbm.at[:, at], inner.at[:, at], sems.at[3 * g + 2]))
    for copy in copies:
        copy.start()
    copies[0].wait()
    ahead = lax.broadcasted_iota(jnp.int32, (BLK, HD), 0).astype(f32) + 1.0
    totals = [jnp.zeros((BLK, HD), f32)] * 2
    for h in range(LOCAL):
        if h % 2 == 0:
            for copy in copies[3 * (h // 2) + 1 : 3 * (h // 2) + 4]:
                copy.wait()
        step = jnp.exp(jnp.full((HD, HD), -rate[h] * BLK, f32))
        decay = jnp.exp(-rate[h] * ahead)
        entering = state[cols(h), :]
        middle = (step * entering.astype(f32) + first[cols(h), :]).astype(bf16)
        for b, block_state in enumerate((entering, middle)):
            rows = slice(b * BLK, (b + 1) * BLK)
            carried = dot(q[rows, cols(h)], block_state, ((1,), (0,)))
            value = inner[rows, cols(h)] + carried * decay
            heads[rows, cols(h)] = value
            totals[b] = totals[b] + value * value
    total = jnp.concatenate(totals, axis=0)
    squares[...] = exact_dot(jnp.ones((8, HD), f32), total, ((1,), (1,)))


def norm_body(heads, gate, gain, s0, s1, s2, s3, out):
    total = s0[...] + s1[...] + s2[...] + s3[...]
    first = (lax.broadcasted_iota(jnp.int32, (8, HD), 0) == 0).astype(f32)
    spread = exact_dot(total, first, ((0,), (0,)))
    inverse = lax.rsqrt(spread / D + 1e-06)
    for h in range(LOCAL):
        scale = gain[:, cols(h)] * jax.nn.sigmoid(gate[:, cols(h)].astype(f32))
        out[:, cols(h)] = (heads[:, cols(h)] * inverse * scale).astype(bf16)


def half(c):
    return pl.ds(pl.multiple_of(c * HALF, HALF), HALF)


def gather_body(index, mask, q, k, v, other, near_q, far_q, pair, tail, flags):
    core = index[0] % 2

    def lay(at, mine):
        theirs = other[at * ROWS : (at + 1) * ROWS, :]
        first = jnp.where(core == 0, mine, theirs)
        second = jnp.where(core == 0, theirs, mine)
        return first, second

    for at, ref in enumerate((q, k, v)):
        low, high = lay(at, ref[:, half(core)])
        if at == 0:
            for out in (near_q, far_q):
                out[:ROWS, :] = low
                out[ROWS : 2 * ROWS, :] = high
        else:
            base = (at - 1) * 2 * ROWS
            pair[base : base + ROWS, :] = low
            pair[base + ROWS : base + 2 * ROWS, :] = high
            base = (at - 1) * 3 * BLK
            tail[base : base + BLK, :] = low[BLK:]
            tail[base + BLK : base + 3 * BLK, :] = high
    own = mask[...].astype(f32)
    theirs = other[3 * ROWS :, :NBLK].astype(f32)[:2]
    first = jnp.where(core == 0, own, theirs)
    second = jnp.where(core == 0, theirs, own)
    rows = jnp.concatenate([first, second, jnp.zeros((12, NBLK), f32)], axis=0)
    flags[...] = rows
    far_q[4 * BLK :, :] = jnp.concatenate([rows.astype(bf16)] * 4, axis=1)


def allowed(docs, flags, i, query, key):
    q_at = jnp.clip(query, 0, NBLK - 1)
    k_at = jnp.clip(key, 0, NBLK - 1)
    inside = (key >= 0) & (key < query) & (query < NBLK) & (docs[k_at] == docs[q_at])
    lane = lax.broadcasted_iota(jnp.int32, (1, NBLK), 1)
    wanted = jnp.where(inside, k_at, -1)
    ok = jnp.sum(jnp.where(lane == wanted, flags[i : i + 1, :], 0.0), axis=1, keepdims=True)
    return jnp.broadcast_to(jnp.where(ok > 0.5, 0.0, FILL), (BLK, BLK))


def block(i):
    return slice(i * BLK, (i + 1) * BLK)


def attend_head(q, keys, values, bias):
    scores = dot(q, keys, ((1,), (1,))) + bias
    top = jnp.max(scores, axis=1, keepdims=True)
    weights = jnp.exp2((scores - top) * EXP2_SCALE).astype(bf16)
    ones = jnp.ones(values.shape, bf16)
    both = dot(weights, jnp.concatenate([values, ones], axis=1), ((1,), (0,)))
    return both[:, :HD], top, both[:, HD:]


def attend_chip(index, docs, rows, ahead, q, pair, out, tops, sums, bias):
    chip = index[0] // 2
    for i in range(4):
        for j in range(4):
            if ahead == 0 and j == i:
                row = lax.broadcasted_iota(jnp.int32, (BLK, BLK), 0)
                col = lax.broadcasted_iota(jnp.int32, (BLK, BLK), 1)
                bias[block(i), block(j)] = jnp.where(col <= row, 0.0, FILL)
            elif ahead == 0 and j > i:
                bias[block(i), block(j)] = jnp.full((BLK, BLK), FILL, f32)
            else:
                bias[block(i), block(j)] = allowed(
                    docs, rows, i, 4 * (chip + ahead) + i, 4 * chip + j
                )
    lane = lax.broadcasted_iota(jnp.int32, (2 * BLK, HD), 1)
    for r in range(2):
        part = slice(r * 2 * BLK, (r + 1) * 2 * BLK)
        count = 4 * BLK if ahead or r else 2 * BLK
        top_table = jnp.zeros((2 * BLK, HD), f32)
        sum_table = jnp.zeros((2 * BLK, HD), f32)
        for h in range(HEADS):
            acc, top, total = attend_head(
                q[part, cols(h)],
                pair[:count, cols(h)],
                pair[4 * BLK : 4 * BLK + count, cols(h)],
                bias[part, :count],
            )
            out[part, cols(h)] = acc / total
            top_table = jnp.where(lane == h, top, top_table)
            sum_table = jnp.where(lane == h, total, sum_table)
        tops[part, :] = top_table
        sums[part, :] = sum_table


def near_body(index, docs, flags, q, pair, out, tops, sums, bias):
    attend_chip(index, docs, flags[...], 0, q, pair, out, tops, sums, bias)


def next_body(index, docs, q, pair, out, tops, sums, bias):
    rows = q[4 * BLK :, :NBLK].astype(f32)
    attend_chip(index, docs, rows, 1, q, pair, out, tops, sums, bias)


def weighed(top1, sum1, top2, sum2):
    top = jnp.maximum(top1, top2)
    part1 = jnp.exp2((top1 - top) * EXP2_SCALE) * sum1
    part2 = jnp.exp2((top2 - top) * EXP2_SCALE) * sum2
    return top, part1 + part2, part2 / (part1 + part2)


def far_body(index, docs, q, tail, done, tops, sums, out, bias):
    chip = index[0] // 2
    flags = q[4 * BLK :, :NBLK].astype(f32)
    for i in range(3):
        for j in range(3):
            bias[block(i), block(j)] = allowed(
                docs, flags, i, 4 * (chip + 1) + i, 4 * (chip - 1) + 1 + j
            )
    rows = slice(0, 3 * BLK)
    rest = slice(3 * BLK, 4 * BLK)
    lane = lax.broadcasted_iota(jnp.int32, (3 * BLK, HD), 1)
    top_table = jnp.zeros((3 * BLK, HD), f32)
    sum_table = jnp.ones((3 * BLK, HD), f32)
    for h in range(HEADS):
        acc, top, total = attend_head(
            q[rows, cols(h)], tail[rows, cols(h)], tail[3 * BLK :, cols(h)], bias[...]
        )
        top_table = jnp.where(lane == h, top, top_table)
        sum_table = jnp.where(lane == h, total, sum_table)
        top1 = tops[rows, h : h + 1]
        _, _, share = weighed(top1, sums[rows, h : h + 1], top, total)
        here = done[rows, cols(h)]
        out[rows, cols(h)] = (here + (acc / total - here) * share).astype(bf16)
        out[rest, cols(h)] = done[rest, cols(h)].astype(bf16)
    top, total, _ = weighed(tops[rows, :], jnp.where(lane < HEADS, sums[rows, :], 1.0), top_table, sum_table)
    top = jnp.concatenate([top, tops[rest, :]], axis=0)
    total = jnp.concatenate([total, sums[rest, :]], axis=0)
    filler = jnp.zeros((LOCAL, 4 * BLK), f32)
    left = jnp.concatenate([top.T[:HEADS], total.T[:HEADS], filler], axis=0)
    for piece in range(3):
        part = left.astype(bf16)
        at = 4 * BLK + piece * 2 * LOCAL
        out[at : at + 2 * LOCAL, :] = part
        left = left - part.astype(f32)


def merge_body(index, near, tops, sums, far, mine, send, share):
    stats = jnp.zeros((2 * LOCAL, HALF), f32)
    for p in range(3):
        at = 4 * BLK + p * 2 * LOCAL
        stats = stats + far[at : at + 2 * LOCAL, :].astype(f32)
    pad = jnp.ones((HD - HEADS, 4 * BLK), f32)
    far_tops = jnp.concatenate([stats[:HEADS], pad], axis=0).T
    far_sums = jnp.concatenate([stats[HEADS : 2 * HEADS], pad], axis=0).T
    lane = lax.broadcasted_iota(jnp.int32, (4 * BLK, HD), 1)
    near_sums = jnp.where(lane < HEADS, sums[...], 1.0)
    share[...] = weighed(tops[...], near_sums, far_tops, far_sums)[2]
    core = index[0] % 2
    for out, which in ((send, 1 - core), (mine, core)):
        rows = pl.ds(pl.multiple_of(which * ROWS, ROWS), ROWS)
        part = share[rows, :]
        for h in range(HEADS):
            own = near[rows, cols(h)]
            there = far[rows, cols(h)].astype(f32)
            out[:, cols(h)] = (own + (there - own) * part[:, h : h + 1]).astype(bf16)


def place_body(index, mine, other, out):
    core = index[0] % 2
    out[:, half(core)] = mine[...]
    out[:, half(1 - core)] = other[...]


def shifted(x, distance):
    return lax.ppermute(x, "seq", [(i, (i + distance) % SHARDS) for i in range(SHARDS)])


def swapped(x):
    return lax.ppermute(x, "seq", [(i, i ^ 1) for i in range(SHARDS)])


def turned(x, distance):
    return lax.ppermute(x, "head", [(i, (i + distance) % 4) for i in range(4)])


def per_device(
    lin_query,
    lin_key,
    lin_value,
    out_gate,
    norm_gain,
    decay_rate,
    soft_query,
    soft_key,
    soft_value,
    doc_ids,
    block_mask,
):
    like = jax.ShapeDtypeStruct
    index = lax.axis_index("seq").astype(jnp.int32).reshape(1)
    wide = like((ROWS, WIDTH), f32)
    narrow = like((ROWS, WIDTH), bf16)

    anywhere = pl.BlockSpec(memory_space=pl.ANY)
    first, state, sent = call(
        start_body,
        [like((WIDTH, HD), f32), like((WIDTH, HD), bf16), like((3 * ROWS + 16, HALF), bf16)],
        (index, decay_rate, block_mask, lin_key, lin_value, soft_query, soft_key, soft_value),
        [SMEM, anywhere, VMEM] + [anywhere] * 5,
        [
            pltpu.SMEM((LOCAL,), f32),
            pltpu.VMEM((ROWS, WIDTH), bf16),
            pltpu.VMEM((ROWS, WIDTH), bf16),
            pltpu.SemaphoreType.DMA,
            pltpu.SemaphoreType.DMA((LOCAL + 3,)),
        ],
        room=56,
    )
    other = swapped(sent)
    parts = lax.all_to_all(state.reshape(SHARDS, 16, HD), "seq", 0, 0)
    near_q, far_q, own_pair, own_tail, flags = call(
        gather_body,
        [
            like((2 * ROWS, HALF), bf16),
            like((2 * ROWS + 16, HALF), bf16),
            like((8 * BLK, HALF), bf16),
            like((6 * BLK, HALF), bf16),
            like((16, NBLK), f32),
        ],
        (index, block_mask, soft_query, soft_key, soft_value, other),
        [SMEM] + [VMEM] * 5,
        room=56,
    )
    tail = shifted(own_tail, 2)
    next_q = shifted(far_q, -2)

    (prefix,) = call(
        prefix_body,
        [like((SHARDS, 16, HD), bf16)],
        (index, decay_rate, parts),
        [SMEM, SMEM, VMEM],
        flops=PREFIX_COST,
    )
    prefix, doc_ids = lax.optimization_barrier((prefix, doc_ids))
    entering = lax.all_to_all(prefix, "seq", 0, 0).reshape(WIDTH, HD)
    (inner,) = call(
        inner_body,
        [wide],
        (decay_rate, lin_query, lin_key, lin_value),
        [SMEM, VMEM, VMEM, VMEM],
    )
    tables = [like((4 * BLK, HALF), f32), like((4 * BLK, HD), f32), like((4 * BLK, HD), f32)]
    near, tops, sums = call(
        near_body,
        tables,
        (index, doc_ids, flags, near_q, own_pair),
        [SMEM] * 2 + [VMEM] * 3,
        [pltpu.VMEM((4 * BLK, 4 * BLK), f32)],
    )
    done, done_tops, done_sums = call(
        next_body,
        tables,
        (index, doc_ids, next_q, own_pair),
        [SMEM] * 2 + [VMEM] * 2,
        [pltpu.VMEM((4 * BLK, 4 * BLK), f32)],
    )
    (far,) = call(
        far_body,
        [like((4 * BLK + 48, HALF), bf16)],
        (index, doc_ids, next_q, tail, done, done_tops, done_sums),
        [SMEM] * 2 + [VMEM] * 5,
        [pltpu.VMEM((3 * BLK, 3 * BLK), f32)],
    )
    far = shifted(far, 2)
    heads, squares = call(
        carry_body,
        [wide, like((8, ROWS), f32)],
        (decay_rate, inner, lin_query, first, entering),
        [anywhere] * 4 + [VMEM],
        [
            pltpu.SMEM((LOCAL,), f32),
            pltpu.VMEM((ROWS, WIDTH), f32),
            pltpu.VMEM((ROWS, WIDTH), bf16),
            pltpu.VMEM((WIDTH, HD), f32),
            pltpu.SemaphoreType.DMA,
            pltpu.SemaphoreType.DMA((3 * LOCAL // 2,)),
        ],
        flops=CARRY_COST,
        room=56,
    )
    others = [turned(squares, d) for d in (1, 2, 3)]
    far, heads = lax.optimization_barrier((far, heads))
    mine, send = call(
        merge_body,
        [like((ROWS, HALF), bf16)] * 2,
        (index, near, tops, sums, far),
        [SMEM] + [VMEM] * 4,
        [pltpu.VMEM((4 * BLK, HD), f32)],
    )
    send, *others = lax.optimization_barrier((send, *others))
    (lin_output,) = call(
        norm_body,
        [narrow],
        (heads, out_gate, norm_gain.reshape(1, WIDTH), squares, *others),
        [VMEM] * 7,
    )

    (soft_output,) = call(
        place_body, [narrow], (index, mine, swapped(send)), [SMEM, VMEM, VMEM]
    )
    return (lin_output, soft_output)


def solution(mesh):
    rows = P("seq", "head")
    return jax.shard_map(
        per_device,
        mesh=mesh,
        in_specs=(
            rows, rows, rows, rows, P("head"), P("head"), rows, rows, rows, P(), P("seq", None),
        ),
        out_specs=(rows, rows),
        check_vma=False,
    )
```

```python
import math

import jax
import jax.numpy as jnp
from jax import lax
from jax.experimental import pallas as pl
from jax.experimental.pallas import tpu as pltpu
from jax.sharding import PartitionSpec as P

HD = 128
BLK = 128
NBLK = 128
ROWS = 256
LOCAL = 8
WIDTH = LOCAL * HD
HALF = WIDTH // 2
HEADS = LOCAL // 2
D = 4096
SHARDS = 64
FILL = -1e30
PREFIX_COST = 5_000_000_000
CARRY_COST = 10_000_000_000
EXP2_SCALE = HD ** (-0.5) * math.log2(math.e)

f32 = jnp.float32
bf16 = jnp.bfloat16

SMEM = pl.BlockSpec(memory_space=pltpu.SMEM)
VMEM = pl.BlockSpec(memory_space=pltpu.VMEM)


def call(body, outs, ins, specs, scratch=(), flops=1, outs_at=None):
    return pl.pallas_call(
        body,
        out_shape=outs,
        in_specs=specs,
        out_specs=outs_at or [VMEM] * len(outs),
        scratch_shapes=list(scratch),
        compiler_params=pltpu.CompilerParams(vmem_limit_bytes=(16 if body in SMALL else 60) * 1024 * 1024),
        cost_estimate=pl.CostEstimate(flops=flops, bytes_accessed=1, transcendentals=0),
    )(*ins)


def cols(h):
    return slice(h * HD, (h + 1) * HD)


def dot(a, b, dims):
    return lax.dot_general(a, b, (dims, ((), ())), preferred_element_type=f32)


def exact_dot(a, b, dims):
    return lax.dot_general(
        a, b, (dims, ((), ())), precision=lax.Precision.HIGHEST, preferred_element_type=f32
    )


def block_state(rate, k, v, h, b):
    rows = slice(b * BLK, (b + 1) * BLK)
    back = (BLK - 1.0) - lax.broadcasted_iota(jnp.int32, (BLK, HD), 0).astype(f32)
    decayed = (k[rows, cols(h)].astype(f32) * jnp.exp(-rate[h] * back)).astype(bf16)
    return dot(decayed, v[rows, cols(h)], ((0,), (0,)))


def start_body(
    index, rate_hbm, mask, k_hbm, v_hbm, sq, sk, sv, out, sent, rate, k, v, packed, rate_sem, sems
):
    other = 1 - index[0] % 2
    copies = [pltpu.make_async_copy(rate_hbm, rate, rate_sem)]
    for g in range(LOCAL // 2):
        at = slice(g * 2 * HD, (g + 1) * 2 * HD)
        copies.append(pltpu.make_async_copy(k_hbm.at[:, at], k.at[:, at], sems.at[2 * g]))
        copies.append(pltpu.make_async_copy(v_hbm.at[:, at], v.at[:, at], sems.at[2 * g + 1]))
    for at, ref in enumerate((sq, sk, sv)):
        rows = slice(at * ROWS, (at + 1) * ROWS)
        copies.append(
            pltpu.make_async_copy(ref.at[:, half(other)], sent.at[rows, :], sems.at[LOCAL + at])
        )
    for copy in copies:
        copy.start()
    flags = mask[...].astype(f32)
    flags = jnp.concatenate([flags, jnp.zeros((14, NBLK), f32)], axis=0).astype(bf16)
    packed[...] = jnp.concatenate([flags] * 4, axis=1)
    copies.append(pltpu.make_async_copy(packed, sent.at[3 * ROWS :, :], sems.at[LOCAL + 3]))
    copies[-1].start()
    copies[0].wait()
    for g in range(LOCAL // 2):
        copies[2 * g + 1].wait()
        copies[2 * g + 2].wait()
        for h in (2 * g, 2 * g + 1):
            step = jnp.exp(jnp.full((HD, HD), -rate[h] * BLK, f32))
            state = step * block_state(rate, k, v, h, 0) + block_state(rate, k, v, h, 1)
            out[cols(h), :] = state.astype(bf16)
    for copy in copies[LOCAL + 1 :]:
        copy.wait()


def prefix_body(index, rate, parts, out):
    step = jnp.exp(jnp.full((16, HD), -rate[index[0] // 8] * ROWS, f32))
    state = jnp.zeros((16, HD), f32)
    for i in range(SHARDS):
        out[i] = state.astype(bf16)
        if i + 1 < SHARDS:
            state = step * state + parts[i].astype(f32)


def inner_body(rate, q, k, v, out, q_out, first, rates):
    row = lax.broadcasted_iota(jnp.int32, (BLK, BLK), 0)
    col = lax.broadcasted_iota(jnp.int32, (BLK, BLK), 1)
    gap = jnp.maximum(row - col, 0).astype(f32)
    q_out[...] = q[...]
    for h in range(LOCAL):
        rates[h : h + 1, :] = jnp.full((1, HD), rate[h], f32)
        first[cols(h), :] = block_state(rate, k, v, h, 0)
        decay = jnp.where(row >= col, jnp.exp(-rate[h] * gap), 0.0)
        for b in range(2):
            rows = slice(b * BLK, (b + 1) * BLK)
            scores = dot(q[rows, cols(h)], k[rows, cols(h)], ((1,), (1,)))
            out[rows, cols(h)] = dot(
                (scores * decay).astype(bf16), v[rows, cols(h)], ((1,), (0,))
            )


def carry_body(rates, inner, q, first, state, heads, squares):
    ahead = lax.broadcasted_iota(jnp.int32, (BLK, HD), 0).astype(f32) + 1.0
    totals = [jnp.zeros((BLK, HD), f32)] * 2
    for h in range(LOCAL):
        rate = rates[h : h + 1, :]
        decay = jnp.exp(-rate * ahead)
        entering = state[cols(h), :]
        middle = (jnp.exp(-rate * BLK) * entering.astype(f32) + first[cols(h), :]).astype(bf16)
        for b, block_start in enumerate((entering, middle)):
            rows = slice(b * BLK, (b + 1) * BLK)
            carried = dot(q[rows, cols(h)], block_start, ((1,), (0,)))
            value = inner[rows, cols(h)] + carried * decay
            heads[rows, cols(h)] = value
            totals[b] = totals[b] + value * value
    total = jnp.concatenate(totals, axis=0)
    squares[...] = exact_dot(jnp.ones((8, HD), f32), total, ((1,), (1,)))


def norm_body(heads, gate, gain, s0, s1, s2, s3, out):
    total = s0[...] + s1[...] + s2[...] + s3[...]
    first = (lax.broadcasted_iota(jnp.int32, (8, HD), 0) == 0).astype(f32)
    spread = exact_dot(total, first, ((0,), (0,)))
    inverse = lax.rsqrt(spread / D + 1e-06)
    for h in range(LOCAL):
        scale = gain[:, cols(h)] * jax.nn.sigmoid(gate[:, cols(h)].astype(f32))
        out[:, cols(h)] = (heads[:, cols(h)] * inverse * scale).astype(bf16)


def half(c):
    return pl.ds(pl.multiple_of(c * HALF, HALF), HALF)


def gather_body(index, mask, q, k, v, other, far_q, head, tail, theirs, packed, sems):
    core = index[0] % 2

    def put(source, target, at):
        return pltpu.make_async_copy(source, target, sems.at[at])

    def layout(mine):
        def part(at, ref, owner, rows):
            if owner == mine:
                return ref.at[rows, half(core)]
            return other.at[slice(at * ROWS + rows.start, at * ROWS + rows.stop), :]

        low, high, whole = slice(0, BLK), slice(BLK, ROWS), slice(0, ROWS)
        copies = [
            put(part(0, q, 0, whole), far_q.at[:ROWS, :], 0),
            put(part(0, q, 1, whole), far_q.at[ROWS : 2 * ROWS, :], 1),
        ]
        for at, ref in ((1, k), (2, v)):
            base = (at - 1) * 3 * BLK
            sem = 3 * at - 1
            copies += [
                put(part(at, ref, 0, low), head.at[(at - 1) * BLK : at * BLK, :], sem),
                put(part(at, ref, 0, high), tail.at[base : base + BLK, :], sem + 1),
                put(part(at, ref, 1, whole), tail.at[base + BLK : base + 3 * BLK, :], sem + 2),
            ]
        return copies

    for mine in range(2):

        @pl.when(core == mine)
        def _():
            for copy in layout(mine):
                copy.start()

    fetch = put(other.at[3 * ROWS :, :NBLK], theirs, 8)
    fetch.start()
    fetch.wait()
    own = mask[...].astype(f32)
    arrived = theirs[...].astype(f32)[:2]
    first = jnp.where(core == 0, own, arrived)
    second = jnp.where(core == 0, arrived, own)
    rows = jnp.concatenate([first, second, jnp.zeros((12, NBLK), f32)], axis=0)
    packed[...] = jnp.concatenate([rows.astype(bf16)] * 4, axis=1)
    flags = put(packed, far_q.at[4 * BLK :, :], 9)
    flags.start()
    for mine in range(2):

        @pl.when(core == mine)
        def _():
            for copy in layout(mine):
                copy.wait()

    flags.wait()


def allowed(docs, flags, i, query, key):
    q_at = jnp.clip(query, 0, NBLK - 1)
    k_at = jnp.clip(key, 0, NBLK - 1)
    inside = (key >= 0) & (key < query) & (query < NBLK) & (docs[k_at] == docs[q_at])
    lane = lax.broadcasted_iota(jnp.int32, (1, NBLK), 1)
    wanted = jnp.where(inside, k_at, -1)
    ok = jnp.sum(jnp.where(lane == wanted, flags[i : i + 1, :], 0.0), axis=1, keepdims=True)
    return jnp.broadcast_to(jnp.where(ok > 0.5, 0.0, FILL), (BLK, BLK))


def block(i):
    return slice(i * BLK, (i + 1) * BLK)


def attend_head(q, keys, values, bias):
    scores = dot(q, keys, ((1,), (1,))) + bias
    top = jnp.max(scores, axis=1, keepdims=True)
    weights = jnp.exp2((scores - top) * EXP2_SCALE).astype(bf16)
    ones = jnp.ones(values.shape, bf16)
    both = dot(weights, jnp.concatenate([values, ones], axis=1), ((1,), (0,)))
    return both[:, :HD], top, both[:, HD:]


def attend_chip(index, docs, ahead, q, head, tail, out, tops, sums, bias):
    chip = index[0] // 2
    rows = q[4 * BLK :, :NBLK].astype(f32)
    for i in range(4):
        for j in range(4):
            if ahead == 0 and j == i:
                row = lax.broadcasted_iota(jnp.int32, (BLK, BLK), 0)
                col = lax.broadcasted_iota(jnp.int32, (BLK, BLK), 1)
                bias[block(i), block(j)] = jnp.where(col <= row, 0.0, FILL)
            elif ahead == 0 and j > i:
                bias[block(i), block(j)] = jnp.full((BLK, BLK), FILL, f32)
            else:
                bias[block(i), block(j)] = allowed(
                    docs, rows, i, 4 * (chip + ahead) + i, 4 * chip + j
                )
    lane = lax.broadcasted_iota(jnp.int32, (2 * BLK, HD), 1)
    for r in range(2):
        part = slice(r * 2 * BLK, (r + 1) * 2 * BLK)
        count = 4 * BLK if ahead or r else 2 * BLK
        top_table = jnp.zeros((2 * BLK, HD), f32)
        sum_table = jnp.zeros((2 * BLK, HD), f32)
        for h in range(HEADS):
            acc, top, total = attend_head(
                q[part, cols(h)],
                jnp.concatenate([head[:BLK, cols(h)], tail[: count - BLK, cols(h)]], axis=0),
                jnp.concatenate(
                    [head[BLK:, cols(h)], tail[3 * BLK : 2 * BLK + count, cols(h)]], axis=0
                ),
                bias[part, :count],
            )
            out[part, cols(h)] = acc / total
            top_table = jnp.where(lane == h, top, top_table)
            sum_table = jnp.where(lane == h, total, sum_table)
        tops[part, :] = top_table
        sums[part, :] = sum_table


def near_body(index, docs, q, head, tail, out, tops, sums, bias):
    attend_chip(index, docs, 0, q, head, tail, out, tops, sums, bias)


def next_body(index, docs, q, head, tail, out, tops, sums, bias):
    attend_chip(index, docs, 1, q, head, tail, out, tops, sums, bias)


def weighed(top1, sum1, top2, sum2):
    top = jnp.maximum(top1, top2)
    part1 = jnp.exp2((top1 - top) * EXP2_SCALE) * sum1
    part2 = jnp.exp2((top2 - top) * EXP2_SCALE) * sum2
    return top, part1 + part2, part2 / (part1 + part2)


def far_body(index, docs, q, tail, done, tops, sums, out, bias):
    chip = index[0] // 2
    flags = q[4 * BLK :, :NBLK].astype(f32)
    for i in range(3):
        for j in range(3):
            bias[block(i), block(j)] = allowed(
                docs, flags, i, 4 * (chip + 1) + i, 4 * (chip - 1) + 1 + j
            )
    rows = slice(0, 3 * BLK)
    rest = slice(3 * BLK, 4 * BLK)
    lane = lax.broadcasted_iota(jnp.int32, (3 * BLK, HD), 1)
    top_table = jnp.zeros((3 * BLK, HD), f32)
    sum_table = jnp.ones((3 * BLK, HD), f32)
    for h in range(HEADS):
        acc, top, total = attend_head(
            q[rows, cols(h)], tail[rows, cols(h)], tail[3 * BLK :, cols(h)], bias[...]
        )
        top_table = jnp.where(lane == h, top, top_table)
        sum_table = jnp.where(lane == h, total, sum_table)
        top1 = tops[rows, h : h + 1]
        _, _, share = weighed(top1, sums[rows, h : h + 1], top, total)
        here = done[rows, cols(h)]
        out[rows, cols(h)] = (here + (acc / total - here) * share).astype(bf16)
        out[rest, cols(h)] = done[rest, cols(h)].astype(bf16)
    top, total, _ = weighed(tops[rows, :], jnp.where(lane < HEADS, sums[rows, :], 1.0), top_table, sum_table)
    top = jnp.concatenate([top, tops[rest, :]], axis=0)
    total = jnp.concatenate([total, sums[rest, :]], axis=0)
    filler = jnp.zeros((LOCAL, 4 * BLK), f32)
    left = jnp.concatenate([top.T[:HEADS], total.T[:HEADS], filler], axis=0)
    for piece in range(3):
        part = left.astype(bf16)
        at = 4 * BLK + piece * 2 * LOCAL
        out[at : at + 2 * LOCAL, :] = part
        left = left - part.astype(f32)


def merge_body(index, near, tops, sums, far, mine, send, share):
    stats = jnp.zeros((2 * LOCAL, HALF), f32)
    for p in range(3):
        at = 4 * BLK + p * 2 * LOCAL
        stats = stats + far[at : at + 2 * LOCAL, :].astype(f32)
    pad = jnp.ones((HD - HEADS, 4 * BLK), f32)
    far_sums = jnp.concatenate([stats[HEADS : 2 * HEADS], pad], axis=0).T
    far_tops = jnp.concatenate([stats[:HEADS], pad], axis=0).T
    far_tops = jnp.where(far_sums > 0.0, far_tops, FILL)
    far_sums = jnp.where(far_sums > 0.0, far_sums, 1.0)
    lane = lax.broadcasted_iota(jnp.int32, (4 * BLK, HD), 1)
    near_sums = jnp.where(lane < HEADS, sums[...], 1.0)
    share[...] = weighed(tops[...], near_sums, far_tops, far_sums)[2]
    core = index[0] % 2
    for out, which in ((send, 1 - core), (mine, core)):
        rows = pl.ds(pl.multiple_of(which * ROWS, ROWS), ROWS)
        part = share[rows, :]
        for h in range(HEADS):
            own = near[rows, cols(h)]
            there = far[rows, cols(h)].astype(f32)
            out[:, cols(h)] = (own + (there - own) * part[:, h : h + 1]).astype(bf16)


def place_body(index, mine, other, out):
    core = index[0] % 2
    out[:, half(core)] = mine[...]
    out[:, half(1 - core)] = other[...]


SMALL = (prefix_body, next_body, far_body, merge_body, norm_body, place_body)


def shifted(x, distance):
    return lax.ppermute(x, "seq", [(i, i + distance) for i in range(SHARDS) if 0 <= i + distance < SHARDS])


def swapped(x):
    return lax.ppermute(x, "seq", [(i, i ^ 1) for i in range(SHARDS)])


def turned(x, distance):
    return lax.ppermute(x, "head", [(i, (i + distance) % 4) for i in range(4)])


def per_device(
    lin_query,
    lin_key,
    lin_value,
    out_gate,
    norm_gain,
    decay_rate,
    soft_query,
    soft_key,
    soft_value,
    doc_ids,
    block_mask,
):
    like = jax.ShapeDtypeStruct
    index = lax.axis_index("seq").astype(jnp.int32).reshape(1)
    wide = like((ROWS, WIDTH), f32)
    narrow = like((ROWS, WIDTH), bf16)

    anywhere = pl.BlockSpec(memory_space=pl.ANY)
    state, sent = call(
        start_body,
        [like((WIDTH, HD), bf16), like((3 * ROWS + 16, HALF), bf16)],
        (index, decay_rate, block_mask, lin_key, lin_value, soft_query, soft_key, soft_value),
        [SMEM, anywhere, VMEM] + [anywhere] * 5,
        [
            pltpu.SMEM((LOCAL,), f32),
            pltpu.VMEM((ROWS, WIDTH), bf16),
            pltpu.VMEM((ROWS, WIDTH), bf16),
            pltpu.VMEM((16, HALF), bf16),
            pltpu.SemaphoreType.DMA,
            pltpu.SemaphoreType.DMA((LOCAL + 4,)),
        ],
        outs_at=[VMEM, anywhere],
    )
    other = swapped(sent)
    parts = lax.all_to_all(state.reshape(SHARDS, 16, HD), "seq", 0, 0)
    far_q, own_head, own_tail = call(
        gather_body,
        [
            like((2 * ROWS + 16, HALF), bf16),
            like((2 * BLK, HALF), bf16),
            like((6 * BLK, HALF), bf16),
        ],
        (index, block_mask, soft_query, soft_key, soft_value, other),
        [SMEM, VMEM] + [anywhere] * 4,
        [
            pltpu.VMEM((16, NBLK), bf16),
            pltpu.VMEM((16, HALF), bf16),
            pltpu.SemaphoreType.DMA((10,)),
        ],
        outs_at=[anywhere] * 3,
    )
    tail = shifted(own_tail, 2)
    next_q = shifted(far_q, -2)

    tables = [like((4 * BLK, HALF), f32), like((4 * BLK, HD), f32), like((4 * BLK, HD), f32)]
    near, tops, sums = call(
        near_body,
        tables,
        (index, doc_ids, far_q, own_head, own_tail),
        [SMEM] * 2 + [VMEM] * 3,
        [pltpu.VMEM((4 * BLK, 4 * BLK), f32)],
    )
    near, parts = lax.optimization_barrier((near, parts))
    (prefix,) = call(
        prefix_body,
        [like((SHARDS, 16, HD), bf16)],
        (index, decay_rate, parts),
        [SMEM, SMEM, VMEM],
        flops=PREFIX_COST,
    )
    prefix, doc_ids = lax.optimization_barrier((prefix, doc_ids))
    entering = lax.all_to_all(prefix, "seq", 0, 0).reshape(WIDTH, HD)
    inner, q_held, first, rates = call(
        inner_body,
        [wide, narrow, like((WIDTH, HD), f32), like((LOCAL, HD), f32)],
        (decay_rate, lin_query, lin_key, lin_value),
        [SMEM, VMEM, VMEM, VMEM],
    )
    done, done_tops, done_sums = call(
        next_body,
        tables,
        (index, doc_ids, next_q, own_head, own_tail),
        [SMEM] * 2 + [VMEM] * 3,
        [pltpu.VMEM((4 * BLK, 4 * BLK), f32)],
    )
    (far,) = call(
        far_body,
        [like((4 * BLK + 48, HALF), bf16)],
        (index, doc_ids, next_q, tail, done, done_tops, done_sums),
        [SMEM] * 2 + [VMEM] * 5,
        [pltpu.VMEM((3 * BLK, 3 * BLK), f32)],
    )
    far = shifted(far, 2)
    heads, squares = call(
        carry_body,
        [wide, like((8, ROWS), f32)],
        (rates, inner, q_held, first, entering),
        [VMEM] * 5,
        flops=CARRY_COST,
    )
    others = [turned(squares, d) for d in (1, 2, 3)]
    far, heads = lax.optimization_barrier((far, heads))
    mine, send = call(
        merge_body,
        [like((ROWS, HALF), bf16)] * 2,
        (index, near, tops, sums, far),
        [SMEM] + [VMEM] * 4,
        [pltpu.VMEM((4 * BLK, HD), f32)],
    )
    send, *others = lax.optimization_barrier((send, *others))
    (lin_output,) = call(
        norm_body,
        [narrow],
        (heads, out_gate, norm_gain.reshape(1, WIDTH), squares, *others),
        [VMEM] * 7,
    )

    (soft_output,) = call(
        place_body, [narrow], (index, mine, swapped(send)), [SMEM, VMEM, VMEM]
    )
    return (lin_output, soft_output)


def solution(mesh):
    rows = P("seq", "head")
    return jax.shard_map(
        per_device,
        mesh=mesh,
        in_specs=(
            rows, rows, rows, rows, P("head"), P("head"), rows, rows, rows, P(), P("seq", None),
        ),
        out_specs=(rows, rows),
        check_vma=False,
    )
```

```python
import math

import jax
import jax.numpy as jnp
from jax import lax
from jax.experimental import pallas as pl
from jax.experimental.pallas import tpu as pltpu
from jax.sharding import PartitionSpec as P

HD = 128
BLK = 128
NBLK = 128
ROWS = 256
LOCAL = 8
WIDTH = LOCAL * HD
HALF = WIDTH // 2
HEADS = LOCAL // 2
D = 4096
SHARDS = 64
FILL = -1e30
PREFIX_COST = 5_000_000_000
CARRY_COST = 10_000_000_000
EXP2_SCALE = HD ** (-0.5) * math.log2(math.e)

f32 = jnp.float32
bf16 = jnp.bfloat16

SMEM = pl.BlockSpec(memory_space=pltpu.SMEM)
VMEM = pl.BlockSpec(memory_space=pltpu.VMEM)


def call(body, outs, ins, specs, scratch=(), flops=1, outs_at=None):
    return pl.pallas_call(
        body,
        out_shape=outs,
        in_specs=specs,
        out_specs=outs_at or [VMEM] * len(outs),
        scratch_shapes=list(scratch),
        compiler_params=pltpu.CompilerParams(vmem_limit_bytes=(16 if body in SMALL else 60) * 1024 * 1024),
        cost_estimate=pl.CostEstimate(flops=flops, bytes_accessed=1, transcendentals=0),
    )(*ins)


def cols(h):
    return slice(h * HD, (h + 1) * HD)


def dot(a, b, dims):
    return lax.dot_general(a, b, (dims, ((), ())), preferred_element_type=f32)


def exact_dot(a, b, dims):
    return lax.dot_general(
        a, b, (dims, ((), ())), precision=lax.Precision.HIGHEST, preferred_element_type=f32
    )


def block_state(rate, k, v, h, b):
    rows = slice(b * BLK, (b + 1) * BLK)
    back = (BLK - 1.0) - lax.broadcasted_iota(jnp.int32, (BLK, HD), 0).astype(f32)
    decayed = (k[rows, cols(h)].astype(f32) * jnp.exp(-rate[h] * back)).astype(bf16)
    return dot(decayed, v[rows, cols(h)], ((0,), (0,)))


def start_body(
    index, rate_hbm, mask, k_hbm, v_hbm, sq, sk, sv, out, sent, rate, k, v, packed, rate_sem, sems
):
    other = 1 - index[0] % 2
    copies = [pltpu.make_async_copy(rate_hbm, rate, rate_sem)]
    for g in range(LOCAL // 2):
        at = slice(g * 2 * HD, (g + 1) * 2 * HD)
        copies.append(pltpu.make_async_copy(k_hbm.at[:, at], k.at[:, at], sems.at[2 * g]))
        copies.append(pltpu.make_async_copy(v_hbm.at[:, at], v.at[:, at], sems.at[2 * g + 1]))
    for at, ref in enumerate((sq, sk, sv)):
        rows = slice(at * ROWS, (at + 1) * ROWS)
        copies.append(
            pltpu.make_async_copy(ref.at[:, half(other)], sent.at[rows, :], sems.at[LOCAL + at])
        )
    for copy in copies:
        copy.start()
    flags = mask[...].astype(f32)
    flags = jnp.concatenate([flags, jnp.zeros((14, NBLK), f32)], axis=0).astype(bf16)
    packed[...] = jnp.concatenate([flags] * 4, axis=1)
    copies.append(pltpu.make_async_copy(packed, sent.at[3 * ROWS :, :], sems.at[LOCAL + 3]))
    copies[-1].start()
    copies[0].wait()
    for g in range(LOCAL // 2):
        copies[2 * g + 1].wait()
        copies[2 * g + 2].wait()
        for h in (2 * g, 2 * g + 1):
            step = jnp.exp(jnp.full((HD, HD), -rate[h] * BLK, f32))
            state = step * block_state(rate, k, v, h, 0) + block_state(rate, k, v, h, 1)
            out[cols(h), :] = state.astype(bf16)
    for copy in copies[LOCAL + 1 :]:
        copy.wait()


def prefix_body(index, rate, parts, out):
    step = jnp.exp(jnp.full((16, HD), -rate[index[0] // 8] * ROWS, f32))
    state = jnp.zeros((16, HD), f32)
    for i in range(SHARDS):
        out[i] = state.astype(bf16)
        if i + 1 < SHARDS:
            state = step * state + parts[i].astype(f32)


def inner_body(rate, q, k, v, out, q_out, first, rates):
    row = lax.broadcasted_iota(jnp.int32, (BLK, BLK), 0)
    col = lax.broadcasted_iota(jnp.int32, (BLK, BLK), 1)
    gap = jnp.maximum(row - col, 0).astype(f32)
    q_out[...] = q[...]
    for h in range(LOCAL):
        rates[h : h + 1, :] = jnp.full((1, HD), rate[h], f32)
        first[cols(h), :] = block_state(rate, k, v, h, 0)
        decay = jnp.where(row >= col, jnp.exp(-rate[h] * gap), 0.0)
        for b in range(2):
            rows = slice(b * BLK, (b + 1) * BLK)
            scores = dot(q[rows, cols(h)], k[rows, cols(h)], ((1,), (1,)))
            out[rows, cols(h)] = dot(
                (scores * decay).astype(bf16), v[rows, cols(h)], ((1,), (0,))
            )


def carry_body(rates, inner, q, first, state, heads, squares):
    ahead = lax.broadcasted_iota(jnp.int32, (BLK, HD), 0).astype(f32) + 1.0
    totals = [jnp.zeros((BLK, HD), f32)] * 2
    for h in range(LOCAL):
        rate = rates[h : h + 1, :]
        decay = jnp.exp(-rate * ahead)
        entering = state[cols(h), :]
        middle = (jnp.exp(-rate * BLK) * entering.astype(f32) + first[cols(h), :]).astype(bf16)
        for b, block_start in enumerate((entering, middle)):
            rows = slice(b * BLK, (b + 1) * BLK)
            carried = dot(q[rows, cols(h)], block_start, ((1,), (0,)))
            value = inner[rows, cols(h)] + carried * decay
            heads[rows, cols(h)] = value
            totals[b] = totals[b] + value * value
    total = jnp.concatenate(totals, axis=0)
    squares[...] = exact_dot(jnp.ones((8, HD), f32), total, ((1,), (1,)))


def norm_body(heads, gate, gain, s0, s1, s2, s3, out):
    total = s0[...] + s1[...] + s2[...] + s3[...]
    first = (lax.broadcasted_iota(jnp.int32, (8, HD), 0) == 0).astype(f32)
    spread = exact_dot(total, first, ((0,), (0,)))
    inverse = lax.rsqrt(spread / D + 1e-06)
    for h in range(LOCAL):
        scale = gain[:, cols(h)] * jax.nn.sigmoid(gate[:, cols(h)].astype(f32))
        out[:, cols(h)] = (heads[:, cols(h)] * inverse * scale).astype(bf16)


def half(c):
    return pl.ds(pl.multiple_of(c * HALF, HALF), HALF)


def gather_body(index, mask, q, k, v, other, far_q, head, tail, theirs, packed, sems):
    core = index[0] % 2

    def put(source, target, at):
        return pltpu.make_async_copy(source, target, sems.at[at])

    def layout(mine):
        def part(at, ref, owner, rows):
            if owner == mine:
                return ref.at[rows, half(core)]
            return other.at[slice(at * ROWS + rows.start, at * ROWS + rows.stop), :]

        low, high, whole = slice(0, BLK), slice(BLK, ROWS), slice(0, ROWS)
        copies = [
            put(part(0, q, 0, whole), far_q.at[:ROWS, :], 0),
            put(part(0, q, 1, whole), far_q.at[ROWS : 2 * ROWS, :], 1),
        ]
        for at, ref in ((1, k), (2, v)):
            base = (at - 1) * 3 * BLK
            sem = 3 * at - 1
            copies += [
                put(part(at, ref, 0, low), head.at[(at - 1) * BLK : at * BLK, :], sem),
                put(part(at, ref, 0, high), tail.at[base : base + BLK, :], sem + 1),
                put(part(at, ref, 1, whole), tail.at[base + BLK : base + 3 * BLK, :], sem + 2),
            ]
        return copies

    for mine in range(2):

        @pl.when(core == mine)
        def _():
            for copy in layout(mine):
                copy.start()

    fetch = put(other.at[3 * ROWS :, :NBLK], theirs, 8)
    fetch.start()
    fetch.wait()
    own = mask[...].astype(f32)
    arrived = theirs[...].astype(f32)[:2]
    first = jnp.where(core == 0, own, arrived)
    second = jnp.where(core == 0, arrived, own)
    rows = jnp.concatenate([first, second, jnp.zeros((12, NBLK), f32)], axis=0)
    packed[...] = jnp.concatenate([rows.astype(bf16)] * 4, axis=1)
    flags = put(packed, far_q.at[4 * BLK :, :], 9)
    flags.start()
    for mine in range(2):

        @pl.when(core == mine)
        def _():
            for copy in layout(mine):
                copy.wait()

    flags.wait()


def allowed(docs, flags, i, query, key):
    q_at = jnp.clip(query, 0, NBLK - 1)
    k_at = jnp.clip(key, 0, NBLK - 1)
    inside = (key >= 0) & (key < query) & (query < NBLK) & (docs[k_at] == docs[q_at])
    lane = lax.broadcasted_iota(jnp.int32, (1, NBLK), 1)
    wanted = jnp.where(inside, k_at, -1)
    ok = jnp.sum(jnp.where(lane == wanted, flags[i : i + 1, :], 0.0), axis=1, keepdims=True)
    return jnp.broadcast_to(jnp.where(ok > 0.5, 0.0, FILL), (BLK, BLK))


def block(i):
    return slice(i * BLK, (i + 1) * BLK)


def attend_head(q, keys, values, bias):
    scores = dot(q, keys, ((1,), (1,))) + bias
    top = jnp.max(scores, axis=1, keepdims=True)
    weights = jnp.exp2((scores - top) * EXP2_SCALE).astype(bf16)
    ones = jnp.ones(values.shape, bf16)
    both = dot(weights, jnp.concatenate([values, ones], axis=1), ((1,), (0,)))
    return both[:, :HD], top, both[:, HD:]


def attend_chip(index, docs, ahead, q, head, tail, out, tops, sums, bias):
    chip = index[0] // 2
    rows = q[4 * BLK :, :NBLK].astype(f32)
    for i in range(4):
        for j in range(4):
            if ahead == 0 and j == i:
                row = lax.broadcasted_iota(jnp.int32, (BLK, BLK), 0)
                col = lax.broadcasted_iota(jnp.int32, (BLK, BLK), 1)
                bias[block(i), block(j)] = jnp.where(col <= row, 0.0, FILL)
            elif ahead == 0 and j > i:
                bias[block(i), block(j)] = jnp.full((BLK, BLK), FILL, f32)
            else:
                bias[block(i), block(j)] = allowed(
                    docs, rows, i, 4 * (chip + ahead) + i, 4 * chip + j
                )
    lane = lax.broadcasted_iota(jnp.int32, (2 * BLK, HD), 1)
    for r in range(2):
        part = slice(r * 2 * BLK, (r + 1) * 2 * BLK)
        count = 4 * BLK if ahead or r else 2 * BLK
        top_table = jnp.zeros((2 * BLK, HD), f32)
        sum_table = jnp.zeros((2 * BLK, HD), f32)
        for h in range(HEADS):
            acc, top, total = attend_head(
                q[part, cols(h)],
                jnp.concatenate([head[:BLK, cols(h)], tail[: count - BLK, cols(h)]], axis=0),
                jnp.concatenate(
                    [head[BLK:, cols(h)], tail[3 * BLK : 2 * BLK + count, cols(h)]], axis=0
                ),
                bias[part, :count],
            )
            out[part, cols(h)] = acc / total
            top_table = jnp.where(lane == h, top, top_table)
            sum_table = jnp.where(lane == h, total, sum_table)
        tops[part, :] = top_table
        sums[part, :] = sum_table


def near_body(index, docs, q, head, tail, out, tops, sums, bias):
    attend_chip(index, docs, 0, q, head, tail, out, tops, sums, bias)


def next_body(index, docs, q, head, tail, out, tops, sums, bias):
    attend_chip(index, docs, 1, q, head, tail, out, tops, sums, bias)


def weighed(top1, sum1, top2, sum2):
    top = jnp.maximum(top1, top2)
    part1 = jnp.exp2((top1 - top) * EXP2_SCALE) * sum1
    part2 = jnp.exp2((top2 - top) * EXP2_SCALE) * sum2
    return top, part1 + part2, part2 / (part1 + part2)


def far_body(index, docs, q, tail, done, tops, sums, out, bias):
    chip = index[0] // 2
    flags = q[4 * BLK :, :NBLK].astype(f32)
    for i in range(3):
        for j in range(3):
            bias[block(i), block(j)] = allowed(
                docs, flags, i, 4 * (chip + 1) + i, 4 * (chip - 1) + 1 + j
            )
    rows = slice(0, 3 * BLK)
    rest = slice(3 * BLK, 4 * BLK)
    lane = lax.broadcasted_iota(jnp.int32, (3 * BLK, HD), 1)
    top_table = jnp.zeros((3 * BLK, HD), f32)
    sum_table = jnp.ones((3 * BLK, HD), f32)
    for h in range(HEADS):
        acc, top, total = attend_head(
            q[rows, cols(h)], tail[rows, cols(h)], tail[3 * BLK :, cols(h)], bias[...]
        )
        top_table = jnp.where(lane == h, top, top_table)
        sum_table = jnp.where(lane == h, total, sum_table)
        top1 = tops[rows, h : h + 1]
        _, _, share = weighed(top1, sums[rows, h : h + 1], top, total)
        here = done[rows, cols(h)]
        out[rows, cols(h)] = (here + (acc / total - here) * share).astype(bf16)
        out[rest, cols(h)] = done[rest, cols(h)].astype(bf16)
    top, total, _ = weighed(tops[rows, :], jnp.where(lane < HEADS, sums[rows, :], 1.0), top_table, sum_table)
    top = jnp.concatenate([top, tops[rest, :]], axis=0)
    total = jnp.concatenate([total, sums[rest, :]], axis=0)
    filler = jnp.zeros((LOCAL, 4 * BLK), f32)
    left = jnp.concatenate([top.T[:HEADS], total.T[:HEADS], filler], axis=0)
    for piece in range(3):
        part = left.astype(bf16)
        at = 4 * BLK + piece * 2 * LOCAL
        out[at : at + 2 * LOCAL, :] = part
        left = left - part.astype(f32)


def merge_body(index, near, tops, sums, far, mine, send, share):
    stats = jnp.zeros((2 * LOCAL, HALF), f32)
    for p in range(3):
        at = 4 * BLK + p * 2 * LOCAL
        stats = stats + far[at : at + 2 * LOCAL, :].astype(f32)
    pad = jnp.ones((HD - HEADS, 4 * BLK), f32)
    far_sums = jnp.concatenate([stats[HEADS : 2 * HEADS], pad], axis=0).T
    far_tops = jnp.concatenate([stats[:HEADS], pad], axis=0).T
    far_tops = jnp.where(far_sums > 0.0, far_tops, FILL)
    far_sums = jnp.where(far_sums > 0.0, far_sums, 1.0)
    lane = lax.broadcasted_iota(jnp.int32, (4 * BLK, HD), 1)
    near_sums = jnp.where(lane < HEADS, sums[...], 1.0)
    share[...] = weighed(tops[...], near_sums, far_tops, far_sums)[2]
    core = index[0] % 2
    for out, which in ((send, 1 - core), (mine, core)):
        rows = pl.ds(pl.multiple_of(which * ROWS, ROWS), ROWS)
        part = share[rows, :]
        for h in range(HEADS):
            own = near[rows, cols(h)]
            there = far[rows, cols(h)].astype(f32)
            out[:, cols(h)] = (own + (there - own) * part[:, h : h + 1]).astype(bf16)


def place_body(index, mine, other, out):
    core = index[0] % 2
    out[:, half(core)] = mine[...]
    out[:, half(1 - core)] = other[...]


SMALL = (gather_body, near_body, prefix_body, next_body, far_body, merge_body, norm_body, place_body)


def shifted(x, distance):
    return lax.ppermute(x, "seq", [(i, i + distance) for i in range(SHARDS) if 0 <= i + distance < SHARDS])


def swapped(x):
    return lax.ppermute(x, "seq", [(i, i ^ 1) for i in range(SHARDS)])


def turned(x, distance):
    return lax.ppermute(x, "head", [(i, (i + distance) % 4) for i in range(4)])


def per_device(
    lin_query,
    lin_key,
    lin_value,
    out_gate,
    norm_gain,
    decay_rate,
    soft_query,
    soft_key,
    soft_value,
    doc_ids,
    block_mask,
):
    like = jax.ShapeDtypeStruct
    index = lax.axis_index("seq").astype(jnp.int32).reshape(1)
    wide = like((ROWS, WIDTH), f32)
    narrow = like((ROWS, WIDTH), bf16)

    anywhere = pl.BlockSpec(memory_space=pl.ANY)
    state, sent = call(
        start_body,
        [like((WIDTH, HD), bf16), like((3 * ROWS + 16, HALF), bf16)],
        (index, decay_rate, block_mask, lin_key, lin_value, soft_query, soft_key, soft_value),
        [SMEM, anywhere, VMEM] + [anywhere] * 5,
        [
            pltpu.SMEM((LOCAL,), f32),
            pltpu.VMEM((ROWS, WIDTH), bf16),
            pltpu.VMEM((ROWS, WIDTH), bf16),
            pltpu.VMEM((16, HALF), bf16),
            pltpu.SemaphoreType.DMA,
            pltpu.SemaphoreType.DMA((LOCAL + 4,)),
        ],
    )
    other = swapped(sent)
    parts = lax.all_to_all(state.reshape(SHARDS, 16, HD), "seq", 0, 0)
    far_q, own_head, own_tail = call(
        gather_body,
        [
            like((2 * ROWS + 16, HALF), bf16),
            like((2 * BLK, HALF), bf16),
            like((6 * BLK, HALF), bf16),
        ],
        (index, block_mask, soft_query, soft_key, soft_value, other),
        [SMEM, VMEM] + [anywhere] * 4,
        [
            pltpu.VMEM((16, NBLK), bf16),
            pltpu.VMEM((16, HALF), bf16),
            pltpu.SemaphoreType.DMA((10,)),
        ],
    )
    tail = shifted(own_tail, 2)
    next_q = shifted(far_q, -2)

    tables = [like((4 * BLK, HALF), f32), like((4 * BLK, HD), f32), like((4 * BLK, HD), f32)]
    near, tops, sums = call(
        near_body,
        tables,
        (index, doc_ids, far_q, own_head, own_tail),
        [SMEM] * 2 + [VMEM] * 3,
        [pltpu.VMEM((4 * BLK, 4 * BLK), f32)],
    )
    near, parts = lax.optimization_barrier((near, parts))
    (prefix,) = call(
        prefix_body,
        [like((SHARDS, 16, HD), bf16)],
        (index, decay_rate, parts),
        [SMEM, SMEM, VMEM],
        flops=PREFIX_COST,
    )
    prefix, doc_ids = lax.optimization_barrier((prefix, doc_ids))
    entering = lax.all_to_all(prefix, "seq", 0, 0).reshape(WIDTH, HD)
    inner, q_held, first, rates = call(
        inner_body,
        [wide, narrow, like((WIDTH, HD), f32), like((LOCAL, HD), f32)],
        (decay_rate, lin_query, lin_key, lin_value),
        [SMEM, VMEM, VMEM, VMEM],
    )
    done, done_tops, done_sums = call(
        next_body,
        tables,
        (index, doc_ids, next_q, own_head, own_tail),
        [SMEM] * 2 + [VMEM] * 3,
        [pltpu.VMEM((4 * BLK, 4 * BLK), f32)],
    )
    (far,) = call(
        far_body,
        [like((4 * BLK + 48, HALF), bf16)],
        (index, doc_ids, next_q, tail, done, done_tops, done_sums),
        [SMEM] * 2 + [VMEM] * 5,
        [pltpu.VMEM((3 * BLK, 3 * BLK), f32)],
    )
    far = shifted(far, 2)
    heads, squares = call(
        carry_body,
        [wide, like((8, ROWS), f32)],
        (rates, inner, q_held, first, entering),
        [VMEM] * 5,
        flops=CARRY_COST,
    )
    others = [turned(squares, d) for d in (1, 2, 3)]
    far, heads = lax.optimization_barrier((far, heads))
    mine, send = call(
        merge_body,
        [like((ROWS, HALF), bf16)] * 2,
        (index, near, tops, sums, far),
        [SMEM] + [VMEM] * 4,
        [pltpu.VMEM((4 * BLK, HD), f32)],
    )
    send, *others = lax.optimization_barrier((send, *others))
    (lin_output,) = call(
        norm_body,
        [narrow],
        (heads, out_gate, norm_gain.reshape(1, WIDTH), squares, *others),
        [VMEM] * 7,
    )

    (soft_output,) = call(
        place_body, [narrow], (index, mine, swapped(send)), [SMEM, VMEM, VMEM]
    )
    return (lin_output, soft_output)


def solution(mesh):
    rows = P("seq", "head")
    return jax.shard_map(
        per_device,
        mesh=mesh,
        in_specs=(
            rows, rows, rows, rows, P("head"), P("head"), rows, rows, rows, P(), P("seq", None),
        ),
        out_specs=(rows, rows),
        check_vma=False,
    )
```

```python
import math

import jax
import jax.numpy as jnp
from jax import lax
from jax.experimental import pallas as pl
from jax.experimental.pallas import tpu as pltpu
from jax.sharding import PartitionSpec as P

HD = 128
BLK = 128
NBLK = 128
ROWS = 256
LOCAL = 8
WIDTH = LOCAL * HD
HALF = WIDTH // 2
HEADS = LOCAL // 2
D = 4096
SHARDS = 64
FILL = -1e30
PREFIX_COST = 5_000_000_000
CARRY_COST = 10_000_000_000
EXP2_SCALE = HD ** (-0.5) * math.log2(math.e)

f32 = jnp.float32
bf16 = jnp.bfloat16

SMEM = pl.BlockSpec(memory_space=pltpu.SMEM)
VMEM = pl.BlockSpec(memory_space=pltpu.VMEM)


def call(body, outs, ins, specs, scratch=(), flops=1, outs_at=None):
    return pl.pallas_call(
        body,
        out_shape=outs,
        in_specs=specs,
        out_specs=outs_at or [VMEM] * len(outs),
        scratch_shapes=list(scratch),
        compiler_params=pltpu.CompilerParams(vmem_limit_bytes=(16 if body in SMALL else 60) * 1024 * 1024),
        cost_estimate=pl.CostEstimate(flops=flops, bytes_accessed=1, transcendentals=0),
    )(*ins)


def cols(h):
    return slice(h * HD, (h + 1) * HD)


def dot(a, b, dims):
    return lax.dot_general(a, b, (dims, ((), ())), preferred_element_type=f32)


def exact_dot(a, b, dims):
    return lax.dot_general(
        a, b, (dims, ((), ())), precision=lax.Precision.HIGHEST, preferred_element_type=f32
    )


def block_state(rate, k, v, h, b):
    rows = slice(b * BLK, (b + 1) * BLK)
    back = (BLK - 1.0) - lax.broadcasted_iota(jnp.int32, (BLK, HD), 0).astype(f32)
    decayed = (k[rows, cols(h)].astype(f32) * jnp.exp(-rate[h] * back)).astype(bf16)
    return dot(decayed, v[rows, cols(h)], ((0,), (0,)))


def start_body(
    index, rate_hbm, mask, k_hbm, v_hbm, sq, sk, sv, out, sent, rate, k, v, packed, rate_sem, sems
):
    other = 1 - index[0] % 2
    copies = [pltpu.make_async_copy(rate_hbm, rate, rate_sem)]
    for g in range(LOCAL // 2):
        at = slice(g * 2 * HD, (g + 1) * 2 * HD)
        copies.append(pltpu.make_async_copy(k_hbm.at[:, at], k.at[:, at], sems.at[2 * g]))
        copies.append(pltpu.make_async_copy(v_hbm.at[:, at], v.at[:, at], sems.at[2 * g + 1]))
    for at, ref in enumerate((sq, sk, sv)):
        rows = slice(at * ROWS, (at + 1) * ROWS)
        copies.append(
            pltpu.make_async_copy(ref.at[:, half(other)], sent.at[rows, :], sems.at[LOCAL + at])
        )
    for copy in copies:
        copy.start()
    flags = mask[...].astype(f32)
    flags = jnp.concatenate([flags, jnp.zeros((14, NBLK), f32)], axis=0).astype(bf16)
    packed[...] = jnp.concatenate([flags] * 4, axis=1)
    copies.append(pltpu.make_async_copy(packed, sent.at[3 * ROWS :, :], sems.at[LOCAL + 3]))
    copies[-1].start()
    copies[0].wait()
    for g in range(LOCAL // 2):
        copies[2 * g + 1].wait()
        copies[2 * g + 2].wait()
        for h in (2 * g, 2 * g + 1):
            step = jnp.exp(jnp.full((HD, HD), -rate[h] * BLK, f32))
            state = step * block_state(rate, k, v, h, 0) + block_state(rate, k, v, h, 1)
            out[cols(h), :] = state.astype(bf16)
    for copy in copies[LOCAL + 1 :]:
        copy.wait()


def prefix_body(index, rate, parts, out):
    step = jnp.exp(jnp.full((16, HD), -rate[index[0] // 8] * ROWS, f32))
    state = jnp.zeros((16, HD), f32)
    for i in range(SHARDS):
        out[i] = state.astype(bf16)
        if i + 1 < SHARDS:
            state = step * state + parts[i].astype(f32)


def inner_body(rate, q, k, v, out, first, rates):
    row = lax.broadcasted_iota(jnp.int32, (BLK, BLK), 0)
    col = lax.broadcasted_iota(jnp.int32, (BLK, BLK), 1)
    gap = jnp.maximum(row - col, 0).astype(f32)
    for h in range(LOCAL):
        rates[h : h + 1, :] = jnp.full((1, HD), rate[h], f32)
        first[cols(h), :] = block_state(rate, k, v, h, 0)
        decay = jnp.where(row >= col, jnp.exp(-rate[h] * gap), 0.0)
        for b in range(2):
            rows = slice(b * BLK, (b + 1) * BLK)
            scores = dot(q[rows, cols(h)], k[rows, cols(h)], ((1,), (1,)))
            out[rows, cols(h)] = dot(
                (scores * decay).astype(bf16), v[rows, cols(h)], ((1,), (0,))
            )


def carry_body(rates, inner, q, first, state, heads, squares):
    ahead = lax.broadcasted_iota(jnp.int32, (BLK, HD), 0).astype(f32) + 1.0
    totals = [jnp.zeros((BLK, HD), f32)] * 2
    for h in range(LOCAL):
        rate = rates[h : h + 1, :]
        decay = jnp.exp(-rate * ahead)
        entering = state[cols(h), :]
        middle = (jnp.exp(-rate * BLK) * entering.astype(f32) + first[cols(h), :]).astype(bf16)
        for b, block_start in enumerate((entering, middle)):
            rows = slice(b * BLK, (b + 1) * BLK)
            carried = dot(q[rows, cols(h)], block_start, ((1,), (0,)))
            value = inner[rows, cols(h)] + carried * decay
            heads[rows, cols(h)] = value
            totals[b] = totals[b] + value * value
    total = jnp.concatenate(totals, axis=0)
    squares[...] = exact_dot(jnp.ones((8, HD), f32), total, ((1,), (1,)))


def norm_body(heads, gate, gain, s0, s1, s2, s3, out):
    total = s0[...] + s1[...] + s2[...] + s3[...]
    first = (lax.broadcasted_iota(jnp.int32, (8, HD), 0) == 0).astype(f32)
    spread = exact_dot(total, first, ((0,), (0,)))
    inverse = lax.rsqrt(spread / D + 1e-06)
    for h in range(LOCAL):
        scale = gain[:, cols(h)] * jax.nn.sigmoid(gate[:, cols(h)].astype(f32))
        out[:, cols(h)] = (heads[:, cols(h)] * inverse * scale).astype(bf16)


def half(c):
    return pl.ds(pl.multiple_of(c * HALF, HALF), HALF)


def gather_body(index, mask, q, k, v, other, far_q, head, tail, theirs, packed, sems):
    core = index[0] % 2

    def put(source, target, at):
        return pltpu.make_async_copy(source, target, sems.at[at])

    def layout(mine):
        def part(at, ref, owner, rows):
            if owner == mine:
                return ref.at[rows, half(core)]
            return other.at[slice(at * ROWS + rows.start, at * ROWS + rows.stop), :]

        low, high, whole = slice(0, BLK), slice(BLK, ROWS), slice(0, ROWS)
        copies = [
            put(part(0, q, 0, whole), far_q.at[:ROWS, :], 0),
            put(part(0, q, 1, whole), far_q.at[ROWS : 2 * ROWS, :], 1),
        ]
        for at, ref in ((1, k), (2, v)):
            base = (at - 1) * 3 * BLK
            sem = 3 * at - 1
            copies += [
                put(part(at, ref, 0, low), head.at[(at - 1) * BLK : at * BLK, :], sem),
                put(part(at, ref, 0, high), tail.at[base : base + BLK, :], sem + 1),
                put(part(at, ref, 1, whole), tail.at[base + BLK : base + 3 * BLK, :], sem + 2),
            ]
        return copies

    for mine in range(2):

        @pl.when(core == mine)
        def _():
            for copy in layout(mine):
                copy.start()

    fetch = put(other.at[3 * ROWS :, :NBLK], theirs, 8)
    fetch.start()
    fetch.wait()
    own = mask[...].astype(f32)
    arrived = theirs[...].astype(f32)[:2]
    first = jnp.where(core == 0, own, arrived)
    second = jnp.where(core == 0, arrived, own)
    rows = jnp.concatenate([first, second, jnp.zeros((12, NBLK), f32)], axis=0)
    packed[...] = jnp.concatenate([rows.astype(bf16)] * 4, axis=1)
    flags = put(packed, far_q.at[4 * BLK :, :], 9)
    flags.start()
    for mine in range(2):

        @pl.when(core == mine)
        def _():
            for copy in layout(mine):
                copy.wait()

    flags.wait()


def allowed(docs, flags, i, query, key):
    q_at = jnp.clip(query, 0, NBLK - 1)
    k_at = jnp.clip(key, 0, NBLK - 1)
    inside = (key >= 0) & (key < query) & (query < NBLK) & (docs[k_at] == docs[q_at])
    lane = lax.broadcasted_iota(jnp.int32, (1, NBLK), 1)
    wanted = jnp.where(inside, k_at, -1)
    ok = jnp.sum(jnp.where(lane == wanted, flags[i : i + 1, :], 0.0), axis=1, keepdims=True)
    return jnp.broadcast_to(jnp.where(ok > 0.5, 0.0, FILL), (BLK, BLK))


def block(i):
    return slice(i * BLK, (i + 1) * BLK)


def attend_head(q, keys, values, bias):
    scores = dot(q, keys, ((1,), (1,))) + bias
    top = jnp.max(scores, axis=1, keepdims=True)
    weights = jnp.exp2((scores - top) * EXP2_SCALE).astype(bf16)
    ones = jnp.ones(values.shape, bf16)
    both = dot(weights, jnp.concatenate([values, ones], axis=1), ((1,), (0,)))
    return both[:, :HD], top, both[:, HD:]


def attend_chip(index, docs, ahead, q, head, tail, out, tops, sums, bias):
    chip = index[0] // 2
    rows = q[4 * BLK :, :NBLK].astype(f32)
    for i in range(4):
        for j in range(4):
            if ahead == 0 and j == i:
                row = lax.broadcasted_iota(jnp.int32, (BLK, BLK), 0)
                col = lax.broadcasted_iota(jnp.int32, (BLK, BLK), 1)
                bias[block(i), block(j)] = jnp.where(col <= row, 0.0, FILL)
            elif ahead == 0 and j > i:
                bias[block(i), block(j)] = jnp.full((BLK, BLK), FILL, f32)
            else:
                bias[block(i), block(j)] = allowed(
                    docs, rows, i, 4 * (chip + ahead) + i, 4 * chip + j
                )
    lane = lax.broadcasted_iota(jnp.int32, (2 * BLK, HD), 1)
    for r in range(2):
        part = slice(r * 2 * BLK, (r + 1) * 2 * BLK)
        count = 4 * BLK if ahead or r else 2 * BLK
        top_table = jnp.zeros((2 * BLK, HD), f32)
        sum_table = jnp.zeros((2 * BLK, HD), f32)
        for h in range(HEADS):
            acc, top, total = attend_head(
                q[part, cols(h)],
                jnp.concatenate([head[:BLK, cols(h)], tail[: count - BLK, cols(h)]], axis=0),
                jnp.concatenate(
                    [head[BLK:, cols(h)], tail[3 * BLK : 2 * BLK + count, cols(h)]], axis=0
                ),
                bias[part, :count],
            )
            out[part, cols(h)] = acc / total
            top_table = jnp.where(lane == h, top, top_table)
            sum_table = jnp.where(lane == h, total, sum_table)
        tops[part, :] = top_table
        sums[part, :] = sum_table


def near_body(index, docs, q, head, tail, out, tops, sums, bias):
    attend_chip(index, docs, 0, q, head, tail, out, tops, sums, bias)


def next_body(index, docs, q, head, tail, out, tops, sums, bias):
    attend_chip(index, docs, 1, q, head, tail, out, tops, sums, bias)


def weighed(top1, sum1, top2, sum2):
    top = jnp.maximum(top1, top2)
    part1 = jnp.exp2((top1 - top) * EXP2_SCALE) * sum1
    part2 = jnp.exp2((top2 - top) * EXP2_SCALE) * sum2
    return top, part1 + part2, part2 / (part1 + part2)


def far_body(index, docs, q, tail, done, tops, sums, out, bias):
    chip = index[0] // 2
    flags = q[4 * BLK :, :NBLK].astype(f32)
    for i in range(3):
        for j in range(3):
            bias[block(i), block(j)] = allowed(
                docs, flags, i, 4 * (chip + 1) + i, 4 * (chip - 1) + 1 + j
            )
    rows = slice(0, 3 * BLK)
    rest = slice(3 * BLK, 4 * BLK)
    lane = lax.broadcasted_iota(jnp.int32, (3 * BLK, HD), 1)
    top_table = jnp.zeros((3 * BLK, HD), f32)
    sum_table = jnp.ones((3 * BLK, HD), f32)
    for h in range(HEADS):
        acc, top, total = attend_head(
            q[rows, cols(h)], tail[rows, cols(h)], tail[3 * BLK :, cols(h)], bias[...]
        )
        top_table = jnp.where(lane == h, top, top_table)
        sum_table = jnp.where(lane == h, total, sum_table)
        top1 = tops[rows, h : h + 1]
        _, _, share = weighed(top1, sums[rows, h : h + 1], top, total)
        here = done[rows, cols(h)]
        out[rows, cols(h)] = (here + (acc / total - here) * share).astype(bf16)
        out[rest, cols(h)] = done[rest, cols(h)].astype(bf16)
    top, total, _ = weighed(tops[rows, :], jnp.where(lane < HEADS, sums[rows, :], 1.0), top_table, sum_table)
    top = jnp.concatenate([top, tops[rest, :]], axis=0)
    total = jnp.concatenate([total, sums[rest, :]], axis=0)
    filler = jnp.zeros((LOCAL, 4 * BLK), f32)
    left = jnp.concatenate([top.T[:HEADS], total.T[:HEADS], filler], axis=0)
    for piece in range(3):
        part = left.astype(bf16)
        at = 4 * BLK + piece * 2 * LOCAL
        out[at : at + 2 * LOCAL, :] = part
        left = left - part.astype(f32)


def merge_body(index, near, tops, sums, far, mine, send, share):
    stats = jnp.zeros((2 * LOCAL, HALF), f32)
    for p in range(3):
        at = 4 * BLK + p * 2 * LOCAL
        stats = stats + far[at : at + 2 * LOCAL, :].astype(f32)
    pad = jnp.ones((HD - HEADS, 4 * BLK), f32)
    far_sums = jnp.concatenate([stats[HEADS : 2 * HEADS], pad], axis=0).T
    far_tops = jnp.concatenate([stats[:HEADS], pad], axis=0).T
    far_tops = jnp.where(far_sums > 0.0, far_tops, FILL)
    far_sums = jnp.where(far_sums > 0.0, far_sums, 1.0)
    lane = lax.broadcasted_iota(jnp.int32, (4 * BLK, HD), 1)
    near_sums = jnp.where(lane < HEADS, sums[...], 1.0)
    share[...] = weighed(tops[...], near_sums, far_tops, far_sums)[2]
    core = index[0] % 2
    for out, which in ((send, 1 - core), (mine, core)):
        rows = pl.ds(pl.multiple_of(which * ROWS, ROWS), ROWS)
        part = share[rows, :]
        for h in range(HEADS):
            own = near[rows, cols(h)]
            there = far[rows, cols(h)].astype(f32)
            out[:, cols(h)] = (own + (there - own) * part[:, h : h + 1]).astype(bf16)


def place_body(index, mine, other, out):
    core = index[0] % 2
    out[:, half(core)] = mine[...]
    out[:, half(1 - core)] = other[...]


SMALL = (gather_body, near_body, prefix_body, next_body, far_body, merge_body, norm_body, place_body)


def shifted(x, distance):
    return lax.ppermute(x, "seq", [(i, i + distance) for i in range(SHARDS) if 0 <= i + distance < SHARDS])


def swapped(x):
    return lax.ppermute(x, "seq", [(i, i ^ 1) for i in range(SHARDS)])


def turned(x, distance):
    return lax.ppermute(x, "head", [(i, (i + distance) % 4) for i in range(4)])


def per_device(
    lin_query,
    lin_key,
    lin_value,
    out_gate,
    norm_gain,
    decay_rate,
    soft_query,
    soft_key,
    soft_value,
    doc_ids,
    block_mask,
):
    like = jax.ShapeDtypeStruct
    index = lax.axis_index("seq").astype(jnp.int32).reshape(1)
    wide = like((ROWS, WIDTH), f32)
    narrow = like((ROWS, WIDTH), bf16)

    anywhere = pl.BlockSpec(memory_space=pl.ANY)
    state, sent = call(
        start_body,
        [like((WIDTH, HD), bf16), like((3 * ROWS + 16, HALF), bf16)],
        (index, decay_rate, block_mask, lin_key, lin_value, soft_query, soft_key, soft_value),
        [SMEM, anywhere, VMEM] + [anywhere] * 5,
        [
            pltpu.SMEM((LOCAL,), f32),
            pltpu.VMEM((ROWS, WIDTH), bf16),
            pltpu.VMEM((ROWS, WIDTH), bf16),
            pltpu.VMEM((16, HALF), bf16),
            pltpu.SemaphoreType.DMA,
            pltpu.SemaphoreType.DMA((LOCAL + 4,)),
        ],
    )
    other = swapped(sent)
    parts = lax.all_to_all(state.reshape(SHARDS, 16, HD), "seq", 0, 0)
    far_q, own_head, own_tail = call(
        gather_body,
        [
            like((2 * ROWS + 16, HALF), bf16),
            like((2 * BLK, HALF), bf16),
            like((6 * BLK, HALF), bf16),
        ],
        (index, block_mask, soft_query, soft_key, soft_value, other),
        [SMEM, VMEM] + [anywhere] * 4,
        [
            pltpu.VMEM((16, NBLK), bf16),
            pltpu.VMEM((16, HALF), bf16),
            pltpu.SemaphoreType.DMA((10,)),
        ],
    )
    tail = shifted(own_tail, 2)
    next_q = shifted(far_q, -2)

    (prefix,) = call(
        prefix_body,
        [like((SHARDS, 16, HD), bf16)],
        (index, decay_rate, parts),
        [SMEM, SMEM, VMEM],
        flops=PREFIX_COST,
    )
    prefix, doc_ids = lax.optimization_barrier((prefix, doc_ids))
    entering = lax.all_to_all(prefix, "seq", 0, 0).reshape(WIDTH, HD)
    inner, first, rates = call(
        inner_body,
        [wide, like((WIDTH, HD), f32), like((LOCAL, HD), f32)],
        (decay_rate, lin_query, lin_key, lin_value),
        [SMEM, VMEM, VMEM, VMEM],
    )
    tables = [like((4 * BLK, HALF), f32), like((4 * BLK, HD), f32), like((4 * BLK, HD), f32)]
    done, done_tops, done_sums = call(
        next_body,
        tables,
        (index, doc_ids, next_q, own_head, own_tail),
        [SMEM] * 2 + [VMEM] * 3,
        [pltpu.VMEM((4 * BLK, 4 * BLK), f32)],
    )
    (far,) = call(
        far_body,
        [like((4 * BLK + 48, HALF), bf16)],
        (index, doc_ids, next_q, tail, done, done_tops, done_sums),
        [SMEM] * 2 + [VMEM] * 5,
        [pltpu.VMEM((3 * BLK, 3 * BLK), f32)],
    )
    far = shifted(far, 2)
    heads, squares = call(
        carry_body,
        [wide, like((8, ROWS), f32)],
        (rates, inner, lin_query, first, entering),
        [VMEM] * 5,
        flops=CARRY_COST,
    )
    heads, own_head = lax.optimization_barrier((heads, own_head))
    others = [turned(squares, d) for d in (1, 2, 3)]
    near, tops, sums = call(
        near_body,
        tables,
        (index, doc_ids, far_q, own_head, own_tail),
        [SMEM] * 2 + [VMEM] * 3,
        [pltpu.VMEM((4 * BLK, 4 * BLK), f32)],
    )
    far, heads = lax.optimization_barrier((far, heads))
    mine, send = call(
        merge_body,
        [like((ROWS, HALF), bf16)] * 2,
        (index, near, tops, sums, far),
        [SMEM] + [VMEM] * 4,
        [pltpu.VMEM((4 * BLK, HD), f32)],
    )
    send, *others = lax.optimization_barrier((send, *others))
    (lin_output,) = call(
        norm_body,
        [narrow],
        (heads, out_gate, norm_gain.reshape(1, WIDTH), squares, *others),
        [VMEM] * 7,
    )

    (soft_output,) = call(
        place_body, [narrow], (index, mine, swapped(send)), [SMEM, VMEM, VMEM]
    )
    return (lin_output, soft_output)


def solution(mesh):
    rows = P("seq", "head")
    return jax.shard_map(
        per_device,
        mesh=mesh,
        in_specs=(
            rows, rows, rows, rows, P("head"), P("head"), rows, rows, rows, P(), P("seq", None),
        ),
        out_specs=(rows, rows),
        check_vma=False,
    )
```

```python
import math

import jax
import jax.numpy as jnp
from jax import lax
from jax.experimental import pallas as pl
from jax.experimental.pallas import tpu as pltpu
from jax.sharding import PartitionSpec as P

HD = 128
BLK = 128
NBLK = 128
ROWS = 256
LOCAL = 8
WIDTH = LOCAL * HD
HALF = WIDTH // 2
HEADS = LOCAL // 2
D = 4096
SHARDS = 64
FILL = -1e30
PREFIX_COST = 1_500_000_000
CARRY_COST = 10_000_000_000
EXP2_SCALE = HD ** (-0.5) * math.log2(math.e)

f32 = jnp.float32
bf16 = jnp.bfloat16

SMEM = pl.BlockSpec(memory_space=pltpu.SMEM)
VMEM = pl.BlockSpec(memory_space=pltpu.VMEM)


def call(body, outs, ins, specs, scratch=(), flops=1, outs_at=None):
    return pl.pallas_call(
        body,
        out_shape=outs,
        in_specs=specs,
        out_specs=outs_at or [VMEM] * len(outs),
        scratch_shapes=list(scratch),
        compiler_params=pltpu.CompilerParams(vmem_limit_bytes=(16 if body in SMALL else 60) * 1024 * 1024),
        cost_estimate=pl.CostEstimate(flops=flops, bytes_accessed=1, transcendentals=0),
    )(*ins)


def cols(h):
    return slice(h * HD, (h + 1) * HD)


def dot(a, b, dims):
    return lax.dot_general(a, b, (dims, ((), ())), preferred_element_type=f32)


def exact_dot(a, b, dims):
    return lax.dot_general(
        a, b, (dims, ((), ())), precision=lax.Precision.HIGHEST, preferred_element_type=f32
    )


def block_state(rate, k, v, h, b):
    rows = slice(b * BLK, (b + 1) * BLK)
    back = (BLK - 1.0) - lax.broadcasted_iota(jnp.int32, (BLK, HD), 0).astype(f32)
    decayed = (k[rows, cols(h)].astype(f32) * jnp.exp(-rate[h] * back)).astype(bf16)
    return dot(decayed, v[rows, cols(h)], ((0,), (0,)))


def start_body(
    index, rate_hbm, mask, k_hbm, v_hbm, sq, sk, sv, out, sent, rate, k, v, packed, rate_sem, sems
):
    other = 1 - index[0] % 2
    copies = [pltpu.make_async_copy(rate_hbm, rate, rate_sem)]
    for g in range(LOCAL // 2):
        at = slice(g * 2 * HD, (g + 1) * 2 * HD)
        copies.append(pltpu.make_async_copy(k_hbm.at[:, at], k.at[:, at], sems.at[2 * g]))
        copies.append(pltpu.make_async_copy(v_hbm.at[:, at], v.at[:, at], sems.at[2 * g + 1]))
    for at, ref in enumerate((sq, sk, sv)):
        rows = slice(at * ROWS, (at + 1) * ROWS)
        copies.append(
            pltpu.make_async_copy(ref.at[:, half(other)], sent.at[rows, :], sems.at[LOCAL + at])
        )
    for copy in copies:
        copy.start()
    flags = mask[...].astype(f32)
    flags = jnp.concatenate([flags, jnp.zeros((14, NBLK), f32)], axis=0).astype(bf16)
    packed[...] = jnp.concatenate([flags] * 4, axis=1)
    copies.append(pltpu.make_async_copy(packed, sent.at[3 * ROWS :, :], sems.at[LOCAL + 3]))
    copies[-1].start()
    copies[0].wait()
    for g in range(LOCAL // 2):
        copies[2 * g + 1].wait()
        copies[2 * g + 2].wait()
        for h in (2 * g, 2 * g + 1):
            step = jnp.exp(jnp.full((HD, HD), -rate[h] * BLK, f32))
            state = step * block_state(rate, k, v, h, 0) + block_state(rate, k, v, h, 1)
            out[cols(h), :] = state.astype(bf16)
    for copy in copies[LOCAL + 1 :]:
        copy.wait()


def prefix_body(index, rate, parts, out):
    step = jnp.exp(jnp.full((16, HD), -rate[index[0] // 8] * ROWS, f32))
    state = jnp.zeros((16, HD), f32)
    for i in range(SHARDS):
        out[i] = state.astype(bf16)
        if i + 1 < SHARDS:
            state = step * state + parts[i].astype(f32)


def inner_body(rate, q, k, v, out, first, rates):
    row = lax.broadcasted_iota(jnp.int32, (BLK, BLK), 0)
    col = lax.broadcasted_iota(jnp.int32, (BLK, BLK), 1)
    gap = jnp.maximum(row - col, 0).astype(f32)
    for h in range(LOCAL):
        rates[h : h + 1, :] = jnp.full((1, HD), rate[h], f32)
        first[cols(h), :] = block_state(rate, k, v, h, 0)
        decay = jnp.where(row >= col, jnp.exp(-rate[h] * gap), 0.0)
        for b in range(2):
            rows = slice(b * BLK, (b + 1) * BLK)
            scores = dot(q[rows, cols(h)], k[rows, cols(h)], ((1,), (1,)))
            out[rows, cols(h)] = dot(
                (scores * decay).astype(bf16), v[rows, cols(h)], ((1,), (0,))
            )


def carry_body(rates, inner, q, first, state, heads, squares):
    ahead = lax.broadcasted_iota(jnp.int32, (BLK, HD), 0).astype(f32) + 1.0
    totals = [jnp.zeros((BLK, HD), f32)] * 2
    for h in range(LOCAL):
        rate = rates[h : h + 1, :]
        decay = jnp.exp(-rate * ahead)
        entering = state[cols(h), :]
        middle = (jnp.exp(-rate * BLK) * entering.astype(f32) + first[cols(h), :]).astype(bf16)
        for b, block_start in enumerate((entering, middle)):
            rows = slice(b * BLK, (b + 1) * BLK)
            carried = dot(q[rows, cols(h)], block_start, ((1,), (0,)))
            value = inner[rows, cols(h)] + carried * decay
            heads[rows, cols(h)] = value
            totals[b] = totals[b] + value * value
    total = jnp.concatenate(totals, axis=0)
    squares[...] = exact_dot(jnp.ones((8, HD), f32), total, ((1,), (1,)))


def norm_body(heads, gate, gain, s0, s1, s2, s3, out):
    total = s0[...] + s1[...] + s2[...] + s3[...]
    first = (lax.broadcasted_iota(jnp.int32, (8, HD), 0) == 0).astype(f32)
    spread = exact_dot(total, first, ((0,), (0,)))
    inverse = lax.rsqrt(spread / D + 1e-06)
    for h in range(LOCAL):
        scale = gain[:, cols(h)] * jax.nn.sigmoid(gate[:, cols(h)].astype(f32))
        out[:, cols(h)] = (heads[:, cols(h)] * inverse * scale).astype(bf16)


def half(c):
    return pl.ds(pl.multiple_of(c * HALF, HALF), HALF)


def gather_body(index, mask, q, k, v, other, far_q, head, tail, theirs, packed, sems):
    core = index[0] % 2

    def put(source, target, at):
        return pltpu.make_async_copy(source, target, sems.at[at])

    def layout(mine):
        def part(at, ref, owner, rows):
            if owner == mine:
                return ref.at[rows, half(core)]
            return other.at[slice(at * ROWS + rows.start, at * ROWS + rows.stop), :]

        low, high, whole = slice(0, BLK), slice(BLK, ROWS), slice(0, ROWS)
        copies = [
            put(part(0, q, 0, whole), far_q.at[:ROWS, :], 0),
            put(part(0, q, 1, whole), far_q.at[ROWS : 2 * ROWS, :], 1),
        ]
        for at, ref in ((1, k), (2, v)):
            base = (at - 1) * 3 * BLK
            sem = 3 * at - 1
            copies += [
                put(part(at, ref, 0, low), head.at[(at - 1) * BLK : at * BLK, :], sem),
                put(part(at, ref, 0, high), tail.at[base : base + BLK, :], sem + 1),
                put(part(at, ref, 1, whole), tail.at[base + BLK : base + 3 * BLK, :], sem + 2),
            ]
        return copies

    for mine in range(2):

        @pl.when(core == mine)
        def _():
            for copy in layout(mine):
                copy.start()

    fetch = put(other.at[3 * ROWS :, :NBLK], theirs, 8)
    fetch.start()
    fetch.wait()
    own = mask[...].astype(f32)
    arrived = theirs[...].astype(f32)[:2]
    first = jnp.where(core == 0, own, arrived)
    second = jnp.where(core == 0, arrived, own)
    rows = jnp.concatenate([first, second, jnp.zeros((12, NBLK), f32)], axis=0)
    packed[...] = jnp.concatenate([rows.astype(bf16)] * 4, axis=1)
    flags = put(packed, far_q.at[4 * BLK :, :], 9)
    flags.start()
    for mine in range(2):

        @pl.when(core == mine)
        def _():
            for copy in layout(mine):
                copy.wait()

    flags.wait()


def allowed(docs, flags, i, query, key):
    q_at = jnp.clip(query, 0, NBLK - 1)
    k_at = jnp.clip(key, 0, NBLK - 1)
    inside = (key >= 0) & (key < query) & (query < NBLK) & (docs[k_at] == docs[q_at])
    lane = lax.broadcasted_iota(jnp.int32, (1, NBLK), 1)
    wanted = jnp.where(inside, k_at, -1)
    ok = jnp.sum(jnp.where(lane == wanted, flags[i : i + 1, :], 0.0), axis=1, keepdims=True)
    return jnp.broadcast_to(jnp.where(ok > 0.5, 0.0, FILL), (BLK, BLK))


def block(i):
    return slice(i * BLK, (i + 1) * BLK)


def attend_head(q, keys, values, bias):
    scores = dot(q, keys, ((1,), (1,))) + bias
    top = jnp.max(scores, axis=1, keepdims=True)
    weights = jnp.exp2((scores - top) * EXP2_SCALE).astype(bf16)
    ones = jnp.ones(values.shape, bf16)
    both = dot(weights, jnp.concatenate([values, ones], axis=1), ((1,), (0,)))
    return both[:, :HD], top, both[:, HD:]


def attend_chip(index, docs, ahead, q, head, tail, out, tops, sums, bias):
    chip = index[0] // 2
    rows = q[4 * BLK :, :NBLK].astype(f32)
    for i in range(4):
        for j in range(4):
            if ahead == 0 and j == i:
                row = lax.broadcasted_iota(jnp.int32, (BLK, BLK), 0)
                col = lax.broadcasted_iota(jnp.int32, (BLK, BLK), 1)
                bias[block(i), block(j)] = jnp.where(col <= row, 0.0, FILL)
            elif ahead == 0 and j > i:
                bias[block(i), block(j)] = jnp.full((BLK, BLK), FILL, f32)
            else:
                bias[block(i), block(j)] = allowed(
                    docs, rows, i, 4 * (chip + ahead) + i, 4 * chip + j
                )
    lane = lax.broadcasted_iota(jnp.int32, (2 * BLK, HD), 1)
    for r in range(2):
        part = slice(r * 2 * BLK, (r + 1) * 2 * BLK)
        count = 4 * BLK if ahead or r else 2 * BLK
        top_table = jnp.zeros((2 * BLK, HD), f32)
        sum_table = jnp.zeros((2 * BLK, HD), f32)
        for h in range(HEADS):
            acc, top, total = attend_head(
                q[part, cols(h)],
                jnp.concatenate([head[:BLK, cols(h)], tail[: count - BLK, cols(h)]], axis=0),
                jnp.concatenate(
                    [head[BLK:, cols(h)], tail[3 * BLK : 2 * BLK + count, cols(h)]], axis=0
                ),
                bias[part, :count],
            )
            out[part, cols(h)] = acc / total
            top_table = jnp.where(lane == h, top, top_table)
            sum_table = jnp.where(lane == h, total, sum_table)
        tops[part, :] = top_table
        sums[part, :] = sum_table


def near_body(index, docs, q, head, tail, out, tops, sums, bias):
    attend_chip(index, docs, 0, q, head, tail, out, tops, sums, bias)


def next_body(index, docs, q, head, tail, out, tops, sums, bias):
    attend_chip(index, docs, 1, q, head, tail, out, tops, sums, bias)


def weighed(top1, sum1, top2, sum2):
    top = jnp.maximum(top1, top2)
    part1 = jnp.exp2((top1 - top) * EXP2_SCALE) * sum1
    part2 = jnp.exp2((top2 - top) * EXP2_SCALE) * sum2
    return top, part1 + part2, part2 / (part1 + part2)


def far_body(index, docs, q, tail, done, tops, sums, out, bias):
    chip = index[0] // 2
    flags = q[4 * BLK :, :NBLK].astype(f32)
    for i in range(3):
        for j in range(3):
            bias[block(i), block(j)] = allowed(
                docs, flags, i, 4 * (chip + 1) + i, 4 * (chip - 1) + 1 + j
            )
    rows = slice(0, 3 * BLK)
    rest = slice(3 * BLK, 4 * BLK)
    lane = lax.broadcasted_iota(jnp.int32, (3 * BLK, HD), 1)
    top_table = jnp.zeros((3 * BLK, HD), f32)
    sum_table = jnp.ones((3 * BLK, HD), f32)
    for h in range(HEADS):
        acc, top, total = attend_head(
            q[rows, cols(h)], tail[rows, cols(h)], tail[3 * BLK :, cols(h)], bias[...]
        )
        top_table = jnp.where(lane == h, top, top_table)
        sum_table = jnp.where(lane == h, total, sum_table)
        top1 = tops[rows, h : h + 1]
        _, _, share = weighed(top1, sums[rows, h : h + 1], top, total)
        here = done[rows, cols(h)]
        out[rows, cols(h)] = (here + (acc / total - here) * share).astype(bf16)
        out[rest, cols(h)] = done[rest, cols(h)].astype(bf16)
    top, total, _ = weighed(tops[rows, :], jnp.where(lane < HEADS, sums[rows, :], 1.0), top_table, sum_table)
    top = jnp.concatenate([top, tops[rest, :]], axis=0)
    total = jnp.concatenate([total, sums[rest, :]], axis=0)
    filler = jnp.zeros((LOCAL, 4 * BLK), f32)
    left = jnp.concatenate([top.T[:HEADS], total.T[:HEADS], filler], axis=0)
    for piece in range(3):
        part = left.astype(bf16)
        at = 4 * BLK + piece * 2 * LOCAL
        out[at : at + 2 * LOCAL, :] = part
        left = left - part.astype(f32)


def merge_body(index, near, tops, sums, far, mine, send, share):
    stats = jnp.zeros((2 * LOCAL, HALF), f32)
    for p in range(3):
        at = 4 * BLK + p * 2 * LOCAL
        stats = stats + far[at : at + 2 * LOCAL, :].astype(f32)
    pad = jnp.ones((HD - HEADS, 4 * BLK), f32)
    far_sums = jnp.concatenate([stats[HEADS : 2 * HEADS], pad], axis=0).T
    far_tops = jnp.concatenate([stats[:HEADS], pad], axis=0).T
    far_tops = jnp.where(far_sums > 0.0, far_tops, FILL)
    far_sums = jnp.where(far_sums > 0.0, far_sums, 1.0)
    lane = lax.broadcasted_iota(jnp.int32, (4 * BLK, HD), 1)
    near_sums = jnp.where(lane < HEADS, sums[...], 1.0)
    share[...] = weighed(tops[...], near_sums, far_tops, far_sums)[2]
    core = index[0] % 2
    for out, which in ((send, 1 - core), (mine, core)):
        rows = pl.ds(pl.multiple_of(which * ROWS, ROWS), ROWS)
        part = share[rows, :]
        for h in range(HEADS):
            own = near[rows, cols(h)]
            there = far[rows, cols(h)].astype(f32)
            out[:, cols(h)] = (own + (there - own) * part[:, h : h + 1]).astype(bf16)


def place_body(index, mine, other, out):
    core = index[0] % 2
    out[:, half(core)] = mine[...]
    out[:, half(1 - core)] = other[...]


SMALL = (gather_body, near_body, prefix_body, next_body, far_body, merge_body, norm_body, place_body)


def shifted(x, distance):
    return lax.ppermute(x, "seq", [(i, i + distance) for i in range(SHARDS) if 0 <= i + distance < SHARDS])


def swapped(x):
    return lax.ppermute(x, "seq", [(i, i ^ 1) for i in range(SHARDS)])


def turned(x, distance):
    return lax.ppermute(x, "head", [(i, (i + distance) % 4) for i in range(4)])


def per_device(
    lin_query,
    lin_key,
    lin_value,
    out_gate,
    norm_gain,
    decay_rate,
    soft_query,
    soft_key,
    soft_value,
    doc_ids,
    block_mask,
):
    like = jax.ShapeDtypeStruct
    index = lax.axis_index("seq").astype(jnp.int32).reshape(1)
    wide = like((ROWS, WIDTH), f32)
    narrow = like((ROWS, WIDTH), bf16)

    anywhere = pl.BlockSpec(memory_space=pl.ANY)
    state, sent = call(
        start_body,
        [like((WIDTH, HD), bf16), like((3 * ROWS + 16, HALF), bf16)],
        (index, decay_rate, block_mask, lin_key, lin_value, soft_query, soft_key, soft_value),
        [SMEM, anywhere, VMEM] + [anywhere] * 5,
        [
            pltpu.SMEM((LOCAL,), f32),
            pltpu.VMEM((ROWS, WIDTH), bf16),
            pltpu.VMEM((ROWS, WIDTH), bf16),
            pltpu.VMEM((16, HALF), bf16),
            pltpu.SemaphoreType.DMA,
            pltpu.SemaphoreType.DMA((LOCAL + 4,)),
        ],
    )
    other = swapped(sent)
    parts = lax.all_to_all(state.reshape(SHARDS, 16, HD), "seq", 0, 0)
    far_q, own_head, own_tail = call(
        gather_body,
        [
            like((2 * ROWS + 16, HALF), bf16),
            like((2 * BLK, HALF), bf16),
            like((6 * BLK, HALF), bf16),
        ],
        (index, block_mask, soft_query, soft_key, soft_value, other),
        [SMEM, VMEM] + [anywhere] * 4,
        [
            pltpu.VMEM((16, NBLK), bf16),
            pltpu.VMEM((16, HALF), bf16),
            pltpu.SemaphoreType.DMA((10,)),
        ],
    )
    tail = shifted(own_tail, 2)
    next_q = shifted(far_q, -2)

    (prefix,) = call(
        prefix_body,
        [like((SHARDS, 16, HD), bf16)],
        (index, decay_rate, parts),
        [SMEM, SMEM, VMEM],
        flops=PREFIX_COST,
    )
    prefix, doc_ids = lax.optimization_barrier((prefix, doc_ids))
    entering = lax.all_to_all(prefix, "seq", 0, 0).reshape(WIDTH, HD)
    inner, first, rates = call(
        inner_body,
        [wide, like((WIDTH, HD), f32), like((LOCAL, HD), f32)],
        (decay_rate, lin_query, lin_key, lin_value),
        [SMEM, VMEM, VMEM, VMEM],
    )
    tables = [like((4 * BLK, HALF), f32), like((4 * BLK, HD), f32), like((4 * BLK, HD), f32)]
    done, done_tops, done_sums = call(
        next_body,
        tables,
        (index, doc_ids, next_q, own_head, own_tail),
        [SMEM] * 2 + [VMEM] * 3,
        [pltpu.VMEM((4 * BLK, 4 * BLK), f32)],
    )
    (far,) = call(
        far_body,
        [like((4 * BLK + 48, HALF), bf16)],
        (index, doc_ids, next_q, tail, done, done_tops, done_sums),
        [SMEM] * 2 + [VMEM] * 5,
        [pltpu.VMEM((3 * BLK, 3 * BLK), f32)],
    )
    far = shifted(far, 2)
    heads, squares = call(
        carry_body,
        [wide, like((8, ROWS), f32)],
        (rates, inner, lin_query, first, entering),
        [VMEM] * 5,
        flops=CARRY_COST,
    )
    heads, own_head = lax.optimization_barrier((heads, own_head))
    others = [turned(squares, d) for d in (1, 2, 3)]
    near, tops, sums = call(
        near_body,
        tables,
        (index, doc_ids, far_q, own_head, own_tail),
        [SMEM] * 2 + [VMEM] * 3,
        [pltpu.VMEM((4 * BLK, 4 * BLK), f32)],
    )
    far, heads = lax.optimization_barrier((far, heads))
    mine, send = call(
        merge_body,
        [like((ROWS, HALF), bf16)] * 2,
        (index, near, tops, sums, far),
        [SMEM] + [VMEM] * 4,
        [pltpu.VMEM((4 * BLK, HD), f32)],
    )
    send, *others = lax.optimization_barrier((send, *others))
    (lin_output,) = call(
        norm_body,
        [narrow],
        (heads, out_gate, norm_gain.reshape(1, WIDTH), squares, *others),
        [VMEM] * 7,
    )

    (soft_output,) = call(
        place_body, [narrow], (index, mine, swapped(send)), [SMEM, VMEM, VMEM]
    )
    return (lin_output, soft_output)


def solution(mesh):
    rows = P("seq", "head")
    return jax.shard_map(
        per_device,
        mesh=mesh,
        in_specs=(
            rows, rows, rows, rows, P("head"), P("head"), rows, rows, rows, P(), P("seq", None),
        ),
        out_specs=(rows, rows),
        check_vma=False,
    )
```

```python
import math

import jax
import jax.numpy as jnp
from jax import lax
from jax.experimental import pallas as pl
from jax.experimental.pallas import tpu as pltpu
from jax.sharding import PartitionSpec as P

HD = 128
BLK = 128
NBLK = 128
ROWS = 256
LOCAL = 8
WIDTH = LOCAL * HD
HALF = WIDTH // 2
HEADS = LOCAL // 2
D = 4096
SHARDS = 64
FILL = -1e30
PREFIX_COST = 1_500_000_000
CARRY_COST = 10_000_000_000
EXP2_SCALE = HD ** (-0.5) * math.log2(math.e)

f32 = jnp.float32
bf16 = jnp.bfloat16

SMEM = pl.BlockSpec(memory_space=pltpu.SMEM)
VMEM = pl.BlockSpec(memory_space=pltpu.VMEM)


def call(body, outs, ins, specs, scratch=(), flops=1, outs_at=None, grid=()):
    return pl.pallas_call(
        body,
        out_shape=outs,
        grid=grid,
        in_specs=specs,
        out_specs=outs_at or [VMEM] * len(outs),
        scratch_shapes=list(scratch),
        compiler_params=pltpu.CompilerParams(vmem_limit_bytes=(16 if body in SMALL else 60) * 1024 * 1024),
        cost_estimate=pl.CostEstimate(flops=flops, bytes_accessed=1, transcendentals=0),
    )(*ins)


def cols(h):
    return slice(h * HD, (h + 1) * HD)


def dot(a, b, dims):
    return lax.dot_general(a, b, (dims, ((), ())), preferred_element_type=f32)


def exact_dot(a, b, dims):
    return lax.dot_general(
        a, b, (dims, ((), ())), precision=lax.Precision.HIGHEST, preferred_element_type=f32
    )


def block_state(rate, k, v, h, b):
    rows = slice(b * BLK, (b + 1) * BLK)
    back = (BLK - 1.0) - lax.broadcasted_iota(jnp.int32, (BLK, HD), 0).astype(f32)
    decayed = (k[rows, cols(h)].astype(f32) * jnp.exp(-rate * back)).astype(bf16)
    return dot(decayed, v[rows, cols(h)], ((0,), (0,)))


def start_body(
    index, rate_hbm, mask, k_hbm, v_hbm, sq, sk, sv, out, sent, rate, k, v, packed, rate_sem, sems
):
    other = 1 - index[0] % 2
    copies = [pltpu.make_async_copy(rate_hbm, rate, rate_sem)]
    for g in range(LOCAL // 2):
        at = slice(g * 2 * HD, (g + 1) * 2 * HD)
        copies.append(pltpu.make_async_copy(k_hbm.at[:, at], k.at[:, at], sems.at[2 * g]))
        copies.append(pltpu.make_async_copy(v_hbm.at[:, at], v.at[:, at], sems.at[2 * g + 1]))
    for at, ref in enumerate((sq, sk, sv)):
        rows = slice(at * ROWS, (at + 1) * ROWS)
        copies.append(
            pltpu.make_async_copy(ref.at[:, half(other)], sent.at[rows, :], sems.at[LOCAL + at])
        )
    for copy in copies:
        copy.start()
    flags = mask[...].astype(f32)
    flags = jnp.concatenate([flags, jnp.zeros((14, NBLK), f32)], axis=0).astype(bf16)
    packed[...] = jnp.concatenate([flags] * 4, axis=1)
    copies.append(pltpu.make_async_copy(packed, sent.at[3 * ROWS :, :], sems.at[LOCAL + 3]))
    copies[-1].start()
    copies[0].wait()
    for g in range(LOCAL // 2):
        copies[2 * g + 1].wait()
        copies[2 * g + 2].wait()
        for h in (2 * g, 2 * g + 1):
            step = jnp.exp(jnp.full((HD, HD), -rate[h] * BLK, f32))
            state = step * block_state(rate[h], k, v, h, 0)
            state = state + block_state(rate[h], k, v, h, 1)
            out[cols(h), :] = state.astype(bf16)
    for copy in copies[LOCAL + 1 :]:
        copy.wait()


def prefix_body(index, rate, parts, out):
    step = jnp.exp(jnp.full((16, HD), -rate[index[0] // 8] * ROWS, f32))
    state = jnp.zeros((16, HD), f32)
    for i in range(SHARDS):
        out[i] = state.astype(bf16)
        if i + 1 < SHARDS:
            state = step * state + parts[i].astype(f32)


def inner_body(rate, q, k, v, out, first, rates):
    row = lax.broadcasted_iota(jnp.int32, (BLK, BLK), 0)
    col = lax.broadcasted_iota(jnp.int32, (BLK, BLK), 1)
    gap = jnp.maximum(row - col, 0).astype(f32)
    for h in range(LOCAL):
        rates[h : h + 1, :] = jnp.full((1, HD), rate[h], f32)
    for h in range(2):
        own = rate[2 * pl.program_id(0) + h]
        first[cols(h), :] = block_state(own, k, v, h, 0)
        decay = jnp.where(row >= col, jnp.exp(-own * gap), 0.0)
        for b in range(2):
            rows = slice(b * BLK, (b + 1) * BLK)
            scores = dot(q[rows, cols(h)], k[rows, cols(h)], ((1,), (1,)))
            out[rows, cols(h)] = dot(
                (scores * decay).astype(bf16), v[rows, cols(h)], ((1,), (0,))
            )


def carry_body(rates, inner, q, first, state, heads, squares, total):
    step = pl.program_id(0)
    ahead = lax.broadcasted_iota(jnp.int32, (BLK, HD), 0).astype(f32) + 1.0
    added = [jnp.zeros((BLK, HD), f32)] * 2
    for h in range(2):
        rate = rates[pl.ds(2 * step + h, 1), :]
        decay = jnp.exp(-rate * ahead)
        entering = state[cols(h), :]
        middle = (jnp.exp(-rate * BLK) * entering.astype(f32) + first[cols(h), :]).astype(bf16)
        for b, block_start in enumerate((entering, middle)):
            rows = slice(b * BLK, (b + 1) * BLK)
            carried = dot(q[rows, cols(h)], block_start, ((1,), (0,)))
            value = inner[rows, cols(h)] + carried * decay
            heads[rows, cols(h)] = value
            added[b] = added[b] + value * value
    both = jnp.concatenate(added, axis=0)

    @pl.when(step == 0)
    def _():
        total[...] = both

    @pl.when(step > 0)
    def _():
        total[...] = total[...] + both

    @pl.when(step == LOCAL // 2 - 1)
    def _():
        squares[...] = exact_dot(jnp.ones((8, HD), f32), total[...], ((1,), (1,)))


def norm_body(heads, gate, gain, s0, s1, s2, s3, out):
    total = s0[...] + s1[...] + s2[...] + s3[...]
    first = (lax.broadcasted_iota(jnp.int32, (8, HD), 0) == 0).astype(f32)
    spread = exact_dot(total, first, ((0,), (0,)))
    inverse = lax.rsqrt(spread / D + 1e-06)
    for h in range(LOCAL):
        scale = gain[:, cols(h)] * jax.nn.sigmoid(gate[:, cols(h)].astype(f32))
        out[:, cols(h)] = (heads[:, cols(h)] * inverse * scale).astype(bf16)


def half(c):
    return pl.ds(pl.multiple_of(c * HALF, HALF), HALF)


def gather_body(index, docs, doc_row, mask, q, k, v, other, far_q, head, tail, theirs, packed, sems):
    core = index[0] % 2

    def put(source, target, at):
        return pltpu.make_async_copy(source, target, sems.at[at])

    def layout(mine):
        def part(at, ref, owner, rows):
            if owner == mine:
                return ref.at[rows, half(core)]
            return other.at[slice(at * ROWS + rows.start, at * ROWS + rows.stop), :]

        low, high, whole = slice(0, BLK), slice(BLK, ROWS), slice(0, ROWS)
        copies = [
            put(part(0, q, 0, whole), far_q.at[:ROWS, :], 0),
            put(part(0, q, 1, whole), far_q.at[ROWS : 2 * ROWS, :], 1),
        ]
        for at, ref in ((1, k), (2, v)):
            base = (at - 1) * 3 * BLK
            sem = 3 * at - 1
            copies += [
                put(part(at, ref, 0, low), head.at[(at - 1) * BLK : at * BLK, :], sem),
                put(part(at, ref, 0, high), tail.at[base : base + BLK, :], sem + 1),
                put(part(at, ref, 1, whole), tail.at[base + BLK : base + 3 * BLK, :], sem + 2),
            ]
        return copies

    for mine in range(2):

        @pl.when(core == mine)
        def _():
            for copy in layout(mine):
                copy.start()

    fetch = put(other.at[3 * ROWS :, :NBLK], theirs, 8)
    fetch.start()
    fetch.wait()
    own = mask[...].astype(f32)
    arrived = theirs[...].astype(f32)[:2]
    first = jnp.where(core == 0, own, arrived)
    second = jnp.where(core == 0, arrived, own)
    rows = jnp.concatenate([first, second, jnp.zeros((12, NBLK), f32)], axis=0)
    line = lax.broadcasted_iota(jnp.int32, (16, NBLK), 0)
    lane = lax.broadcasted_iota(jnp.int32, (16, NBLK), 1)
    query = 4 * (index[0] // 2)
    document = jnp.full((16, NBLK), -1, jnp.int32)
    for i in range(4):
        document = jnp.where(line == i, docs[query + i], document)
    reach = (doc_row[...] == document) & (lane < query + line)
    rows = jnp.where(reach, rows, 0.0)
    packed[...] = jnp.concatenate([rows.astype(bf16)] * 4, axis=1)
    flags = put(packed, far_q.at[4 * BLK :, :], 9)
    flags.start()
    for mine in range(2):

        @pl.when(core == mine)
        def _():
            for copy in layout(mine):
                copy.wait()

    flags.wait()


def allowed(flags, i, key):
    lane = lax.broadcasted_iota(jnp.int32, (1, NBLK), 1)
    ok = jnp.sum(jnp.where(lane == key, flags[i : i + 1, :], 0.0), axis=1, keepdims=True)
    return jnp.broadcast_to(jnp.where(ok > 0.5, 0.0, FILL), (BLK, BLK))


def block(i):
    return slice(i * BLK, (i + 1) * BLK)


def attend_head(q, keys, values, bias):
    scores = dot(q, keys, ((1,), (1,))) + bias
    top = jnp.max(scores, axis=1, keepdims=True)
    weights = jnp.exp2((scores - top) * EXP2_SCALE).astype(bf16)
    ones = jnp.ones(values.shape, bf16)
    both = dot(weights, jnp.concatenate([values, ones], axis=1), ((1,), (0,)))
    return both[:, :HD], top, both[:, HD:]


def attend_chip(index, ahead, q, head, tail, out, tops, sums, bias):
    chip = index[0] // 2
    rows = q[4 * BLK :, :NBLK].astype(f32)
    for i in range(4):
        for j in range(4):
            if ahead == 0 and j == i:
                row = lax.broadcasted_iota(jnp.int32, (BLK, BLK), 0)
                col = lax.broadcasted_iota(jnp.int32, (BLK, BLK), 1)
                bias[block(i), block(j)] = jnp.where(col <= row, 0.0, FILL)
            elif ahead == 0 and j > i:
                bias[block(i), block(j)] = jnp.full((BLK, BLK), FILL, f32)
            else:
                bias[block(i), block(j)] = allowed(rows, i, 4 * chip + j)
    lane = lax.broadcasted_iota(jnp.int32, (2 * BLK, HD), 1)
    for r in range(2):
        part = slice(r * 2 * BLK, (r + 1) * 2 * BLK)
        count = 4 * BLK if ahead or r else 2 * BLK
        top_table = jnp.zeros((2 * BLK, HD), f32)
        sum_table = jnp.zeros((2 * BLK, HD), f32)
        for h in range(HEADS):
            acc, top, total = attend_head(
                q[part, cols(h)],
                jnp.concatenate([head[:BLK, cols(h)], tail[: count - BLK, cols(h)]], axis=0),
                jnp.concatenate(
                    [head[BLK:, cols(h)], tail[3 * BLK : 2 * BLK + count, cols(h)]], axis=0
                ),
                bias[part, :count],
            )
            out[part, cols(h)] = acc / total
            top_table = jnp.where(lane == h, top, top_table)
            sum_table = jnp.where(lane == h, total, sum_table)
        tops[part, :] = top_table
        sums[part, :] = sum_table


def near_body(index, q, head, tail, out, tops, sums, bias):
    attend_chip(index, 0, q, head, tail, out, tops, sums, bias)


def next_body(index, q, head, tail, out, tops, sums, bias):
    attend_chip(index, 1, q, head, tail, out, tops, sums, bias)


def weighed(top1, sum1, top2, sum2):
    top = jnp.maximum(top1, top2)
    part1 = jnp.exp2((top1 - top) * EXP2_SCALE) * sum1
    part2 = jnp.exp2((top2 - top) * EXP2_SCALE) * sum2
    return top, part1 + part2, part2 / (part1 + part2)


def far_body(index, q, tail, done, tops, sums, out, bias):
    chip = index[0] // 2
    flags = q[4 * BLK :, :NBLK].astype(f32)
    for i in range(3):
        for j in range(3):
            bias[block(i), block(j)] = allowed(flags, i, 4 * (chip - 1) + 1 + j)
    rows = slice(0, 3 * BLK)
    rest = slice(3 * BLK, 4 * BLK)
    lane = lax.broadcasted_iota(jnp.int32, (3 * BLK, HD), 1)
    top_table = jnp.zeros((3 * BLK, HD), f32)
    sum_table = jnp.ones((3 * BLK, HD), f32)
    for h in range(HEADS):
        acc, top, total = attend_head(
            q[rows, cols(h)], tail[rows, cols(h)], tail[3 * BLK :, cols(h)], bias[...]
        )
        top_table = jnp.where(lane == h, top, top_table)
        sum_table = jnp.where(lane == h, total, sum_table)
        top1 = tops[rows, h : h + 1]
        _, _, share = weighed(top1, sums[rows, h : h + 1], top, total)
        here = done[rows, cols(h)]
        out[rows, cols(h)] = (here + (acc / total - here) * share).astype(bf16)
        out[rest, cols(h)] = done[rest, cols(h)].astype(bf16)
    top, total, _ = weighed(tops[rows, :], jnp.where(lane < HEADS, sums[rows, :], 1.0), top_table, sum_table)
    top = jnp.concatenate([top, tops[rest, :]], axis=0)
    total = jnp.concatenate([total, sums[rest, :]], axis=0)
    filler = jnp.zeros((LOCAL, 4 * BLK), f32)
    left = jnp.concatenate([top.T[:HEADS], total.T[:HEADS], filler], axis=0)
    for piece in range(3):
        part = left.astype(bf16)
        at = 4 * BLK + piece * 2 * LOCAL
        out[at : at + 2 * LOCAL, :] = part
        left = left - part.astype(f32)


def merge_body(index, near, tops, sums, far, mine, send, share):
    stats = jnp.zeros((2 * LOCAL, HALF), f32)
    for p in range(3):
        at = 4 * BLK + p * 2 * LOCAL
        stats = stats + far[at : at + 2 * LOCAL, :].astype(f32)
    pad = jnp.ones((HD - HEADS, 4 * BLK), f32)
    far_sums = jnp.concatenate([stats[HEADS : 2 * HEADS], pad], axis=0).T
    far_tops = jnp.concatenate([stats[:HEADS], pad], axis=0).T
    far_tops = jnp.where(far_sums > 0.0, far_tops, FILL)
    far_sums = jnp.where(far_sums > 0.0, far_sums, 1.0)
    lane = lax.broadcasted_iota(jnp.int32, (4 * BLK, HD), 1)
    near_sums = jnp.where(lane < HEADS, sums[...], 1.0)
    share[...] = weighed(tops[...], near_sums, far_tops, far_sums)[2]
    core = index[0] % 2
    for out, which in ((send, 1 - core), (mine, core)):
        rows = pl.ds(pl.multiple_of(which * ROWS, ROWS), ROWS)
        part = share[rows, :]
        for h in range(HEADS):
            own = near[rows, cols(h)]
            there = far[rows, cols(h)].astype(f32)
            out[:, cols(h)] = (own + (there - own) * part[:, h : h + 1]).astype(bf16)


def place_body(index, mine, other, out):
    core = index[0] % 2
    out[:, half(core)] = mine[...]
    out[:, half(1 - core)] = other[...]


SMALL = (gather_body, near_body, prefix_body, next_body, far_body, merge_body, norm_body, place_body)


def shifted(x, distance):
    return lax.ppermute(x, "seq", [(i, i + distance) for i in range(SHARDS) if 0 <= i + distance < SHARDS])


def swapped(x):
    return lax.ppermute(x, "seq", [(i, i ^ 1) for i in range(SHARDS)])


def turned(x, distance):
    return lax.ppermute(x, "head", [(i, (i + distance) % 4) for i in range(4)])


def per_device(
    lin_query,
    lin_key,
    lin_value,
    out_gate,
    norm_gain,
    decay_rate,
    soft_query,
    soft_key,
    soft_value,
    doc_ids,
    block_mask,
):
    like = jax.ShapeDtypeStruct
    index = lax.axis_index("seq").astype(jnp.int32).reshape(1)
    wide = like((ROWS, WIDTH), f32)
    narrow = like((ROWS, WIDTH), bf16)

    anywhere = pl.BlockSpec(memory_space=pl.ANY)
    state, sent = call(
        start_body,
        [like((WIDTH, HD), bf16), like((3 * ROWS + 16, HALF), bf16)],
        (index, decay_rate, block_mask, lin_key, lin_value, soft_query, soft_key, soft_value),
        [SMEM, anywhere, VMEM] + [anywhere] * 5,
        [
            pltpu.SMEM((LOCAL,), f32),
            pltpu.VMEM((ROWS, WIDTH), bf16),
            pltpu.VMEM((ROWS, WIDTH), bf16),
            pltpu.VMEM((16, HALF), bf16),
            pltpu.SemaphoreType.DMA,
            pltpu.SemaphoreType.DMA((LOCAL + 4,)),
        ],
    )
    other = swapped(sent)
    parts = lax.all_to_all(state.reshape(SHARDS, 16, HD), "seq", 0, 0)
    far_q, own_head, own_tail = call(
        gather_body,
        [
            like((2 * ROWS + 16, HALF), bf16),
            like((2 * BLK, HALF), bf16),
            like((6 * BLK, HALF), bf16),
        ],
        (
            index, doc_ids, doc_ids.reshape(1, NBLK), block_mask,
            soft_query, soft_key, soft_value, other,
        ),
        [SMEM, SMEM, VMEM, VMEM] + [anywhere] * 4,
        [
            pltpu.VMEM((16, NBLK), bf16),
            pltpu.VMEM((16, HALF), bf16),
            pltpu.SemaphoreType.DMA((10,)),
        ],
    )
    tail = shifted(own_tail, 2)
    next_q = shifted(far_q, -2)

    (prefix,) = call(
        prefix_body,
        [like((SHARDS, 16, HD), bf16)],
        (index, decay_rate, parts),
        [SMEM, SMEM, VMEM],
        flops=PREFIX_COST,
    )
    prefix, own_head = lax.optimization_barrier((prefix, own_head))
    entering = lax.all_to_all(prefix, "seq", 0, 0).reshape(WIDTH, HD)
    pair_columns = pl.BlockSpec((ROWS, 2 * HD), lambda g: (0, g))
    pair_rows = pl.BlockSpec((2 * HD, HD), lambda g: (g, 0))
    whole_rates = pl.BlockSpec((LOCAL, HD), lambda g: (0, 0))
    inner, first, rates = call(
        inner_body,
        [wide, like((WIDTH, HD), f32), like((LOCAL, HD), f32)],
        (decay_rate, lin_query, lin_key, lin_value),
        [SMEM] + [pair_columns] * 3,
        outs_at=[pair_columns, pair_rows, whole_rates],
        grid=(LOCAL // 2,),
    )
    tables = [like((4 * BLK, HALF), f32), like((4 * BLK, HD), f32), like((4 * BLK, HD), f32)]
    done, done_tops, done_sums = call(
        next_body,
        tables,
        (index, next_q, own_head, own_tail),
        [SMEM] + [VMEM] * 3,
        [pltpu.VMEM((4 * BLK, 4 * BLK), f32)],
    )
    (far,) = call(
        far_body,
        [like((4 * BLK + 48, HALF), bf16)],
        (index, next_q, tail, done, done_tops, done_sums),
        [SMEM] + [VMEM] * 5,
        [pltpu.VMEM((3 * BLK, 3 * BLK), f32)],
    )
    far = shifted(far, 2)
    heads, squares = call(
        carry_body,
        [wide, like((8, ROWS), f32)],
        (rates, inner, lin_query, first, entering),
        [whole_rates, pair_columns, pair_columns, pair_rows, pair_rows],
        [pltpu.VMEM((ROWS, HD), f32)],
        outs_at=[pair_columns, pl.BlockSpec((8, ROWS), lambda g: (0, 0))],
        grid=(LOCAL // 2,),
        flops=CARRY_COST,
    )
    heads, own_head = lax.optimization_barrier((heads, own_head))
    others = [turned(squares, d) for d in (1, 2, 3)]
    near, tops, sums = call(
        near_body,
        tables,
        (index, far_q, own_head, own_tail),
        [SMEM] + [VMEM] * 3,
        [pltpu.VMEM((4 * BLK, 4 * BLK), f32)],
    )
    far, heads = lax.optimization_barrier((far, heads))
    mine, send = call(
        merge_body,
        [like((ROWS, HALF), bf16)] * 2,
        (index, near, tops, sums, far),
        [SMEM] + [VMEM] * 4,
        [pltpu.VMEM((4 * BLK, HD), f32)],
    )
    send, *others = lax.optimization_barrier((send, *others))
    (lin_output,) = call(
        norm_body,
        [narrow],
        (heads, out_gate, norm_gain.reshape(1, WIDTH), squares, *others),
        [VMEM] * 7,
    )

    (soft_output,) = call(
        place_body, [narrow], (index, mine, swapped(send)), [SMEM, VMEM, VMEM]
    )
    return (lin_output, soft_output)


def solution(mesh):
    rows = P("seq", "head")
    return jax.shard_map(
        per_device,
        mesh=mesh,
        in_specs=(
            rows, rows, rows, rows, P("head"), P("head"), rows, rows, rows, P(), P("seq", None),
        ),
        out_specs=(rows, rows),
        check_vma=False,
    )
```

```python
import math

import jax
import jax.numpy as jnp
from jax import lax
from jax.experimental import pallas as pl
from jax.experimental.pallas import tpu as pltpu
from jax.sharding import PartitionSpec as P

HD = 128
BLK = 128
NBLK = 128
ROWS = 256
LOCAL = 8
WIDTH = LOCAL * HD
HALF = WIDTH // 2
HEADS = LOCAL // 2
D = 4096
SHARDS = 64
FILL = -1e30
PREFIX_COST = 1_500_000_000
CARRY_COST = 10_000_000_000
EXP2_SCALE = HD ** (-0.5) * math.log2(math.e)

f32 = jnp.float32
bf16 = jnp.bfloat16

SMEM = pl.BlockSpec(memory_space=pltpu.SMEM)
VMEM = pl.BlockSpec(memory_space=pltpu.VMEM)


def call(body, outs, ins, specs, scratch=(), flops=1):
    return pl.pallas_call(
        body,
        out_shape=outs,
        in_specs=specs,
        out_specs=[VMEM] * len(outs),
        scratch_shapes=list(scratch),
        compiler_params=pltpu.CompilerParams(vmem_limit_bytes=(16 if body in SMALL else 60) * 1024 * 1024),
        cost_estimate=pl.CostEstimate(flops=flops, bytes_accessed=1, transcendentals=0),
    )(*ins)


def cols(h):
    return slice(h * HD, (h + 1) * HD)


def dot(a, b, dims):
    return lax.dot_general(a, b, (dims, ((), ())), preferred_element_type=f32)


def exact_dot(a, b, dims):
    return lax.dot_general(
        a, b, (dims, ((), ())), precision=lax.Precision.HIGHEST, preferred_element_type=f32
    )


def block_state(rate, k, v, h, b):
    rows = slice(b * BLK, (b + 1) * BLK)
    back = (BLK - 1.0) - lax.broadcasted_iota(jnp.int32, (BLK, HD), 0).astype(f32)
    decayed = (k[rows, cols(h)].astype(f32) * jnp.exp(-rate * back)).astype(bf16)
    return dot(decayed, v[rows, cols(h)], ((0,), (0,)))


def start_body(
    index, docs, doc_row, rate_hbm, mask, k_hbm, v_hbm, sq, sk, sv, out, sent, own, rate, k, v, packed, rate_sem, sems
):
    other = 1 - index[0] % 2
    copies = [pltpu.make_async_copy(rate_hbm, rate, rate_sem)]
    for g in range(LOCAL // 2):
        at = slice(g * 2 * HD, (g + 1) * 2 * HD)
        copies.append(pltpu.make_async_copy(k_hbm.at[:, at], k.at[:, at], sems.at[2 * g]))
        copies.append(pltpu.make_async_copy(v_hbm.at[:, at], v.at[:, at], sems.at[2 * g + 1]))
    for at, ref in enumerate((sq, sk, sv)):
        rows = slice(at * ROWS, (at + 1) * ROWS)
        copies.append(
            pltpu.make_async_copy(ref.at[:, half(other)], sent.at[rows, :], sems.at[LOCAL + at])
        )
    for copy in copies:
        copy.start()
    line = lax.broadcasted_iota(jnp.int32, (2, NBLK), 0)
    lane = lax.broadcasted_iota(jnp.int32, (2, NBLK), 1)
    query = 2 * index[0]
    document = jnp.where(line == 0, docs[query], docs[query + 1])
    reach = (doc_row[...] == document) & (lane < query + line) & (mask[...] == 1)
    flags = jnp.where(reach, 1.0, 0.0)
    flags = jnp.concatenate([flags, jnp.zeros((14, NBLK), f32)], axis=0)
    own[...] = flags
    flags = flags.astype(bf16)
    packed[...] = jnp.concatenate([flags] * 4, axis=1)
    copies.append(pltpu.make_async_copy(packed, sent.at[3 * ROWS :, :], sems.at[LOCAL + 3]))
    copies[-1].start()
    copies[0].wait()
    for g in range(LOCAL // 2):
        copies[2 * g + 1].wait()
        copies[2 * g + 2].wait()
        for h in (2 * g, 2 * g + 1):
            step = jnp.exp(jnp.full((HD, HD), -rate[h] * BLK, f32))
            state = step * block_state(rate[h], k, v, h, 0)
            state = state + block_state(rate[h], k, v, h, 1)
            out[cols(h), :] = state.astype(bf16)
    for copy in copies[LOCAL + 1 :]:
        copy.wait()


def prefix_body(index, rate, parts, out):
    step = jnp.exp(jnp.full((16, HD), -rate[index[0] // 8] * ROWS, f32))
    state = jnp.zeros((16, HD), f32)
    for i in range(SHARDS):
        out[i] = state.astype(bf16)
        if i + 1 < SHARDS:
            state = step * state + parts[i].astype(f32)


def inner_body(rate, q, k, v, out, first, rates):
    row = lax.broadcasted_iota(jnp.int32, (BLK, BLK), 0)
    col = lax.broadcasted_iota(jnp.int32, (BLK, BLK), 1)
    gap = jnp.maximum(row - col, 0).astype(f32)
    for h in range(LOCAL):
        rates[h : h + 1, :] = jnp.full((1, HD), rate[h], f32)
        first[cols(h), :] = block_state(rate[h], k, v, h, 0)
        decay = jnp.where(row >= col, jnp.exp(-rate[h] * gap), 0.0)
        for b in range(2):
            rows = slice(b * BLK, (b + 1) * BLK)
            scores = dot(q[rows, cols(h)], k[rows, cols(h)], ((1,), (1,)))
            out[rows, cols(h)] = dot(
                (scores * decay).astype(bf16), v[rows, cols(h)], ((1,), (0,))
            )


def carry_body(rates, inner, q, first, state, heads, squares):
    ahead = lax.broadcasted_iota(jnp.int32, (BLK, HD), 0).astype(f32) + 1.0
    totals = [jnp.zeros((BLK, HD), f32)] * 2
    for h in range(LOCAL):
        rate = rates[h : h + 1, :]
        decay = jnp.exp(-rate * ahead)
        entering = state[cols(h), :]
        middle = (jnp.exp(-rate * BLK) * entering.astype(f32) + first[cols(h), :]).astype(bf16)
        for b, block_start in enumerate((entering, middle)):
            rows = slice(b * BLK, (b + 1) * BLK)
            carried = dot(q[rows, cols(h)], block_start, ((1,), (0,)))
            value = inner[rows, cols(h)] + carried * decay
            heads[rows, cols(h)] = value
            totals[b] = totals[b] + value * value
    total = jnp.concatenate(totals, axis=0)
    squares[...] = exact_dot(jnp.ones((8, HD), f32), total, ((1,), (1,)))


def norm_body(heads, gate, gain, s0, s1, s2, s3, out):
    total = s0[...] + s1[...] + s2[...] + s3[...]
    first = (lax.broadcasted_iota(jnp.int32, (8, HD), 0) == 0).astype(f32)
    spread = exact_dot(total, first, ((0,), (0,)))
    inverse = lax.rsqrt(spread / D + 1e-06)
    for h in range(LOCAL):
        scale = gain[:, cols(h)] * jax.nn.sigmoid(gate[:, cols(h)].astype(f32))
        out[:, cols(h)] = (heads[:, cols(h)] * inverse * scale).astype(bf16)


def half(c):
    return pl.ds(pl.multiple_of(c * HALF, HALF), HALF)


def gather_body(index, flags_own, q, k, v, other, far_q, head, tail, theirs, packed, sems):
    core = index[0] % 2

    def put(source, target, at):
        return pltpu.make_async_copy(source, target, sems.at[at])

    def layout(mine):
        def part(at, ref, owner, rows):
            if owner == mine:
                return ref.at[rows, half(core)]
            return other.at[slice(at * ROWS + rows.start, at * ROWS + rows.stop), :]

        low, high, whole = slice(0, BLK), slice(BLK, ROWS), slice(0, ROWS)
        copies = [
            put(part(0, q, 0, whole), far_q.at[:ROWS, :], 0),
            put(part(0, q, 1, whole), far_q.at[ROWS : 2 * ROWS, :], 1),
        ]
        for at, ref in ((1, k), (2, v)):
            base = (at - 1) * 3 * BLK
            sem = 3 * at - 1
            copies += [
                put(part(at, ref, 0, low), head.at[(at - 1) * BLK : at * BLK, :], sem),
                put(part(at, ref, 0, high), tail.at[base : base + BLK, :], sem + 1),
                put(part(at, ref, 1, whole), tail.at[base + BLK : base + 3 * BLK, :], sem + 2),
            ]
        return copies

    for mine in range(2):

        @pl.when(core == mine)
        def _():
            for copy in layout(mine):
                copy.start()

    fetch = put(other.at[3 * ROWS :, :NBLK], theirs, 8)
    fetch.start()
    fetch.wait()
    own = flags_own[:2, :]
    arrived = theirs[...].astype(f32)[:2]
    first = jnp.where(core == 0, own, arrived)
    second = jnp.where(core == 0, arrived, own)
    rows = jnp.concatenate([first, second, jnp.zeros((12, NBLK), f32)], axis=0)
    packed[...] = jnp.concatenate([rows.astype(bf16)] * 4, axis=1)
    flags = put(packed, far_q.at[4 * BLK :, :], 9)
    flags.start()
    for mine in range(2):

        @pl.when(core == mine)
        def _():
            for copy in layout(mine):
                copy.wait()

    flags.wait()


def allowed(flags, i, key):
    lane = lax.broadcasted_iota(jnp.int32, (1, NBLK), 1)
    ok = jnp.sum(jnp.where(lane == key, flags[i : i + 1, :], 0.0), axis=1, keepdims=True)
    return jnp.broadcast_to(jnp.where(ok > 0.5, 0.0, FILL), (BLK, BLK))


def block(i):
    return slice(i * BLK, (i + 1) * BLK)


def attend_head(q, keys, values, bias):
    scores = dot(q, keys, ((1,), (1,))) + bias
    top = jnp.max(scores, axis=1, keepdims=True)
    weights = jnp.exp2((scores - top) * EXP2_SCALE).astype(bf16)
    ones = jnp.ones(values.shape, bf16)
    both = dot(weights, jnp.concatenate([values, ones], axis=1), ((1,), (0,)))
    return both[:, :HD], top, both[:, HD:]


def attend_chip(index, ahead, q, head, tail, out, tops, sums, bias):
    chip = index[0] // 2
    rows = q[4 * BLK :, :NBLK].astype(f32)
    for i in range(4):
        for j in range(4):
            if ahead == 0 and j == i:
                row = lax.broadcasted_iota(jnp.int32, (BLK, BLK), 0)
                col = lax.broadcasted_iota(jnp.int32, (BLK, BLK), 1)
                bias[block(i), block(j)] = jnp.where(col <= row, 0.0, FILL)
            elif ahead == 0 and j > i:
                bias[block(i), block(j)] = jnp.full((BLK, BLK), FILL, f32)
            else:
                bias[block(i), block(j)] = allowed(rows, i, 4 * chip + j)
    lane = lax.broadcasted_iota(jnp.int32, (2 * BLK, HD), 1)
    for r in range(2):
        part = slice(r * 2 * BLK, (r + 1) * 2 * BLK)
        count = 4 * BLK if ahead or r else 2 * BLK
        top_table = jnp.zeros((2 * BLK, HD), f32)
        sum_table = jnp.zeros((2 * BLK, HD), f32)
        for h in range(HEADS):
            acc, top, total = attend_head(
                q[part, cols(h)],
                jnp.concatenate([head[:BLK, cols(h)], tail[: count - BLK, cols(h)]], axis=0),
                jnp.concatenate(
                    [head[BLK:, cols(h)], tail[3 * BLK : 2 * BLK + count, cols(h)]], axis=0
                ),
                bias[part, :count],
            )
            out[part, cols(h)] = acc / total
            top_table = jnp.where(lane == h, top, top_table)
            sum_table = jnp.where(lane == h, total, sum_table)
        tops[part, :] = top_table
        sums[part, :] = sum_table


def near_body(index, q, head, tail, out, tops, sums, bias):
    attend_chip(index, 0, q, head, tail, out, tops, sums, bias)


def next_body(index, q, head, tail, out, tops, sums, bias):
    attend_chip(index, 1, q, head, tail, out, tops, sums, bias)


def weighed(top1, sum1, top2, sum2):
    top = jnp.maximum(top1, top2)
    part1 = jnp.exp2((top1 - top) * EXP2_SCALE) * sum1
    part2 = jnp.exp2((top2 - top) * EXP2_SCALE) * sum2
    return top, part1 + part2, part2 / (part1 + part2)


def far_body(index, q, tail, done, tops, sums, out, bias):
    chip = index[0] // 2
    flags = q[4 * BLK :, :NBLK].astype(f32)
    for i in range(3):
        for j in range(3):
            bias[block(i), block(j)] = allowed(flags, i, 4 * (chip - 1) + 1 + j)
    rows = slice(0, 3 * BLK)
    rest = slice(3 * BLK, 4 * BLK)
    lane = lax.broadcasted_iota(jnp.int32, (3 * BLK, HD), 1)
    top_table = jnp.zeros((3 * BLK, HD), f32)
    sum_table = jnp.ones((3 * BLK, HD), f32)
    for h in range(HEADS):
        acc, top, total = attend_head(
            q[rows, cols(h)], tail[rows, cols(h)], tail[3 * BLK :, cols(h)], bias[...]
        )
        top_table = jnp.where(lane == h, top, top_table)
        sum_table = jnp.where(lane == h, total, sum_table)
        top1 = tops[rows, h : h + 1]
        _, _, share = weighed(top1, sums[rows, h : h + 1], top, total)
        here = done[rows, cols(h)]
        out[rows, cols(h)] = (here + (acc / total - here) * share).astype(bf16)
        out[rest, cols(h)] = done[rest, cols(h)].astype(bf16)
    top, total, _ = weighed(tops[rows, :], jnp.where(lane < HEADS, sums[rows, :], 1.0), top_table, sum_table)
    top = jnp.concatenate([top, tops[rest, :]], axis=0)
    total = jnp.concatenate([total, sums[rest, :]], axis=0)
    filler = jnp.zeros((LOCAL, 4 * BLK), f32)
    left = jnp.concatenate([top.T[:HEADS], total.T[:HEADS], filler], axis=0)
    for piece in range(3):
        part = left.astype(bf16)
        at = 4 * BLK + piece * 2 * LOCAL
        out[at : at + 2 * LOCAL, :] = part
        left = left - part.astype(f32)


def merge_body(index, near, tops, sums, far, mine, send, share):
    stats = jnp.zeros((2 * LOCAL, HALF), f32)
    for p in range(3):
        at = 4 * BLK + p * 2 * LOCAL
        stats = stats + far[at : at + 2 * LOCAL, :].astype(f32)
    pad = jnp.ones((HD - HEADS, 4 * BLK), f32)
    far_sums = jnp.concatenate([stats[HEADS : 2 * HEADS], pad], axis=0).T
    far_tops = jnp.concatenate([stats[:HEADS], pad], axis=0).T
    far_tops = jnp.where(far_sums > 0.0, far_tops, FILL)
    far_sums = jnp.where(far_sums > 0.0, far_sums, 1.0)
    lane = lax.broadcasted_iota(jnp.int32, (4 * BLK, HD), 1)
    near_sums = jnp.where(lane < HEADS, sums[...], 1.0)
    share[...] = weighed(tops[...], near_sums, far_tops, far_sums)[2]
    core = index[0] % 2
    for out, which in ((send, 1 - core), (mine, core)):
        rows = pl.ds(pl.multiple_of(which * ROWS, ROWS), ROWS)
        part = share[rows, :]
        for h in range(HEADS):
            own = near[rows, cols(h)]
            there = far[rows, cols(h)].astype(f32)
            out[:, cols(h)] = (own + (there - own) * part[:, h : h + 1]).astype(bf16)


def place_body(index, mine, other, out):
    core = index[0] % 2
    out[:, half(core)] = mine[...]
    out[:, half(1 - core)] = other[...]


SMALL = (gather_body, near_body, prefix_body, next_body, far_body, merge_body, norm_body, place_body)


def shifted(x, distance):
    return lax.ppermute(x, "seq", [(i, i + distance) for i in range(SHARDS) if 0 <= i + distance < SHARDS])


def swapped(x):
    return lax.ppermute(x, "seq", [(i, i ^ 1) for i in range(SHARDS)])


def turned(x, distance):
    return lax.ppermute(x, "head", [(i, (i + distance) % 4) for i in range(4)])


def per_device(
    lin_query,
    lin_key,
    lin_value,
    out_gate,
    norm_gain,
    decay_rate,
    soft_query,
    soft_key,
    soft_value,
    doc_ids,
    block_mask,
):
    like = jax.ShapeDtypeStruct
    index = lax.axis_index("seq").astype(jnp.int32).reshape(1)
    wide = like((ROWS, WIDTH), f32)
    narrow = like((ROWS, WIDTH), bf16)

    anywhere = pl.BlockSpec(memory_space=pl.ANY)
    state, sent, own_flags = call(
        start_body,
        [like((WIDTH, HD), bf16), like((3 * ROWS + 16, HALF), bf16), like((16, NBLK), f32)],
        (
            index, doc_ids, doc_ids.reshape(1, NBLK), decay_rate, block_mask,
            lin_key, lin_value, soft_query, soft_key, soft_value,
        ),
        [SMEM, SMEM, VMEM, anywhere, VMEM] + [anywhere] * 5,
        [
            pltpu.SMEM((LOCAL,), f32),
            pltpu.VMEM((ROWS, WIDTH), bf16),
            pltpu.VMEM((ROWS, WIDTH), bf16),
            pltpu.VMEM((16, HALF), bf16),
            pltpu.SemaphoreType.DMA,
            pltpu.SemaphoreType.DMA((LOCAL + 4,)),
        ],
    )
    other = swapped(sent)
    parts = lax.all_to_all(state.reshape(SHARDS, 16, HD), "seq", 0, 0)
    far_q, own_head, own_tail = call(
        gather_body,
        [
            like((2 * ROWS + 16, HALF), bf16),
            like((2 * BLK, HALF), bf16),
            like((6 * BLK, HALF), bf16),
        ],
        (index, own_flags, soft_query, soft_key, soft_value, other),
        [SMEM, VMEM] + [anywhere] * 4,
        [
            pltpu.VMEM((16, NBLK), bf16),
            pltpu.VMEM((16, HALF), bf16),
            pltpu.SemaphoreType.DMA((10,)),
        ],
    )
    tail = shifted(own_tail, 2)
    next_q = shifted(far_q, -2)

    (prefix,) = call(
        prefix_body,
        [like((SHARDS, 16, HD), bf16)],
        (index, decay_rate, parts),
        [SMEM, SMEM, VMEM],
        flops=PREFIX_COST,
    )
    prefix, own_head = lax.optimization_barrier((prefix, own_head))
    entering = lax.all_to_all(prefix, "seq", 0, 0).reshape(WIDTH, HD)
    tables = [like((4 * BLK, HALF), f32), like((4 * BLK, HD), f32), like((4 * BLK, HD), f32)]
    done, done_tops, done_sums = call(
        next_body,
        tables,
        (index, next_q, own_head, own_tail),
        [SMEM] + [VMEM] * 3,
        [pltpu.VMEM((4 * BLK, 4 * BLK), f32)],
    )
    (far,) = call(
        far_body,
        [like((4 * BLK + 48, HALF), bf16)],
        (index, next_q, tail, done, done_tops, done_sums),
        [SMEM] + [VMEM] * 5,
        [pltpu.VMEM((3 * BLK, 3 * BLK), f32)],
    )
    far, lin_query = lax.optimization_barrier((far, lin_query))
    far = shifted(far, 2)
    inner, first, rates = call(
        inner_body,
        [wide, like((WIDTH, HD), f32), like((LOCAL, HD), f32)],
        (decay_rate, lin_query, lin_key, lin_value),
        [SMEM] + [VMEM] * 3,
    )
    heads, squares = call(
        carry_body,
        [wide, like((8, ROWS), f32)],
        (rates, inner, lin_query, first, entering),
        [VMEM] * 5,
        flops=CARRY_COST,
    )
    heads, own_head = lax.optimization_barrier((heads, own_head))
    others = [turned(squares, d) for d in (1, 2, 3)]
    near, tops, sums = call(
        near_body,
        tables,
        (index, far_q, own_head, own_tail),
        [SMEM] + [VMEM] * 3,
        [pltpu.VMEM((4 * BLK, 4 * BLK), f32)],
    )
    far, heads = lax.optimization_barrier((far, heads))
    mine, send = call(
        merge_body,
        [like((ROWS, HALF), bf16)] * 2,
        (index, near, tops, sums, far),
        [SMEM] + [VMEM] * 4,
        [pltpu.VMEM((4 * BLK, HD), f32)],
    )
    send, *others = lax.optimization_barrier((send, *others))
    (lin_output,) = call(
        norm_body,
        [narrow],
        (heads, out_gate, norm_gain.reshape(1, WIDTH), squares, *others),
        [VMEM] * 7,
    )

    (soft_output,) = call(
        place_body, [narrow], (index, mine, swapped(send)), [SMEM, VMEM, VMEM]
    )
    return (lin_output, soft_output)


def solution(mesh):
    rows = P("seq", "head")
    return jax.shard_map(
        per_device,
        mesh=mesh,
        in_specs=(
            rows, rows, rows, rows, P("head"), P("head"), rows, rows, rows, P(), P("seq", None),
        ),
        out_specs=(rows, rows),
        check_vma=False,
    )
```

```python
import math

import jax
import jax.numpy as jnp
from jax import lax
from jax.experimental import pallas as pl
from jax.experimental.pallas import tpu as pltpu
from jax.sharding import PartitionSpec as P

HD = 128
BLK = 128
NBLK = 128
ROWS = 256
LOCAL = 8
WIDTH = LOCAL * HD
HALF = WIDTH // 2
HEADS = LOCAL // 2
D = 4096
SHARDS = 64
FILL = -1e30
PREFIX_COST = 1_500_000_000
CARRY_COST = 10_000_000_000
EXP2_SCALE = HD ** (-0.5) * math.log2(math.e)

f32 = jnp.float32
bf16 = jnp.bfloat16

SMEM = pl.BlockSpec(memory_space=pltpu.SMEM)
VMEM = pl.BlockSpec(memory_space=pltpu.VMEM)


def call(body, outs, ins, specs, scratch=(), flops=1):
    return pl.pallas_call(
        body,
        out_shape=outs,
        in_specs=specs,
        out_specs=[VMEM] * len(outs),
        scratch_shapes=list(scratch),
        compiler_params=pltpu.CompilerParams(vmem_limit_bytes=(16 if body in SMALL else 60) * 1024 * 1024),
        cost_estimate=pl.CostEstimate(flops=flops, bytes_accessed=1, transcendentals=0),
    )(*ins)


def cols(h):
    return slice(h * HD, (h + 1) * HD)


def dot(a, b, dims):
    return lax.dot_general(a, b, (dims, ((), ())), preferred_element_type=f32)


def exact_dot(a, b, dims):
    return lax.dot_general(
        a, b, (dims, ((), ())), precision=lax.Precision.HIGHEST, preferred_element_type=f32
    )


def block_state(rate, k, v, h, b):
    rows = slice(b * BLK, (b + 1) * BLK)
    back = (BLK - 1.0) - lax.broadcasted_iota(jnp.int32, (BLK, HD), 0).astype(f32)
    decayed = (k[rows, cols(h)].astype(f32) * jnp.exp(-rate * back)).astype(bf16)
    return dot(decayed, v[rows, cols(h)], ((0,), (0,)))


def start_body(
    index, docs, doc_row, rate_hbm, mask, k_hbm, v_hbm, sq, sk, sv, first, out, sent, own, rate, k, v, packed, rate_sem, sems
):
    other = 1 - index[0] % 2
    copies = [pltpu.make_async_copy(rate_hbm, rate, rate_sem)]
    for g in range(LOCAL // 2):
        at = slice(g * 2 * HD, (g + 1) * 2 * HD)
        copies.append(pltpu.make_async_copy(k_hbm.at[:, at], k.at[:, at], sems.at[2 * g]))
        copies.append(pltpu.make_async_copy(v_hbm.at[:, at], v.at[:, at], sems.at[2 * g + 1]))
    for at, ref in enumerate((sq, sk, sv)):
        rows = slice(at * ROWS, (at + 1) * ROWS)
        copies.append(
            pltpu.make_async_copy(ref.at[:, half(other)], sent.at[rows, :], sems.at[LOCAL + at])
        )
    for copy in copies:
        copy.start()
    line = lax.broadcasted_iota(jnp.int32, (2, NBLK), 0)
    lane = lax.broadcasted_iota(jnp.int32, (2, NBLK), 1)
    query = 2 * index[0]
    document = jnp.where(line == 0, docs[query], docs[query + 1])
    reach = (doc_row[...] == document) & (lane < query + line) & (mask[...] == 1)
    flags = jnp.where(reach, 1.0, 0.0)
    flags = jnp.concatenate([flags, jnp.zeros((14, NBLK), f32)], axis=0)
    own[...] = flags
    flags = flags.astype(bf16)
    packed[...] = jnp.concatenate([flags] * 4, axis=1)
    copies.append(pltpu.make_async_copy(packed, sent.at[3 * ROWS :, :], sems.at[LOCAL + 3]))
    copies[-1].start()
    copies[0].wait()
    for g in range(LOCAL // 2):
        copies[2 * g + 1].wait()
        copies[2 * g + 2].wait()
        for h in (2 * g, 2 * g + 1):
            step = jnp.exp(jnp.full((HD, HD), -rate[h] * BLK, f32))
            early = block_state(rate[h], k, v, h, 0)
            first[cols(h), :] = early
            out[cols(h), :] = (step * early + block_state(rate[h], k, v, h, 1)).astype(bf16)
    for copy in copies[LOCAL + 1 :]:
        copy.wait()


def prefix_body(index, rate, parts, out):
    step = jnp.exp(jnp.full((16, HD), -rate[index[0] // 8] * ROWS, f32))
    state = jnp.zeros((16, HD), f32)
    for i in range(SHARDS):
        out[i] = state.astype(bf16)
        if i + 1 < SHARDS:
            state = step * state + parts[i].astype(f32)


def inner_body(rate, q, k, v, out, rates):
    row = lax.broadcasted_iota(jnp.int32, (ROWS, ROWS), 0)
    col = lax.broadcasted_iota(jnp.int32, (ROWS, ROWS), 1)
    gap = jnp.maximum(row - col, 0).astype(f32)
    inside = (row >= col) & ((row >= BLK) == (col >= BLK))
    for h in range(LOCAL):
        rates[h : h + 1, :] = jnp.full((1, HD), rate[h], f32)
        decay = jnp.where(inside, jnp.exp(-rate[h] * gap), 0.0)
        scores = dot(q[:, cols(h)], k[:, cols(h)], ((1,), (1,)))
        out[:, cols(h)] = dot((scores * decay).astype(bf16), v[:, cols(h)], ((1,), (0,)))


def carry_body(rates, inner, q, first, state, heads, squares):
    ahead = lax.broadcasted_iota(jnp.int32, (BLK, HD), 0).astype(f32) + 1.0
    totals = [jnp.zeros((BLK, HD), f32)] * 2
    for h in range(LOCAL):
        rate = rates[h : h + 1, :]
        decay = jnp.exp(-rate * ahead)
        entering = state[cols(h), :]
        middle = (jnp.exp(-rate * BLK) * entering.astype(f32) + first[cols(h), :]).astype(bf16)
        for b, block_start in enumerate((entering, middle)):
            rows = slice(b * BLK, (b + 1) * BLK)
            carried = dot(q[rows, cols(h)], block_start, ((1,), (0,)))
            value = inner[rows, cols(h)] + carried * decay
            heads[rows, cols(h)] = value
            totals[b] = totals[b] + value * value
    total = jnp.concatenate(totals, axis=0)
    squares[...] = exact_dot(jnp.ones((8, HD), f32), total, ((1,), (1,)))


def norm_body(heads, gate, gain, s0, s1, s2, s3, out):
    total = s0[...] + s1[...] + s2[...] + s3[...]
    first = (lax.broadcasted_iota(jnp.int32, (8, HD), 0) == 0).astype(f32)
    spread = exact_dot(total, first, ((0,), (0,)))
    inverse = lax.rsqrt(spread / D + 1e-06)
    for h in range(LOCAL):
        scale = gain[:, cols(h)] * jax.nn.sigmoid(gate[:, cols(h)].astype(f32))
        out[:, cols(h)] = (heads[:, cols(h)] * inverse * scale).astype(bf16)


def half(c):
    return pl.ds(pl.multiple_of(c * HALF, HALF), HALF)


def gather_body(index, flags_own, q, k, v, other, far_q, head, tail, theirs, packed, sems):
    core = index[0] % 2

    def put(source, target, at):
        return pltpu.make_async_copy(source, target, sems.at[at])

    def layout(mine):
        def part(at, ref, owner, rows):
            if owner == mine:
                return ref.at[rows, half(core)]
            return other.at[slice(at * ROWS + rows.start, at * ROWS + rows.stop), :]

        low, high, whole = slice(0, BLK), slice(BLK, ROWS), slice(0, ROWS)
        copies = [
            put(part(0, q, 0, whole), far_q.at[:ROWS, :], 0),
            put(part(0, q, 1, whole), far_q.at[ROWS : 2 * ROWS, :], 1),
        ]
        for at, ref in ((1, k), (2, v)):
            base = (at - 1) * 3 * BLK
            sem = 3 * at - 1
            copies += [
                put(part(at, ref, 0, low), head.at[(at - 1) * BLK : at * BLK, :], sem),
                put(part(at, ref, 0, high), tail.at[base : base + BLK, :], sem + 1),
                put(part(at, ref, 1, whole), tail.at[base + BLK : base + 3 * BLK, :], sem + 2),
            ]
        return copies

    for mine in range(2):

        @pl.when(core == mine)
        def _():
            for copy in layout(mine):
                copy.start()

    fetch = put(other.at[3 * ROWS :, :NBLK], theirs, 8)
    fetch.start()
    fetch.wait()
    own = flags_own[:2, :]
    arrived = theirs[...].astype(f32)[:2]
    first = jnp.where(core == 0, own, arrived)
    second = jnp.where(core == 0, arrived, own)
    rows = jnp.concatenate([first, second, jnp.zeros((12, NBLK), f32)], axis=0)
    packed[...] = jnp.concatenate([rows.astype(bf16)] * 4, axis=1)
    flags = put(packed, far_q.at[4 * BLK :, :], 9)
    flags.start()
    for mine in range(2):

        @pl.when(core == mine)
        def _():
            for copy in layout(mine):
                copy.wait()

    flags.wait()


def allowed(flags, i, key):
    lane = lax.broadcasted_iota(jnp.int32, (1, NBLK), 1)
    ok = jnp.sum(jnp.where(lane == key, flags[i : i + 1, :], 0.0), axis=1, keepdims=True)
    return jnp.broadcast_to(jnp.where(ok > 0.5, 0.0, FILL), (BLK, BLK))


def block(i):
    return slice(i * BLK, (i + 1) * BLK)


def attend_head(q, keys, values, bias):
    scores = dot(q, keys, ((1,), (1,))) + bias
    top = jnp.max(scores, axis=1, keepdims=True)
    weights = jnp.exp2((scores - top) * EXP2_SCALE).astype(bf16)
    ones = jnp.ones(values.shape, bf16)
    both = dot(weights, jnp.concatenate([values, ones], axis=1), ((1,), (0,)))
    return both[:, :HD], top, both[:, HD:]


def attend_chip(index, ahead, q, head, tail, out, tops, sums, bias):
    chip = index[0] // 2
    rows = q[4 * BLK :, :NBLK].astype(f32)
    for i in range(4):
        for j in range(4):
            if ahead == 0 and j == i:
                row = lax.broadcasted_iota(jnp.int32, (BLK, BLK), 0)
                col = lax.broadcasted_iota(jnp.int32, (BLK, BLK), 1)
                bias[block(i), block(j)] = jnp.where(col <= row, 0.0, FILL)
            elif ahead == 0 and j > i:
                bias[block(i), block(j)] = jnp.full((BLK, BLK), FILL, f32)
            else:
                bias[block(i), block(j)] = allowed(rows, i, 4 * chip + j)
    lane = lax.broadcasted_iota(jnp.int32, (2 * BLK, HD), 1)
    for r in range(2):
        part = slice(r * 2 * BLK, (r + 1) * 2 * BLK)
        count = 4 * BLK if ahead or r else 2 * BLK
        top_table = jnp.zeros((2 * BLK, HD), f32)
        sum_table = jnp.zeros((2 * BLK, HD), f32)
        for h in range(HEADS):
            acc, top, total = attend_head(
                q[part, cols(h)],
                jnp.concatenate([head[:BLK, cols(h)], tail[: count - BLK, cols(h)]], axis=0),
                jnp.concatenate(
                    [head[BLK:, cols(h)], tail[3 * BLK : 2 * BLK + count, cols(h)]], axis=0
                ),
                bias[part, :count],
            )
            out[part, cols(h)] = acc / total
            top_table = jnp.where(lane == h, top, top_table)
            sum_table = jnp.where(lane == h, total, sum_table)
        tops[part, :] = top_table
        sums[part, :] = sum_table


def near_body(index, q, head, tail, out, tops, sums, bias):
    attend_chip(index, 0, q, head, tail, out, tops, sums, bias)


def next_body(index, q, head, tail, out, tops, sums, bias):
    attend_chip(index, 1, q, head, tail, out, tops, sums, bias)


def weighed(top1, sum1, top2, sum2):
    top = jnp.maximum(top1, top2)
    part1 = jnp.exp2((top1 - top) * EXP2_SCALE) * sum1
    part2 = jnp.exp2((top2 - top) * EXP2_SCALE) * sum2
    return top, part1 + part2, part2 / (part1 + part2)


def far_body(index, q, tail, done, tops, sums, out, bias):
    chip = index[0] // 2
    flags = q[4 * BLK :, :NBLK].astype(f32)
    for i in range(3):
        for j in range(3):
            bias[block(i), block(j)] = allowed(flags, i, 4 * (chip - 1) + 1 + j)
    rows = slice(0, 3 * BLK)
    rest = slice(3 * BLK, 4 * BLK)
    lane = lax.broadcasted_iota(jnp.int32, (3 * BLK, HD), 1)
    top_table = jnp.zeros((3 * BLK, HD), f32)
    sum_table = jnp.ones((3 * BLK, HD), f32)
    for h in range(HEADS):
        acc, top, total = attend_head(
            q[rows, cols(h)], tail[rows, cols(h)], tail[3 * BLK :, cols(h)], bias[...]
        )
        top_table = jnp.where(lane == h, top, top_table)
        sum_table = jnp.where(lane == h, total, sum_table)
        top1 = tops[rows, h : h + 1]
        _, _, share = weighed(top1, sums[rows, h : h + 1], top, total)
        here = done[rows, cols(h)]
        out[rows, cols(h)] = (here + (acc / total - here) * share).astype(bf16)
        out[rest, cols(h)] = done[rest, cols(h)].astype(bf16)
    top, total, _ = weighed(tops[rows, :], jnp.where(lane < HEADS, sums[rows, :], 1.0), top_table, sum_table)
    top = jnp.concatenate([top, tops[rest, :]], axis=0)
    total = jnp.concatenate([total, sums[rest, :]], axis=0)
    filler = jnp.zeros((LOCAL, 4 * BLK), f32)
    left = jnp.concatenate([top.T[:HEADS], total.T[:HEADS], filler], axis=0)
    for piece in range(3):
        part = left.astype(bf16)
        at = 4 * BLK + piece * 2 * LOCAL
        out[at : at + 2 * LOCAL, :] = part
        left = left - part.astype(f32)


def merge_body(index, near, tops, sums, far, mine, send, share):
    stats = jnp.zeros((2 * LOCAL, HALF), f32)
    for p in range(3):
        at = 4 * BLK + p * 2 * LOCAL
        stats = stats + far[at : at + 2 * LOCAL, :].astype(f32)
    pad = jnp.ones((HD - HEADS, 4 * BLK), f32)
    far_sums = jnp.concatenate([stats[HEADS : 2 * HEADS], pad], axis=0).T
    far_tops = jnp.concatenate([stats[:HEADS], pad], axis=0).T
    far_tops = jnp.where(far_sums > 0.0, far_tops, FILL)
    far_sums = jnp.where(far_sums > 0.0, far_sums, 1.0)
    lane = lax.broadcasted_iota(jnp.int32, (4 * BLK, HD), 1)
    near_sums = jnp.where(lane < HEADS, sums[...], 1.0)
    share[...] = weighed(tops[...], near_sums, far_tops, far_sums)[2]
    core = index[0] % 2
    for out, which in ((send, 1 - core), (mine, core)):
        rows = pl.ds(pl.multiple_of(which * ROWS, ROWS), ROWS)
        part = share[rows, :]
        for h in range(HEADS):
            own = near[rows, cols(h)]
            there = far[rows, cols(h)].astype(f32)
            out[:, cols(h)] = (own + (there - own) * part[:, h : h + 1]).astype(bf16)


def place_body(index, mine, other, out):
    core = index[0] % 2
    out[:, half(core)] = mine[...]
    out[:, half(1 - core)] = other[...]


SMALL = (gather_body, near_body, prefix_body, next_body, far_body, merge_body, norm_body, place_body)


def shifted(x, distance):
    return lax.ppermute(x, "seq", [(i, i + distance) for i in range(SHARDS) if 0 <= i + distance < SHARDS])


def swapped(x):
    return lax.ppermute(x, "seq", [(i, i ^ 1) for i in range(SHARDS)])


def turned(x, distance):
    return lax.ppermute(x, "head", [(i, (i + distance) % 4) for i in range(4)])


def per_device(
    lin_query,
    lin_key,
    lin_value,
    out_gate,
    norm_gain,
    decay_rate,
    soft_query,
    soft_key,
    soft_value,
    doc_ids,
    block_mask,
):
    like = jax.ShapeDtypeStruct
    index = lax.axis_index("seq").astype(jnp.int32).reshape(1)
    wide = like((ROWS, WIDTH), f32)
    narrow = like((ROWS, WIDTH), bf16)

    anywhere = pl.BlockSpec(memory_space=pl.ANY)
    first, state, sent, own_flags = call(
        start_body,
        [like((WIDTH, HD), f32), like((WIDTH, HD), bf16), like((3 * ROWS + 16, HALF), bf16), like((16, NBLK), f32)],
        (
            index, doc_ids, doc_ids.reshape(1, NBLK), decay_rate, block_mask,
            lin_key, lin_value, soft_query, soft_key, soft_value,
        ),
        [SMEM, SMEM, VMEM, anywhere, VMEM] + [anywhere] * 5,
        [
            pltpu.SMEM((LOCAL,), f32),
            pltpu.VMEM((ROWS, WIDTH), bf16),
            pltpu.VMEM((ROWS, WIDTH), bf16),
            pltpu.VMEM((16, HALF), bf16),
            pltpu.SemaphoreType.DMA,
            pltpu.SemaphoreType.DMA((LOCAL + 4,)),
        ],
    )
    other = swapped(sent)
    parts = lax.all_to_all(state.reshape(SHARDS, 16, HD), "seq", 0, 0)
    far_q, own_head, own_tail = call(
        gather_body,
        [
            like((2 * ROWS + 16, HALF), bf16),
            like((2 * BLK, HALF), bf16),
            like((6 * BLK, HALF), bf16),
        ],
        (index, own_flags, soft_query, soft_key, soft_value, other),
        [SMEM, VMEM] + [anywhere] * 4,
        [
            pltpu.VMEM((16, NBLK), bf16),
            pltpu.VMEM((16, HALF), bf16),
            pltpu.SemaphoreType.DMA((10,)),
        ],
    )
    tail = shifted(own_tail, 2)
    next_q = shifted(far_q, -2)

    (prefix,) = call(
        prefix_body,
        [like((SHARDS, 16, HD), bf16)],
        (index, decay_rate, parts),
        [SMEM, SMEM, VMEM],
        flops=PREFIX_COST,
    )
    prefix, own_head = lax.optimization_barrier((prefix, own_head))
    entering = lax.all_to_all(prefix, "seq", 0, 0).reshape(WIDTH, HD)
    tables = [like((4 * BLK, HALF), f32), like((4 * BLK, HD), f32), like((4 * BLK, HD), f32)]
    done, done_tops, done_sums = call(
        next_body,
        tables,
        (index, next_q, own_head, own_tail),
        [SMEM] + [VMEM] * 3,
        [pltpu.VMEM((4 * BLK, 4 * BLK), f32)],
    )
    (far,) = call(
        far_body,
        [like((4 * BLK + 48, HALF), bf16)],
        (index, next_q, tail, done, done_tops, done_sums),
        [SMEM] + [VMEM] * 5,
        [pltpu.VMEM((3 * BLK, 3 * BLK), f32)],
    )
    far, lin_query = lax.optimization_barrier((far, lin_query))
    far = shifted(far, 2)
    inner, rates = call(
        inner_body,
        [wide, like((LOCAL, HD), f32)],
        (decay_rate, lin_query, lin_key, lin_value),
        [SMEM] + [VMEM] * 3,
    )
    heads, squares = call(
        carry_body,
        [wide, like((8, ROWS), f32)],
        (rates, inner, lin_query, first, entering),
        [VMEM] * 5,
        flops=CARRY_COST,
    )
    heads, own_head = lax.optimization_barrier((heads, own_head))
    others = [turned(squares, d) for d in (1, 2, 3)]
    near, tops, sums = call(
        near_body,
        tables,
        (index, far_q, own_head, own_tail),
        [SMEM] + [VMEM] * 3,
        [pltpu.VMEM((4 * BLK, 4 * BLK), f32)],
    )
    far, heads = lax.optimization_barrier((far, heads))
    mine, send = call(
        merge_body,
        [like((ROWS, HALF), bf16)] * 2,
        (index, near, tops, sums, far),
        [SMEM] + [VMEM] * 4,
        [pltpu.VMEM((4 * BLK, HD), f32)],
    )
    send, *others = lax.optimization_barrier((send, *others))
    (lin_output,) = call(
        norm_body,
        [narrow],
        (heads, out_gate, norm_gain.reshape(1, WIDTH), squares, *others),
        [VMEM] * 7,
    )

    (soft_output,) = call(
        place_body, [narrow], (index, mine, swapped(send)), [SMEM, VMEM, VMEM]
    )
    return (lin_output, soft_output)


def solution(mesh):
    rows = P("seq", "head")
    return jax.shard_map(
        per_device,
        mesh=mesh,
        in_specs=(
            rows, rows, rows, rows, P("head"), P("head"), rows, rows, rows, P(), P("seq", None),
        ),
        out_specs=(rows, rows),
        check_vma=False,
    )
```

```python
import math

import jax
import jax.numpy as jnp
from jax import lax
from jax.experimental import pallas as pl
from jax.experimental.pallas import tpu as pltpu
from jax.sharding import PartitionSpec as P

HD = 128
BLK = 128
NBLK = 128
ROWS = 256
LOCAL = 8
WIDTH = LOCAL * HD
HALF = WIDTH // 2
HEADS = LOCAL // 2
D = 4096
SHARDS = 64
FILL = -1e30
PREFIX_COST = 1_500_000_000
CARRY_COST = 10_000_000_000
EXP2_SCALE = HD ** (-0.5) * math.log2(math.e)

f32 = jnp.float32
bf16 = jnp.bfloat16

SMEM = pl.BlockSpec(memory_space=pltpu.SMEM)
VMEM = pl.BlockSpec(memory_space=pltpu.VMEM)


def call(body, outs, ins, specs, scratch=(), flops=1):
    return pl.pallas_call(
        body,
        out_shape=outs,
        in_specs=specs,
        out_specs=[VMEM] * len(outs),
        scratch_shapes=list(scratch),
        compiler_params=pltpu.CompilerParams(vmem_limit_bytes=(16 if body in SMALL else 60) * 1024 * 1024),
        cost_estimate=pl.CostEstimate(flops=flops, bytes_accessed=1, transcendentals=0),
    )(*ins)


def cols(h):
    return slice(h * HD, (h + 1) * HD)


def dot(a, b, dims):
    return lax.dot_general(a, b, (dims, ((), ())), preferred_element_type=f32)


def exact_dot(a, b, dims):
    return lax.dot_general(
        a, b, (dims, ((), ())), precision=lax.Precision.HIGHEST, preferred_element_type=f32
    )


def block_state(rate, k, v, h, b):
    rows = slice(b * BLK, (b + 1) * BLK)
    back = (BLK - 1.0) - lax.broadcasted_iota(jnp.int32, (BLK, HD), 0).astype(f32)
    decayed = (k[rows, cols(h)].astype(f32) * jnp.exp(-rate * back)).astype(bf16)
    return dot(decayed, v[rows, cols(h)], ((0,), (0,)))


def start_body(
    index, docs, doc_row, rate_hbm, mask, k_hbm, v_hbm, sq, sk, sv, first, out, sent, rate, k, v, packed, rate_sem, sems
):
    other = 1 - index[0] % 2
    copies = [pltpu.make_async_copy(rate_hbm, rate, rate_sem)]
    for g in range(LOCAL // 2):
        at = slice(g * 2 * HD, (g + 1) * 2 * HD)
        copies.append(pltpu.make_async_copy(k_hbm.at[:, at], k.at[:, at], sems.at[2 * g]))
        copies.append(pltpu.make_async_copy(v_hbm.at[:, at], v.at[:, at], sems.at[2 * g + 1]))
    for at, ref in enumerate((sq, sk, sv)):
        rows = slice(at * ROWS, (at + 1) * ROWS)
        copies.append(
            pltpu.make_async_copy(ref.at[:, half(other)], sent.at[rows, :], sems.at[LOCAL + at])
        )
    for copy in copies:
        copy.start()
    line = lax.broadcasted_iota(jnp.int32, (2, NBLK), 0)
    lane = lax.broadcasted_iota(jnp.int32, (2, NBLK), 1)
    query = 2 * index[0]
    document = jnp.where(line == 0, docs[query], docs[query + 1])
    reach = (doc_row[...] == document) & (lane < query + line) & (mask[...] == 1)
    flags = jnp.where(reach, 1.0, 0.0)
    flags = jnp.concatenate([flags, jnp.zeros((14, NBLK), f32)], axis=0)
    flags = flags.astype(bf16)
    packed[...] = jnp.concatenate([flags] * 4, axis=1)
    copies.append(pltpu.make_async_copy(packed, sent.at[3 * ROWS :, :], sems.at[LOCAL + 3]))
    copies[-1].start()
    copies[0].wait()
    for g in range(LOCAL // 2):
        copies[2 * g + 1].wait()
        copies[2 * g + 2].wait()
        for h in (2 * g, 2 * g + 1):
            step = jnp.exp(jnp.full((HD, HD), -rate[h] * BLK, f32))
            early = block_state(rate[h], k, v, h, 0)
            first[cols(h), :] = early
            out[cols(h), :] = (step * early + block_state(rate[h], k, v, h, 1)).astype(bf16)
    for copy in copies[LOCAL + 1 :]:
        copy.wait()


def prefix_body(index, rate, parts, out):
    step = jnp.exp(jnp.full((16, HD), -rate[index[0] // 8] * ROWS, f32))
    state = jnp.zeros((16, HD), f32)
    for i in range(SHARDS):
        out[i] = state.astype(bf16)
        if i + 1 < SHARDS:
            state = step * state + parts[i].astype(f32)


def inner_body(rate, q, k, v, out, rates):
    row = lax.broadcasted_iota(jnp.int32, (ROWS, ROWS), 0)
    col = lax.broadcasted_iota(jnp.int32, (ROWS, ROWS), 1)
    gap = jnp.maximum(row - col, 0).astype(f32)
    inside = (row >= col) & ((row >= BLK) == (col >= BLK))
    for h in range(LOCAL):
        rates[h : h + 1, :] = jnp.full((1, HD), rate[h], f32)
        decay = jnp.where(inside, jnp.exp(-rate[h] * gap), 0.0)
        scores = dot(q[:, cols(h)], k[:, cols(h)], ((1,), (1,)))
        out[:, cols(h)] = dot((scores * decay).astype(bf16), v[:, cols(h)], ((1,), (0,)))


def carry_body(rates, inner, q, first, state, heads, squares):
    ahead = lax.broadcasted_iota(jnp.int32, (BLK, HD), 0).astype(f32) + 1.0
    totals = [jnp.zeros((BLK, HD), f32)] * 2
    for h in range(LOCAL):
        rate = rates[h : h + 1, :]
        decay = jnp.exp(-rate * ahead)
        entering = state[cols(h), :]
        middle = (jnp.exp(-rate * BLK) * entering.astype(f32) + first[cols(h), :]).astype(bf16)
        for b, block_start in enumerate((entering, middle)):
            rows = slice(b * BLK, (b + 1) * BLK)
            carried = dot(q[rows, cols(h)], block_start, ((1,), (0,)))
            value = inner[rows, cols(h)] + carried * decay
            heads[rows, cols(h)] = value
            totals[b] = totals[b] + value * value
    total = jnp.concatenate(totals, axis=0)
    squares[...] = exact_dot(jnp.ones((8, HD), f32), total, ((1,), (1,)))


def norm_body(heads, gate, gain, s0, s1, s2, s3, out):
    total = s0[...] + s1[...] + s2[...] + s3[...]
    first = (lax.broadcasted_iota(jnp.int32, (8, HD), 0) == 0).astype(f32)
    spread = exact_dot(total, first, ((0,), (0,)))
    inverse = lax.rsqrt(spread / D + 1e-06)
    for h in range(LOCAL):
        scale = gain[:, cols(h)] * jax.nn.sigmoid(gate[:, cols(h)].astype(f32))
        out[:, cols(h)] = (heads[:, cols(h)] * inverse * scale).astype(bf16)


def half(c):
    return pl.ds(pl.multiple_of(c * HALF, HALF), HALF)


def gather_body(index, sent, q, k, v, other, far_q, head, tail, ours, theirs, packed, sems):
    core = index[0] % 2

    def put(source, target, at):
        return pltpu.make_async_copy(source, target, sems.at[at])

    def layout(mine):
        def part(at, ref, owner, rows):
            if owner == mine:
                return ref.at[rows, half(core)]
            return other.at[slice(at * ROWS + rows.start, at * ROWS + rows.stop), :]

        low, high, whole = slice(0, BLK), slice(BLK, ROWS), slice(0, ROWS)
        copies = [
            put(part(0, q, 0, whole), far_q.at[:ROWS, :], 0),
            put(part(0, q, 1, whole), far_q.at[ROWS : 2 * ROWS, :], 1),
        ]
        for at, ref in ((1, k), (2, v)):
            base = (at - 1) * 3 * BLK
            sem = 3 * at - 1
            copies += [
                put(part(at, ref, 0, low), head.at[(at - 1) * BLK : at * BLK, :], sem),
                put(part(at, ref, 0, high), tail.at[base : base + BLK, :], sem + 1),
                put(part(at, ref, 1, whole), tail.at[base + BLK : base + 3 * BLK, :], sem + 2),
            ]
        return copies

    for mine in range(2):

        @pl.when(core == mine)
        def _():
            for copy in layout(mine):
                copy.start()

    fetch = put(other.at[3 * ROWS :, :NBLK], theirs, 8)
    fetch.start()
    fetch_own = put(sent.at[3 * ROWS :, :NBLK], ours, 10)
    fetch_own.start()
    fetch.wait()
    fetch_own.wait()
    own = ours[...].astype(f32)[:2]
    arrived = theirs[...].astype(f32)[:2]
    first = jnp.where(core == 0, own, arrived)
    second = jnp.where(core == 0, arrived, own)
    rows = jnp.concatenate([first, second, jnp.zeros((12, NBLK), f32)], axis=0)
    packed[...] = jnp.concatenate([rows.astype(bf16)] * 4, axis=1)
    flags = put(packed, far_q.at[4 * BLK :, :], 9)
    flags.start()
    for mine in range(2):

        @pl.when(core == mine)
        def _():
            for copy in layout(mine):
                copy.wait()

    flags.wait()


def allowed(flags, i, key):
    lane = lax.broadcasted_iota(jnp.int32, (1, NBLK), 1)
    ok = jnp.sum(jnp.where(lane == key, flags[i : i + 1, :], 0.0), axis=1, keepdims=True)
    return jnp.broadcast_to(jnp.where(ok > 0.5, 0.0, FILL), (BLK, BLK))


def block(i):
    return slice(i * BLK, (i + 1) * BLK)


def attend_head(q, keys, values, bias):
    scores = dot(q, keys, ((1,), (1,))) + bias
    top = jnp.max(scores, axis=1, keepdims=True)
    weights = jnp.exp2((scores - top) * EXP2_SCALE).astype(bf16)
    ones = jnp.ones(values.shape, bf16)
    both = dot(weights, jnp.concatenate([values, ones], axis=1), ((1,), (0,)))
    return both[:, :HD], top, both[:, HD:]


def attend_chip(index, ahead, q, head, tail, out, tops, sums, bias):
    chip = index[0] // 2
    rows = q[4 * BLK :, :NBLK].astype(f32)
    for i in range(4):
        for j in range(4):
            if ahead == 0 and j == i:
                row = lax.broadcasted_iota(jnp.int32, (BLK, BLK), 0)
                col = lax.broadcasted_iota(jnp.int32, (BLK, BLK), 1)
                bias[block(i), block(j)] = jnp.where(col <= row, 0.0, FILL)
            elif ahead == 0 and j > i:
                bias[block(i), block(j)] = jnp.full((BLK, BLK), FILL, f32)
            else:
                bias[block(i), block(j)] = allowed(rows, i, 4 * chip + j)
    lane = lax.broadcasted_iota(jnp.int32, (2 * BLK, HD), 1)
    for r in range(2):
        part = slice(r * 2 * BLK, (r + 1) * 2 * BLK)
        count = 4 * BLK if ahead or r else 2 * BLK
        top_table = jnp.zeros((2 * BLK, HD), f32)
        sum_table = jnp.zeros((2 * BLK, HD), f32)
        for h in range(HEADS):
            acc, top, total = attend_head(
                q[part, cols(h)],
                jnp.concatenate([head[:BLK, cols(h)], tail[: count - BLK, cols(h)]], axis=0),
                jnp.concatenate(
                    [head[BLK:, cols(h)], tail[3 * BLK : 2 * BLK + count, cols(h)]], axis=0
                ),
                bias[part, :count],
            )
            out[part, cols(h)] = acc / total
            top_table = jnp.where(lane == h, top, top_table)
            sum_table = jnp.where(lane == h, total, sum_table)
        tops[part, :] = top_table
        sums[part, :] = sum_table


def near_body(index, q, head, tail, out, tops, sums, bias):
    attend_chip(index, 0, q, head, tail, out, tops, sums, bias)


def next_body(index, q, head, tail, out, tops, sums, bias):
    attend_chip(index, 1, q, head, tail, out, tops, sums, bias)


def weighed(top1, sum1, top2, sum2):
    top = jnp.maximum(top1, top2)
    part1 = jnp.exp2((top1 - top) * EXP2_SCALE) * sum1
    part2 = jnp.exp2((top2 - top) * EXP2_SCALE) * sum2
    return top, part1 + part2, part2 / (part1 + part2)


def far_body(index, q, tail, done, tops, sums, out, bias):
    chip = index[0] // 2
    flags = q[4 * BLK :, :NBLK].astype(f32)
    for i in range(3):
        for j in range(3):
            bias[block(i), block(j)] = allowed(flags, i, 4 * (chip - 1) + 1 + j)
    rows = slice(0, 3 * BLK)
    rest = slice(3 * BLK, 4 * BLK)
    lane = lax.broadcasted_iota(jnp.int32, (3 * BLK, HD), 1)
    top_table = jnp.zeros((3 * BLK, HD), f32)
    sum_table = jnp.ones((3 * BLK, HD), f32)
    for h in range(HEADS):
        acc, top, total = attend_head(
            q[rows, cols(h)], tail[rows, cols(h)], tail[3 * BLK :, cols(h)], bias[...]
        )
        top_table = jnp.where(lane == h, top, top_table)
        sum_table = jnp.where(lane == h, total, sum_table)
        top1 = tops[rows, h : h + 1]
        _, _, share = weighed(top1, sums[rows, h : h + 1], top, total)
        here = done[rows, cols(h)]
        out[rows, cols(h)] = (here + (acc / total - here) * share).astype(bf16)
        out[rest, cols(h)] = done[rest, cols(h)].astype(bf16)
    top, total, _ = weighed(tops[rows, :], jnp.where(lane < HEADS, sums[rows, :], 1.0), top_table, sum_table)
    top = jnp.concatenate([top, tops[rest, :]], axis=0)
    total = jnp.concatenate([total, sums[rest, :]], axis=0)
    filler = jnp.zeros((LOCAL, 4 * BLK), f32)
    left = jnp.concatenate([top.T[:HEADS], total.T[:HEADS], filler], axis=0)
    for piece in range(3):
        part = left.astype(bf16)
        at = 4 * BLK + piece * 2 * LOCAL
        out[at : at + 2 * LOCAL, :] = part
        left = left - part.astype(f32)


def merge_body(index, near, tops, sums, far, mine, send, share):
    stats = jnp.zeros((2 * LOCAL, HALF), f32)
    for p in range(3):
        at = 4 * BLK + p * 2 * LOCAL
        stats = stats + far[at : at + 2 * LOCAL, :].astype(f32)
    pad = jnp.ones((HD - HEADS, 4 * BLK), f32)
    far_sums = jnp.concatenate([stats[HEADS : 2 * HEADS], pad], axis=0).T
    far_tops = jnp.concatenate([stats[:HEADS], pad], axis=0).T
    far_tops = jnp.where(far_sums > 0.0, far_tops, FILL)
    far_sums = jnp.where(far_sums > 0.0, far_sums, 1.0)
    lane = lax.broadcasted_iota(jnp.int32, (4 * BLK, HD), 1)
    near_sums = jnp.where(lane < HEADS, sums[...], 1.0)
    share[...] = weighed(tops[...], near_sums, far_tops, far_sums)[2]
    core = index[0] % 2
    for out, which in ((send, 1 - core), (mine, core)):
        rows = pl.ds(pl.multiple_of(which * ROWS, ROWS), ROWS)
        part = share[rows, :]
        for h in range(HEADS):
            own = near[rows, cols(h)]
            there = far[rows, cols(h)].astype(f32)
            out[:, cols(h)] = (own + (there - own) * part[:, h : h + 1]).astype(bf16)


def place_body(index, mine, other, out):
    core = index[0] % 2
    out[:, half(core)] = mine[...]
    out[:, half(1 - core)] = other[...]


SMALL = (gather_body, near_body, prefix_body, next_body, far_body, merge_body, norm_body, place_body)


def shifted(x, distance):
    return lax.ppermute(x, "seq", [(i, i + distance) for i in range(SHARDS) if 0 <= i + distance < SHARDS])


def swapped(x):
    return lax.ppermute(x, "seq", [(i, i ^ 1) for i in range(SHARDS)])


def turned(x, distance):
    return lax.ppermute(x, "head", [(i, (i + distance) % 4) for i in range(4)])


def per_device(
    lin_query,
    lin_key,
    lin_value,
    out_gate,
    norm_gain,
    decay_rate,
    soft_query,
    soft_key,
    soft_value,
    doc_ids,
    block_mask,
):
    like = jax.ShapeDtypeStruct
    index = lax.axis_index("seq").astype(jnp.int32).reshape(1)
    wide = like((ROWS, WIDTH), f32)
    narrow = like((ROWS, WIDTH), bf16)

    anywhere = pl.BlockSpec(memory_space=pl.ANY)
    first, state, sent = call(
        start_body,
        [like((WIDTH, HD), f32), like((WIDTH, HD), bf16), like((3 * ROWS + 16, HALF), bf16)],
        (
            index, doc_ids, doc_ids.reshape(1, NBLK), decay_rate, block_mask,
            lin_key, lin_value, soft_query, soft_key, soft_value,
        ),
        [SMEM, SMEM, VMEM, anywhere, VMEM] + [anywhere] * 5,
        [
            pltpu.SMEM((LOCAL,), f32),
            pltpu.VMEM((ROWS, WIDTH), bf16),
            pltpu.VMEM((ROWS, WIDTH), bf16),
            pltpu.VMEM((16, HALF), bf16),
            pltpu.SemaphoreType.DMA,
            pltpu.SemaphoreType.DMA((LOCAL + 4,)),
        ],
    )
    other = swapped(sent)
    parts = lax.all_to_all(state.reshape(SHARDS, 16, HD), "seq", 0, 0)
    far_q, own_head, own_tail = call(
        gather_body,
        [
            like((2 * ROWS + 16, HALF), bf16),
            like((2 * BLK, HALF), bf16),
            like((6 * BLK, HALF), bf16),
        ],
        (index, sent, soft_query, soft_key, soft_value, other),
        [SMEM] + [anywhere] * 5,
        [
            pltpu.VMEM((16, NBLK), bf16),
            pltpu.VMEM((16, NBLK), bf16),
            pltpu.VMEM((16, HALF), bf16),
            pltpu.SemaphoreType.DMA((11,)),
        ],
    )
    tail = shifted(own_tail, 2)
    next_q = shifted(far_q, -2)

    (prefix,) = call(
        prefix_body,
        [like((SHARDS, 16, HD), bf16)],
        (index, decay_rate, parts),
        [SMEM, SMEM, VMEM],
        flops=PREFIX_COST,
    )
    prefix, own_head = lax.optimization_barrier((prefix, own_head))
    entering = lax.all_to_all(prefix, "seq", 0, 0).reshape(WIDTH, HD)
    tables = [like((4 * BLK, HALF), f32), like((4 * BLK, HD), f32), like((4 * BLK, HD), f32)]
    done, done_tops, done_sums = call(
        next_body,
        tables,
        (index, next_q, own_head, own_tail),
        [SMEM] + [VMEM] * 3,
        [pltpu.VMEM((4 * BLK, 4 * BLK), f32)],
    )
    (far,) = call(
        far_body,
        [like((4 * BLK + 48, HALF), bf16)],
        (index, next_q, tail, done, done_tops, done_sums),
        [SMEM] + [VMEM] * 5,
        [pltpu.VMEM((3 * BLK, 3 * BLK), f32)],
    )
    far, lin_query = lax.optimization_barrier((far, lin_query))
    far = shifted(far, 2)
    inner, rates = call(
        inner_body,
        [wide, like((LOCAL, HD), f32)],
        (decay_rate, lin_query, lin_key, lin_value),
        [SMEM] + [VMEM] * 3,
    )
    heads, squares = call(
        carry_body,
        [wide, like((8, ROWS), f32)],
        (rates, inner, lin_query, first, entering),
        [VMEM] * 5,
        flops=CARRY_COST,
    )
    heads, own_head = lax.optimization_barrier((heads, own_head))
    others = [turned(squares, d) for d in (1, 2, 3)]
    near, tops, sums = call(
        near_body,
        tables,
        (index, far_q, own_head, own_tail),
        [SMEM] + [VMEM] * 3,
        [pltpu.VMEM((4 * BLK, 4 * BLK), f32)],
    )
    far, heads = lax.optimization_barrier((far, heads))
    mine, send = call(
        merge_body,
        [like((ROWS, HALF), bf16)] * 2,
        (index, near, tops, sums, far),
        [SMEM] + [VMEM] * 4,
        [pltpu.VMEM((4 * BLK, HD), f32)],
    )
    send, *others = lax.optimization_barrier((send, *others))
    (lin_output,) = call(
        norm_body,
        [narrow],
        (heads, out_gate, norm_gain.reshape(1, WIDTH), squares, *others),
        [VMEM] * 7,
    )

    (soft_output,) = call(
        place_body, [narrow], (index, mine, swapped(send)), [SMEM, VMEM, VMEM]
    )
    return (lin_output, soft_output)


def solution(mesh):
    rows = P("seq", "head")
    return jax.shard_map(
        per_device,
        mesh=mesh,
        in_specs=(
            rows, rows, rows, rows, P("head"), P("head"), rows, rows, rows, P(), P("seq", None),
        ),
        out_specs=(rows, rows),
        check_vma=False,
    )
```

```python
import math

import jax
import jax.numpy as jnp
from jax import lax
from jax.experimental import pallas as pl
from jax.experimental.pallas import tpu as pltpu
from jax.sharding import PartitionSpec as P

HD = 128
BLK = 128
NBLK = 128
ROWS = 256
LOCAL = 8
WIDTH = LOCAL * HD
HALF = WIDTH // 2
HEADS = LOCAL // 2
D = 4096
SHARDS = 64
FILL = -1e30
PREFIX_COST = 1_500_000_000
CARRY_COST = 10_000_000_000
EXP2_SCALE = HD ** (-0.5) * math.log2(math.e)

f32 = jnp.float32
bf16 = jnp.bfloat16

SMEM = pl.BlockSpec(memory_space=pltpu.SMEM)
VMEM = pl.BlockSpec(memory_space=pltpu.VMEM)


def call(body, outs, ins, specs, scratch=(), flops=1):
    return pl.pallas_call(
        body,
        out_shape=outs,
        in_specs=specs,
        out_specs=[VMEM] * len(outs),
        scratch_shapes=list(scratch),
        compiler_params=pltpu.CompilerParams(vmem_limit_bytes=(16 if body in SMALL else 60) * 1024 * 1024),
        cost_estimate=pl.CostEstimate(flops=flops, bytes_accessed=1, transcendentals=0),
    )(*ins)


def cols(h):
    return slice(h * HD, (h + 1) * HD)


def dot(a, b, dims):
    return lax.dot_general(a, b, (dims, ((), ())), preferred_element_type=f32)


def exact_dot(a, b, dims):
    return lax.dot_general(
        a, b, (dims, ((), ())), precision=lax.Precision.HIGHEST, preferred_element_type=f32
    )


def block_state(rate, k, v, h, b):
    rows = slice(b * BLK, (b + 1) * BLK)
    back = (BLK - 1.0) - lax.broadcasted_iota(jnp.int32, (BLK, HD), 0).astype(f32)
    decayed = (k[rows, cols(h)].astype(f32) * jnp.exp(-rate * back)).astype(bf16)
    return dot(decayed, v[rows, cols(h)], ((0,), (0,)))


def start_body(
    index, docs, doc_row, rate_hbm, mask, k_hbm, v_hbm, sq, sk, sv, first, out, sent, rate, k, v, packed, rate_sem, sems
):
    other = 1 - index[0] % 2
    copies = [pltpu.make_async_copy(rate_hbm, rate, rate_sem)]
    for g in range(LOCAL // 2):
        at = slice(g * 2 * HD, (g + 1) * 2 * HD)
        copies.append(pltpu.make_async_copy(k_hbm.at[:, at], k.at[:, at], sems.at[2 * g]))
        copies.append(pltpu.make_async_copy(v_hbm.at[:, at], v.at[:, at], sems.at[2 * g + 1]))
    for at, ref in enumerate((sq, sk, sv)):
        rows = slice(at * ROWS, (at + 1) * ROWS)
        copies.append(
            pltpu.make_async_copy(ref.at[:, half(other)], sent.at[rows, :], sems.at[LOCAL + at])
        )
    for copy in copies:
        copy.start()
    line = lax.broadcasted_iota(jnp.int32, (2, NBLK), 0)
    lane = lax.broadcasted_iota(jnp.int32, (2, NBLK), 1)
    query = 2 * index[0]
    document = jnp.where(line == 0, docs[query], docs[query + 1])
    reach = (doc_row[...] == document) & (lane < query + line) & (mask[...] == 1)
    flags = jnp.where(reach, 1.0, 0.0)
    ids = doc_row[...].astype(f32)
    flags = jnp.concatenate([flags, ids, jnp.zeros((13, NBLK), f32)], axis=0).astype(bf16)
    packed[...] = jnp.concatenate([flags] * 4, axis=1)
    copies.append(pltpu.make_async_copy(packed, sent.at[3 * ROWS :, :], sems.at[LOCAL + 3]))
    copies[-1].start()
    copies[0].wait()
    for g in range(LOCAL // 2):
        copies[2 * g + 1].wait()
        copies[2 * g + 2].wait()
        for h in (2 * g, 2 * g + 1):
            step = jnp.exp(jnp.full((HD, HD), -rate[h] * BLK, f32))
            early = block_state(rate[h], k, v, h, 0)
            first[cols(h), :] = early
            out[cols(h), :] = (step * early + block_state(rate[h], k, v, h, 1)).astype(bf16)
    for copy in copies[LOCAL + 1 :]:
        copy.wait()


def prefix_body(index, rate, parts, out):
    step = jnp.exp(jnp.full((16, HD), -rate[index[0] // 8] * ROWS, f32))
    state = jnp.zeros((16, HD), f32)
    for i in range(SHARDS):
        out[i] = state.astype(bf16)
        if i + 1 < SHARDS:
            state = step * state + parts[i].astype(f32)


def inner_body(rate, q, k, v, out, rates):
    row = lax.broadcasted_iota(jnp.int32, (ROWS, ROWS), 0)
    col = lax.broadcasted_iota(jnp.int32, (ROWS, ROWS), 1)
    gap = jnp.maximum(row - col, 0).astype(f32)
    inside = (row >= col) & ((row >= BLK) == (col >= BLK))
    for h in range(LOCAL):
        rates[h : h + 1, :] = jnp.full((1, HD), rate[h], f32)
        decay = jnp.where(inside, jnp.exp(-rate[h] * gap), 0.0)
        scores = dot(q[:, cols(h)], k[:, cols(h)], ((1,), (1,)))
        out[:, cols(h)] = dot((scores * decay).astype(bf16), v[:, cols(h)], ((1,), (0,)))


def carry_body(rates, inner, q, first, state, heads, squares):
    ahead = lax.broadcasted_iota(jnp.int32, (BLK, HD), 0).astype(f32) + 1.0
    totals = [jnp.zeros((BLK, HD), f32)] * 2
    for h in range(LOCAL):
        rate = rates[h : h + 1, :]
        decay = jnp.exp(-rate * ahead)
        entering = state[cols(h), :]
        middle = (jnp.exp(-rate * BLK) * entering.astype(f32) + first[cols(h), :]).astype(bf16)
        for b, block_start in enumerate((entering, middle)):
            rows = slice(b * BLK, (b + 1) * BLK)
            carried = dot(q[rows, cols(h)], block_start, ((1,), (0,)))
            value = inner[rows, cols(h)] + carried * decay
            heads[rows, cols(h)] = value
            totals[b] = totals[b] + value * value
    total = jnp.concatenate(totals, axis=0)
    squares[...] = exact_dot(jnp.ones((8, HD), f32), total, ((1,), (1,)))


def norm_body(heads, gate, gain, s0, s1, s2, s3, out):
    total = s0[...] + s1[...] + s2[...] + s3[...]
    first = (lax.broadcasted_iota(jnp.int32, (8, HD), 0) == 0).astype(f32)
    spread = exact_dot(total, first, ((0,), (0,)))
    inverse = lax.rsqrt(spread / D + 1e-06)
    for h in range(LOCAL):
        scale = gain[:, cols(h)] * jax.nn.sigmoid(gate[:, cols(h)].astype(f32))
        out[:, cols(h)] = (heads[:, cols(h)] * inverse * scale).astype(bf16)


def half(c):
    return pl.ds(pl.multiple_of(c * HALF, HALF), HALF)


def gather_body(index, mask, q, k, v, other, far_q, head, tail, theirs, packed, sems):
    core = index[0] % 2

    def put(source, target, at):
        return pltpu.make_async_copy(source, target, sems.at[at])

    def layout(mine):
        def part(at, ref, owner, rows):
            if owner == mine:
                return ref.at[rows, half(core)]
            return other.at[slice(at * ROWS + rows.start, at * ROWS + rows.stop), :]

        low, high, whole = slice(0, BLK), slice(BLK, ROWS), slice(0, ROWS)
        copies = [
            put(part(0, q, 0, whole), far_q.at[:ROWS, :], 0),
            put(part(0, q, 1, whole), far_q.at[ROWS : 2 * ROWS, :], 1),
        ]
        for at, ref in ((1, k), (2, v)):
            base = (at - 1) * 3 * BLK
            sem = 3 * at - 1
            copies += [
                put(part(at, ref, 0, low), head.at[(at - 1) * BLK : at * BLK, :], sem),
                put(part(at, ref, 0, high), tail.at[base : base + BLK, :], sem + 1),
                put(part(at, ref, 1, whole), tail.at[base + BLK : base + 3 * BLK, :], sem + 2),
            ]
        return copies

    for mine in range(2):

        @pl.when(core == mine)
        def _():
            for copy in layout(mine):
                copy.start()

    fetch = put(other.at[3 * ROWS :, :NBLK], theirs, 8)
    fetch.start()
    fetch.wait()
    arrived = theirs[...].astype(f32)
    ids = arrived[2:3, :]
    line = lax.broadcasted_iota(jnp.int32, (2, NBLK), 0)
    lane = lax.broadcasted_iota(jnp.int32, (2, NBLK), 1)
    query = 2 * index[0] + line
    document = jnp.sum(jnp.where(lane == query, ids, 0.0), axis=1, keepdims=True)
    reach = (ids == document) & (lane < query) & (mask[...] == 1)
    own = jnp.where(reach, 1.0, 0.0)
    arrived = arrived[:2, :]
    first = jnp.where(core == 0, own, arrived)
    second = jnp.where(core == 0, arrived, own)
    rows = jnp.concatenate([first, second, jnp.zeros((12, NBLK), f32)], axis=0)
    packed[...] = jnp.concatenate([rows.astype(bf16)] * 4, axis=1)
    flags = put(packed, far_q.at[4 * BLK :, :], 9)
    flags.start()
    for mine in range(2):

        @pl.when(core == mine)
        def _():
            for copy in layout(mine):
                copy.wait()

    flags.wait()


def allowed(flags, i, key):
    lane = lax.broadcasted_iota(jnp.int32, (1, NBLK), 1)
    ok = jnp.sum(jnp.where(lane == key, flags[i : i + 1, :], 0.0), axis=1, keepdims=True)
    return jnp.broadcast_to(jnp.where(ok > 0.5, 0.0, FILL), (BLK, BLK))


def block(i):
    return slice(i * BLK, (i + 1) * BLK)


def attend_head(q, keys, values, bias):
    scores = dot(q, keys, ((1,), (1,))) + bias
    top = jnp.max(scores, axis=1, keepdims=True)
    weights = jnp.exp2((scores - top) * EXP2_SCALE).astype(bf16)
    ones = jnp.ones(values.shape, bf16)
    both = dot(weights, jnp.concatenate([values, ones], axis=1), ((1,), (0,)))
    return both[:, :HD], top, both[:, HD:]


def attend_chip(index, ahead, q, head, tail, out, tops, sums, bias):
    chip = index[0] // 2
    rows = q[4 * BLK :, :NBLK].astype(f32)
    for i in range(4):
        for j in range(4):
            if ahead == 0 and j == i:
                row = lax.broadcasted_iota(jnp.int32, (BLK, BLK), 0)
                col = lax.broadcasted_iota(jnp.int32, (BLK, BLK), 1)
                bias[block(i), block(j)] = jnp.where(col <= row, 0.0, FILL)
            elif ahead == 0 and j > i:
                bias[block(i), block(j)] = jnp.full((BLK, BLK), FILL, f32)
            else:
                bias[block(i), block(j)] = allowed(rows, i, 4 * chip + j)
    lane = lax.broadcasted_iota(jnp.int32, (2 * BLK, HD), 1)
    for r in range(2):
        part = slice(r * 2 * BLK, (r + 1) * 2 * BLK)
        count = 4 * BLK if ahead or r else 2 * BLK
        top_table = jnp.zeros((2 * BLK, HD), f32)
        sum_table = jnp.zeros((2 * BLK, HD), f32)
        for h in range(HEADS):
            acc, top, total = attend_head(
                q[part, cols(h)],
                jnp.concatenate([head[:BLK, cols(h)], tail[: count - BLK, cols(h)]], axis=0),
                jnp.concatenate(
                    [head[BLK:, cols(h)], tail[3 * BLK : 2 * BLK + count, cols(h)]], axis=0
                ),
                bias[part, :count],
            )
            out[part, cols(h)] = acc / total
            top_table = jnp.where(lane == h, top, top_table)
            sum_table = jnp.where(lane == h, total, sum_table)
        tops[part, :] = top_table
        sums[part, :] = sum_table


def near_body(index, q, head, tail, out, tops, sums, bias):
    attend_chip(index, 0, q, head, tail, out, tops, sums, bias)


def next_body(index, q, head, tail, out, tops, sums, bias):
    attend_chip(index, 1, q, head, tail, out, tops, sums, bias)


def weighed(top1, sum1, top2, sum2):
    top = jnp.maximum(top1, top2)
    part1 = jnp.exp2((top1 - top) * EXP2_SCALE) * sum1
    part2 = jnp.exp2((top2 - top) * EXP2_SCALE) * sum2
    return top, part1 + part2, part2 / (part1 + part2)


def far_body(index, q, tail, done, tops, sums, out, bias):
    chip = index[0] // 2
    flags = q[4 * BLK :, :NBLK].astype(f32)
    for i in range(3):
        for j in range(3):
            bias[block(i), block(j)] = allowed(flags, i, 4 * (chip - 1) + 1 + j)
    rows = slice(0, 3 * BLK)
    rest = slice(3 * BLK, 4 * BLK)
    lane = lax.broadcasted_iota(jnp.int32, (3 * BLK, HD), 1)
    top_table = jnp.zeros((3 * BLK, HD), f32)
    sum_table = jnp.ones((3 * BLK, HD), f32)
    for h in range(HEADS):
        acc, top, total = attend_head(
            q[rows, cols(h)], tail[rows, cols(h)], tail[3 * BLK :, cols(h)], bias[...]
        )
        top_table = jnp.where(lane == h, top, top_table)
        sum_table = jnp.where(lane == h, total, sum_table)
        top1 = tops[rows, h : h + 1]
        _, _, share = weighed(top1, sums[rows, h : h + 1], top, total)
        here = done[rows, cols(h)]
        out[rows, cols(h)] = (here + (acc / total - here) * share).astype(bf16)
        out[rest, cols(h)] = done[rest, cols(h)].astype(bf16)
    top, total, _ = weighed(tops[rows, :], jnp.where(lane < HEADS, sums[rows, :], 1.0), top_table, sum_table)
    top = jnp.concatenate([top, tops[rest, :]], axis=0)
    total = jnp.concatenate([total, sums[rest, :]], axis=0)
    filler = jnp.zeros((LOCAL, 4 * BLK), f32)
    left = jnp.concatenate([top.T[:HEADS], total.T[:HEADS], filler], axis=0)
    for piece in range(3):
        part = left.astype(bf16)
        at = 4 * BLK + piece * 2 * LOCAL
        out[at : at + 2 * LOCAL, :] = part
        left = left - part.astype(f32)


def merge_body(index, near, tops, sums, far, mine, send, share):
    stats = jnp.zeros((2 * LOCAL, HALF), f32)
    for p in range(3):
        at = 4 * BLK + p * 2 * LOCAL
        stats = stats + far[at : at + 2 * LOCAL, :].astype(f32)
    pad = jnp.ones((HD - HEADS, 4 * BLK), f32)
    far_sums = jnp.concatenate([stats[HEADS : 2 * HEADS], pad], axis=0).T
    far_tops = jnp.concatenate([stats[:HEADS], pad], axis=0).T
    far_tops = jnp.where(far_sums > 0.0, far_tops, FILL)
    far_sums = jnp.where(far_sums > 0.0, far_sums, 1.0)
    lane = lax.broadcasted_iota(jnp.int32, (4 * BLK, HD), 1)
    near_sums = jnp.where(lane < HEADS, sums[...], 1.0)
    share[...] = weighed(tops[...], near_sums, far_tops, far_sums)[2]
    core = index[0] % 2
    for out, which in ((send, 1 - core), (mine, core)):
        rows = pl.ds(pl.multiple_of(which * ROWS, ROWS), ROWS)
        part = share[rows, :]
        for h in range(HEADS):
            own = near[rows, cols(h)]
            there = far[rows, cols(h)].astype(f32)
            out[:, cols(h)] = (own + (there - own) * part[:, h : h + 1]).astype(bf16)


def place_body(index, mine, other, out):
    core = index[0] % 2
    out[:, half(core)] = mine[...]
    out[:, half(1 - core)] = other[...]


SMALL = (gather_body, near_body, prefix_body, next_body, far_body, merge_body, norm_body, place_body)


def shifted(x, distance):
    return lax.ppermute(x, "seq", [(i, i + distance) for i in range(SHARDS) if 0 <= i + distance < SHARDS])


def swapped(x):
    return lax.ppermute(x, "seq", [(i, i ^ 1) for i in range(SHARDS)])


def turned(x, distance):
    return lax.ppermute(x, "head", [(i, (i + distance) % 4) for i in range(4)])


def per_device(
    lin_query,
    lin_key,
    lin_value,
    out_gate,
    norm_gain,
    decay_rate,
    soft_query,
    soft_key,
    soft_value,
    doc_ids,
    block_mask,
):
    like = jax.ShapeDtypeStruct
    index = lax.axis_index("seq").astype(jnp.int32).reshape(1)
    wide = like((ROWS, WIDTH), f32)
    narrow = like((ROWS, WIDTH), bf16)

    anywhere = pl.BlockSpec(memory_space=pl.ANY)
    first, state, sent = call(
        start_body,
        [like((WIDTH, HD), f32), like((WIDTH, HD), bf16), like((3 * ROWS + 16, HALF), bf16)],
        (
            index, doc_ids, doc_ids.reshape(1, NBLK), decay_rate, block_mask,
            lin_key, lin_value, soft_query, soft_key, soft_value,
        ),
        [SMEM, SMEM, VMEM, anywhere, VMEM] + [anywhere] * 5,
        [
            pltpu.SMEM((LOCAL,), f32),
            pltpu.VMEM((ROWS, WIDTH), bf16),
            pltpu.VMEM((ROWS, WIDTH), bf16),
            pltpu.VMEM((16, HALF), bf16),
            pltpu.SemaphoreType.DMA,
            pltpu.SemaphoreType.DMA((LOCAL + 4,)),
        ],
    )
    other = swapped(sent)
    parts = lax.all_to_all(state.reshape(SHARDS, 16, HD), "seq", 0, 0)
    far_q, own_head, own_tail = call(
        gather_body,
        [
            like((2 * ROWS + 16, HALF), bf16),
            like((2 * BLK, HALF), bf16),
            like((6 * BLK, HALF), bf16),
        ],
        (index, block_mask, soft_query, soft_key, soft_value, other),
        [SMEM, VMEM] + [anywhere] * 4,
        [
            pltpu.VMEM((16, NBLK), bf16),
            pltpu.VMEM((16, HALF), bf16),
            pltpu.SemaphoreType.DMA((10,)),
        ],
    )
    tail = shifted(own_tail, 2)
    next_q = shifted(far_q, -2)

    (prefix,) = call(
        prefix_body,
        [like((SHARDS, 16, HD), bf16)],
        (index, decay_rate, parts),
        [SMEM, SMEM, VMEM],
        flops=PREFIX_COST,
    )
    prefix, own_head = lax.optimization_barrier((prefix, own_head))
    entering = lax.all_to_all(prefix, "seq", 0, 0).reshape(WIDTH, HD)
    tables = [like((4 * BLK, HALF), f32), like((4 * BLK, HD), f32), like((4 * BLK, HD), f32)]
    done, done_tops, done_sums = call(
        next_body,
        tables,
        (index, next_q, own_head, own_tail),
        [SMEM] + [VMEM] * 3,
        [pltpu.VMEM((4 * BLK, 4 * BLK), f32)],
    )
    (far,) = call(
        far_body,
        [like((4 * BLK + 48, HALF), bf16)],
        (index, next_q, tail, done, done_tops, done_sums),
        [SMEM] + [VMEM] * 5,
        [pltpu.VMEM((3 * BLK, 3 * BLK), f32)],
    )
    far, lin_query = lax.optimization_barrier((far, lin_query))
    far = shifted(far, 2)
    inner, rates = call(
        inner_body,
        [wide, like((LOCAL, HD), f32)],
        (decay_rate, lin_query, lin_key, lin_value),
        [SMEM] + [VMEM] * 3,
    )
    heads, squares = call(
        carry_body,
        [wide, like((8, ROWS), f32)],
        (rates, inner, lin_query, first, entering),
        [VMEM] * 5,
        flops=CARRY_COST,
    )
    heads, own_head = lax.optimization_barrier((heads, own_head))
    others = [turned(squares, d) for d in (1, 2, 3)]
    near, tops, sums = call(
        near_body,
        tables,
        (index, far_q, own_head, own_tail),
        [SMEM] + [VMEM] * 3,
        [pltpu.VMEM((4 * BLK, 4 * BLK), f32)],
    )
    far, heads = lax.optimization_barrier((far, heads))
    mine, send = call(
        merge_body,
        [like((ROWS, HALF), bf16)] * 2,
        (index, near, tops, sums, far),
        [SMEM] + [VMEM] * 4,
        [pltpu.VMEM((4 * BLK, HD), f32)],
    )
    send, *others = lax.optimization_barrier((send, *others))
    (lin_output,) = call(
        norm_body,
        [narrow],
        (heads, out_gate, norm_gain.reshape(1, WIDTH), squares, *others),
        [VMEM] * 7,
    )

    (soft_output,) = call(
        place_body, [narrow], (index, mine, swapped(send)), [SMEM, VMEM, VMEM]
    )
    return (lin_output, soft_output)


def solution(mesh):
    rows = P("seq", "head")
    return jax.shard_map(
        per_device,
        mesh=mesh,
        in_specs=(
            rows, rows, rows, rows, P("head"), P("head"), rows, rows, rows, P(), P("seq", None),
        ),
        out_specs=(rows, rows),
        check_vma=False,
    )
```

```python
import math

import jax
import jax.numpy as jnp
from jax import lax
from jax.experimental import pallas as pl
from jax.experimental.pallas import tpu as pltpu
from jax.sharding import PartitionSpec as P

HD = 128
BLK = 128
NBLK = 128
ROWS = 256
LOCAL = 8
WIDTH = LOCAL * HD
HALF = WIDTH // 2
HEADS = LOCAL // 2
D = 4096
SHARDS = 64
FILL = -1e30
PREFIX_COST = 1_500_000_000
CARRY_COST = 2000000000
EXP2_SCALE = HD ** (-0.5) * math.log2(math.e)

f32 = jnp.float32
bf16 = jnp.bfloat16

SMEM = pl.BlockSpec(memory_space=pltpu.SMEM)
VMEM = pl.BlockSpec(memory_space=pltpu.VMEM)


def call(body, outs, ins, specs, scratch=(), flops=1):
    return pl.pallas_call(
        body,
        out_shape=outs,
        in_specs=specs,
        out_specs=[VMEM] * len(outs),
        scratch_shapes=list(scratch),
        compiler_params=pltpu.CompilerParams(vmem_limit_bytes=(16 if body in SMALL else 60) * 1024 * 1024),
        cost_estimate=pl.CostEstimate(flops=flops, bytes_accessed=1, transcendentals=0),
    )(*ins)


def cols(h):
    return slice(h * HD, (h + 1) * HD)


def dot(a, b, dims):
    return lax.dot_general(a, b, (dims, ((), ())), preferred_element_type=f32)


def exact_dot(a, b, dims):
    return lax.dot_general(
        a, b, (dims, ((), ())), precision=lax.Precision.HIGHEST, preferred_element_type=f32
    )


def block_state(rate, k, v, h, b):
    rows = slice(b * BLK, (b + 1) * BLK)
    back = (BLK - 1.0) - lax.broadcasted_iota(jnp.int32, (BLK, HD), 0).astype(f32)
    decayed = (k[rows, cols(h)].astype(f32) * jnp.exp(-rate * back)).astype(bf16)
    return dot(decayed, v[rows, cols(h)], ((0,), (0,)))


def start_body(
    index, docs, doc_row, rate_hbm, mask, k_hbm, v_hbm, sq, sk, sv, first, out, sent, rate, k, v, packed, rate_sem, sems
):
    other = 1 - index[0] % 2
    copies = [pltpu.make_async_copy(rate_hbm, rate, rate_sem)]
    for g in range(LOCAL // 2):
        at = slice(g * 2 * HD, (g + 1) * 2 * HD)
        copies.append(pltpu.make_async_copy(k_hbm.at[:, at], k.at[:, at], sems.at[2 * g]))
        copies.append(pltpu.make_async_copy(v_hbm.at[:, at], v.at[:, at], sems.at[2 * g + 1]))
    for at, ref in enumerate((sq, sk, sv)):
        rows = slice(at * ROWS, (at + 1) * ROWS)
        copies.append(
            pltpu.make_async_copy(ref.at[:, half(other)], sent.at[rows, :], sems.at[LOCAL + at])
        )
    for copy in copies:
        copy.start()
    line = lax.broadcasted_iota(jnp.int32, (2, NBLK), 0)
    lane = lax.broadcasted_iota(jnp.int32, (2, NBLK), 1)
    query = 2 * index[0]
    document = jnp.where(line == 0, docs[query], docs[query + 1])
    reach = (doc_row[...] == document) & (lane < query + line) & (mask[...] == 1)
    flags = jnp.where(reach, 1.0, 0.0)
    ids = doc_row[...].astype(f32)
    flags = jnp.concatenate([flags, ids, jnp.zeros((13, NBLK), f32)], axis=0).astype(bf16)
    packed[...] = jnp.concatenate([flags] * 4, axis=1)
    copies.append(pltpu.make_async_copy(packed, sent.at[3 * ROWS :, :], sems.at[LOCAL + 3]))
    copies[-1].start()
    copies[0].wait()
    for g in range(LOCAL // 2):
        copies[2 * g + 1].wait()
        copies[2 * g + 2].wait()
        for h in (2 * g, 2 * g + 1):
            step = jnp.exp(jnp.full((HD, HD), -rate[h] * BLK, f32))
            early = block_state(rate[h], k, v, h, 0)
            first[cols(h), :] = early
            out[cols(h), :] = (step * early + block_state(rate[h], k, v, h, 1)).astype(bf16)
    for copy in copies[LOCAL + 1 :]:
        copy.wait()


def prefix_body(index, rate, parts, out):
    step = jnp.exp(jnp.full((16, HD), -rate[index[0] // 8] * ROWS, f32))
    state = jnp.zeros((16, HD), f32)
    for i in range(SHARDS):
        out[i] = state.astype(bf16)
        if i + 1 < SHARDS:
            state = step * state + parts[i].astype(f32)


def inner_body(rate, q, k, v, out, rates):
    row = lax.broadcasted_iota(jnp.int32, (ROWS, ROWS), 0)
    col = lax.broadcasted_iota(jnp.int32, (ROWS, ROWS), 1)
    gap = jnp.maximum(row - col, 0).astype(f32)
    inside = (row >= col) & ((row >= BLK) == (col >= BLK))
    for h in range(LOCAL):
        rates[h : h + 1, :] = jnp.full((1, HD), rate[h], f32)
        decay = jnp.where(inside, jnp.exp(-rate[h] * gap), 0.0)
        scores = dot(q[:, cols(h)], k[:, cols(h)], ((1,), (1,)))
        out[:, cols(h)] = dot((scores * decay).astype(bf16), v[:, cols(h)], ((1,), (0,)))


def carry_body(rates, inner, q, first, state, heads, squares):
    ahead = lax.broadcasted_iota(jnp.int32, (BLK, HD), 0).astype(f32) + 1.0
    totals = [jnp.zeros((BLK, HD), f32)] * 2
    for h in range(LOCAL):
        rate = rates[h : h + 1, :]
        decay = jnp.exp(-rate * ahead)
        entering = state[cols(h), :]
        middle = (jnp.exp(-rate * BLK) * entering.astype(f32) + first[cols(h), :]).astype(bf16)
        for b, block_start in enumerate((entering, middle)):
            rows = slice(b * BLK, (b + 1) * BLK)
            carried = dot(q[rows, cols(h)], block_start, ((1,), (0,)))
            value = inner[rows, cols(h)] + carried * decay
            heads[rows, cols(h)] = value
            totals[b] = totals[b] + value * value
    total = jnp.concatenate(totals, axis=0)
    squares[...] = exact_dot(jnp.ones((8, HD), f32), total, ((1,), (1,)))


def norm_body(heads, gate, gain, s0, s1, s2, s3, out):
    total = s0[...] + s1[...] + s2[...] + s3[...]
    first = (lax.broadcasted_iota(jnp.int32, (8, HD), 0) == 0).astype(f32)
    spread = exact_dot(total, first, ((0,), (0,)))
    inverse = lax.rsqrt(spread / D + 1e-06)
    for h in range(LOCAL):
        scale = gain[:, cols(h)] * jax.nn.sigmoid(gate[:, cols(h)].astype(f32))
        out[:, cols(h)] = (heads[:, cols(h)] * inverse * scale).astype(bf16)


def half(c):
    return pl.ds(pl.multiple_of(c * HALF, HALF), HALF)


def gather_body(index, mask, q, k, v, other, far_q, head, tail, theirs, packed, sems):
    core = index[0] % 2

    def put(source, target, at):
        return pltpu.make_async_copy(source, target, sems.at[at])

    def layout(mine):
        def part(at, ref, owner, rows):
            if owner == mine:
                return ref.at[rows, half(core)]
            return other.at[slice(at * ROWS + rows.start, at * ROWS + rows.stop), :]

        low, high, whole = slice(0, BLK), slice(BLK, ROWS), slice(0, ROWS)
        copies = [
            put(part(0, q, 0, whole), far_q.at[:ROWS, :], 0),
            put(part(0, q, 1, whole), far_q.at[ROWS : 2 * ROWS, :], 1),
        ]
        for at, ref in ((1, k), (2, v)):
            base = (at - 1) * 3 * BLK
            sem = 3 * at - 1
            copies += [
                put(part(at, ref, 0, low), head.at[(at - 1) * BLK : at * BLK, :], sem),
                put(part(at, ref, 0, high), tail.at[base : base + BLK, :], sem + 1),
                put(part(at, ref, 1, whole), tail.at[base + BLK : base + 3 * BLK, :], sem + 2),
            ]
        return copies

    for mine in range(2):

        @pl.when(core == mine)
        def _():
            for copy in layout(mine):
                copy.start()

    fetch = put(other.at[3 * ROWS :, :NBLK], theirs, 8)
    fetch.start()
    fetch.wait()
    arrived = theirs[...].astype(f32)
    ids = arrived[2:3, :]
    line = lax.broadcasted_iota(jnp.int32, (2, NBLK), 0)
    lane = lax.broadcasted_iota(jnp.int32, (2, NBLK), 1)
    query = 2 * index[0] + line
    document = jnp.sum(jnp.where(lane == query, ids, 0.0), axis=1, keepdims=True)
    reach = (ids == document) & (lane < query) & (mask[...] == 1)
    own = jnp.where(reach, 1.0, 0.0)
    arrived = arrived[:2, :]
    first = jnp.where(core == 0, own, arrived)
    second = jnp.where(core == 0, arrived, own)
    rows = jnp.concatenate([first, second, jnp.zeros((12, NBLK), f32)], axis=0)
    packed[...] = jnp.concatenate([rows.astype(bf16)] * 4, axis=1)
    flags = put(packed, far_q.at[4 * BLK :, :], 9)
    flags.start()
    for mine in range(2):

        @pl.when(core == mine)
        def _():
            for copy in layout(mine):
                copy.wait()

    flags.wait()


def allowed(flags, i, key):
    lane = lax.broadcasted_iota(jnp.int32, (1, NBLK), 1)
    ok = jnp.sum(jnp.where(lane == key, flags[i : i + 1, :], 0.0), axis=1, keepdims=True)
    return jnp.broadcast_to(jnp.where(ok > 0.5, 0.0, FILL), (BLK, BLK))


def block(i):
    return slice(i * BLK, (i + 1) * BLK)


def attend_head(q, keys, values, bias):
    scores = dot(q, keys, ((1,), (1,))) + bias
    top = jnp.max(scores, axis=1, keepdims=True)
    weights = jnp.exp2((scores - top) * EXP2_SCALE).astype(bf16)
    ones = jnp.ones(values.shape, bf16)
    both = dot(weights, jnp.concatenate([values, ones], axis=1), ((1,), (0,)))
    return both[:, :HD], top, both[:, HD:]


def attend_chip(index, ahead, q, head, tail, out, tops, sums, bias):
    chip = index[0] // 2
    rows = q[4 * BLK :, :NBLK].astype(f32)
    for i in range(4):
        for j in range(4):
            if ahead == 0 and j == i:
                row = lax.broadcasted_iota(jnp.int32, (BLK, BLK), 0)
                col = lax.broadcasted_iota(jnp.int32, (BLK, BLK), 1)
                bias[block(i), block(j)] = jnp.where(col <= row, 0.0, FILL)
            elif ahead == 0 and j > i:
                bias[block(i), block(j)] = jnp.full((BLK, BLK), FILL, f32)
            else:
                bias[block(i), block(j)] = allowed(rows, i, 4 * chip + j)
    lane = lax.broadcasted_iota(jnp.int32, (2 * BLK, HD), 1)
    for r in range(2):
        part = slice(r * 2 * BLK, (r + 1) * 2 * BLK)
        count = 4 * BLK if ahead or r else 2 * BLK
        top_table = jnp.zeros((2 * BLK, HD), f32)
        sum_table = jnp.zeros((2 * BLK, HD), f32)
        for h in range(HEADS):
            acc, top, total = attend_head(
                q[part, cols(h)],
                jnp.concatenate([head[:BLK, cols(h)], tail[: count - BLK, cols(h)]], axis=0),
                jnp.concatenate(
                    [head[BLK:, cols(h)], tail[3 * BLK : 2 * BLK + count, cols(h)]], axis=0
                ),
                bias[part, :count],
            )
            out[part, cols(h)] = acc / total
            top_table = jnp.where(lane == h, top, top_table)
            sum_table = jnp.where(lane == h, total, sum_table)
        tops[part, :] = top_table
        sums[part, :] = sum_table


def near_body(index, q, head, tail, out, tops, sums, bias):
    attend_chip(index, 0, q, head, tail, out, tops, sums, bias)


def next_body(index, q, head, tail, out, tops, sums, bias):
    attend_chip(index, 1, q, head, tail, out, tops, sums, bias)


def weighed(top1, sum1, top2, sum2):
    top = jnp.maximum(top1, top2)
    part1 = jnp.exp2((top1 - top) * EXP2_SCALE) * sum1
    part2 = jnp.exp2((top2 - top) * EXP2_SCALE) * sum2
    return top, part1 + part2, part2 / (part1 + part2)


def far_body(index, q, tail, done, tops, sums, out, bias):
    chip = index[0] // 2
    flags = q[4 * BLK :, :NBLK].astype(f32)
    for i in range(3):
        for j in range(3):
            bias[block(i), block(j)] = allowed(flags, i, 4 * (chip - 1) + 1 + j)
    rows = slice(0, 3 * BLK)
    rest = slice(3 * BLK, 4 * BLK)
    lane = lax.broadcasted_iota(jnp.int32, (3 * BLK, HD), 1)
    top_table = jnp.zeros((3 * BLK, HD), f32)
    sum_table = jnp.ones((3 * BLK, HD), f32)
    for h in range(HEADS):
        acc, top, total = attend_head(
            q[rows, cols(h)], tail[rows, cols(h)], tail[3 * BLK :, cols(h)], bias[...]
        )
        top_table = jnp.where(lane == h, top, top_table)
        sum_table = jnp.where(lane == h, total, sum_table)
        top1 = tops[rows, h : h + 1]
        _, _, share = weighed(top1, sums[rows, h : h + 1], top, total)
        here = done[rows, cols(h)]
        out[rows, cols(h)] = (here + (acc / total - here) * share).astype(bf16)
        out[rest, cols(h)] = done[rest, cols(h)].astype(bf16)
    top, total, _ = weighed(tops[rows, :], jnp.where(lane < HEADS, sums[rows, :], 1.0), top_table, sum_table)
    top = jnp.concatenate([top, tops[rest, :]], axis=0)
    total = jnp.concatenate([total, sums[rest, :]], axis=0)
    filler = jnp.zeros((LOCAL, 4 * BLK), f32)
    left = jnp.concatenate([top.T[:HEADS], total.T[:HEADS], filler], axis=0)
    for piece in range(3):
        part = left.astype(bf16)
        at = 4 * BLK + piece * 2 * LOCAL
        out[at : at + 2 * LOCAL, :] = part
        left = left - part.astype(f32)


def merge_body(index, near, tops, sums, far, mine, send, share):
    stats = jnp.zeros((2 * LOCAL, HALF), f32)
    for p in range(3):
        at = 4 * BLK + p * 2 * LOCAL
        stats = stats + far[at : at + 2 * LOCAL, :].astype(f32)
    pad = jnp.ones((HD - HEADS, 4 * BLK), f32)
    far_sums = jnp.concatenate([stats[HEADS : 2 * HEADS], pad], axis=0).T
    far_tops = jnp.concatenate([stats[:HEADS], pad], axis=0).T
    far_tops = jnp.where(far_sums > 0.0, far_tops, FILL)
    far_sums = jnp.where(far_sums > 0.0, far_sums, 1.0)
    lane = lax.broadcasted_iota(jnp.int32, (4 * BLK, HD), 1)
    near_sums = jnp.where(lane < HEADS, sums[...], 1.0)
    share[...] = weighed(tops[...], near_sums, far_tops, far_sums)[2]
    core = index[0] % 2
    for out, which in ((send, 1 - core), (mine, core)):
        rows = pl.ds(pl.multiple_of(which * ROWS, ROWS), ROWS)
        part = share[rows, :]
        for h in range(HEADS):
            own = near[rows, cols(h)]
            there = far[rows, cols(h)].astype(f32)
            out[:, cols(h)] = (own + (there - own) * part[:, h : h + 1]).astype(bf16)


def place_body(index, mine, other, out):
    core = index[0] % 2
    out[:, half(core)] = mine[...]
    out[:, half(1 - core)] = other[...]


SMALL = (gather_body, near_body, prefix_body, next_body, far_body, merge_body, norm_body, place_body)


def shifted(x, distance):
    return lax.ppermute(x, "seq", [(i, i + distance) for i in range(SHARDS) if 0 <= i + distance < SHARDS])


def swapped(x):
    return lax.ppermute(x, "seq", [(i, i ^ 1) for i in range(SHARDS)])


def turned(x, distance):
    return lax.ppermute(x, "head", [(i, (i + distance) % 4) for i in range(4)])


def per_device(
    lin_query,
    lin_key,
    lin_value,
    out_gate,
    norm_gain,
    decay_rate,
    soft_query,
    soft_key,
    soft_value,
    doc_ids,
    block_mask,
):
    like = jax.ShapeDtypeStruct
    index = lax.axis_index("seq").astype(jnp.int32).reshape(1)
    wide = like((ROWS, WIDTH), f32)
    narrow = like((ROWS, WIDTH), bf16)

    anywhere = pl.BlockSpec(memory_space=pl.ANY)
    first, state, sent = call(
        start_body,
        [like((WIDTH, HD), f32), like((WIDTH, HD), bf16), like((3 * ROWS + 16, HALF), bf16)],
        (
            index, doc_ids, doc_ids.reshape(1, NBLK), decay_rate, block_mask,
            lin_key, lin_value, soft_query, soft_key, soft_value,
        ),
        [SMEM, SMEM, VMEM, anywhere, VMEM] + [anywhere] * 5,
        [
            pltpu.SMEM((LOCAL,), f32),
            pltpu.VMEM((ROWS, WIDTH), bf16),
            pltpu.VMEM((ROWS, WIDTH), bf16),
            pltpu.VMEM((16, HALF), bf16),
            pltpu.SemaphoreType.DMA,
            pltpu.SemaphoreType.DMA((LOCAL + 4,)),
        ],
    )
    other = swapped(sent)
    parts = lax.all_to_all(state.reshape(SHARDS, 16, HD), "seq", 0, 0)
    far_q, own_head, own_tail = call(
        gather_body,
        [
            like((2 * ROWS + 16, HALF), bf16),
            like((2 * BLK, HALF), bf16),
            like((6 * BLK, HALF), bf16),
        ],
        (index, block_mask, soft_query, soft_key, soft_value, other),
        [SMEM, VMEM] + [anywhere] * 4,
        [
            pltpu.VMEM((16, NBLK), bf16),
            pltpu.VMEM((16, HALF), bf16),
            pltpu.SemaphoreType.DMA((10,)),
        ],
    )
    tail = shifted(own_tail, 2)
    next_q = shifted(far_q, -2)

    (prefix,) = call(
        prefix_body,
        [like((SHARDS, 16, HD), bf16)],
        (index, decay_rate, parts),
        [SMEM, SMEM, VMEM],
        flops=PREFIX_COST,
    )
    prefix, own_head = lax.optimization_barrier((prefix, own_head))
    entering = lax.all_to_all(prefix, "seq", 0, 0).reshape(WIDTH, HD)
    tables = [like((4 * BLK, HALF), f32), like((4 * BLK, HD), f32), like((4 * BLK, HD), f32)]
    done, done_tops, done_sums = call(
        next_body,
        tables,
        (index, next_q, own_head, own_tail),
        [SMEM] + [VMEM] * 3,
        [pltpu.VMEM((4 * BLK, 4 * BLK), f32)],
    )
    near, tops, sums = call(
        near_body,
        tables,
        (index, far_q, own_head, own_tail),
        [SMEM] + [VMEM] * 3,
        [pltpu.VMEM((4 * BLK, 4 * BLK), f32)],
    )
    near, tail = lax.optimization_barrier((near, tail))
    (far,) = call(
        far_body,
        [like((4 * BLK + 48, HALF), bf16)],
        (index, next_q, tail, done, done_tops, done_sums),
        [SMEM] + [VMEM] * 5,
        [pltpu.VMEM((3 * BLK, 3 * BLK), f32)],
    )
    far, lin_query = lax.optimization_barrier((far, lin_query))
    far = shifted(far, 2)
    inner, rates = call(
        inner_body,
        [wide, like((LOCAL, HD), f32)],
        (decay_rate, lin_query, lin_key, lin_value),
        [SMEM] + [VMEM] * 3,
    )
    heads, squares = call(
        carry_body,
        [wide, like((8, ROWS), f32)],
        (rates, inner, lin_query, first, entering),
        [VMEM] * 5,
        flops=CARRY_COST,
    )
    others = [turned(squares, d) for d in (1, 2, 3)]
    far, heads = lax.optimization_barrier((far, heads))
    mine, send = call(
        merge_body,
        [like((ROWS, HALF), bf16)] * 2,
        (index, near, tops, sums, far),
        [SMEM] + [VMEM] * 4,
        [pltpu.VMEM((4 * BLK, HD), f32)],
    )
    send, *others = lax.optimization_barrier((send, *others))
    (lin_output,) = call(
        norm_body,
        [narrow],
        (heads, out_gate, norm_gain.reshape(1, WIDTH), squares, *others),
        [VMEM] * 7,
    )

    (soft_output,) = call(
        place_body, [narrow], (index, mine, swapped(send)), [SMEM, VMEM, VMEM]
    )
    return (lin_output, soft_output)


def solution(mesh):
    rows = P("seq", "head")
    return jax.shard_map(
        per_device,
        mesh=mesh,
        in_specs=(
            rows, rows, rows, rows, P("head"), P("head"), rows, rows, rows, P(), P("seq", None),
        ),
        out_specs=(rows, rows),
        check_vma=False,
    )
```
